32 devices in a mesh: dp: 4 (over y, x), expert: 8 (over z, core).
Axes of the slice: x: 2, y: 2, z: 4, core: 2. Of those that a mesh axis runs over, the one named last changes fastest.
Arguments:
- cotangent: bfloat16 [4096, 4096], P(('dp', 'expert')), may hold values from -6 to 6
- hidden: bfloat16 [4, 8, 128, 768], P('dp', 'expert'), may hold values from -6 to 6
- down_matrix: bfloat16 [8, 4096, 768], P('expert'), may hold values from -0.21875 to 0.21875
- adapter_in: bfloat16 [2, 128, 768], replicated, may hold values from -0.21875 to 0.21875
- adapter_out: bfloat16 [2, 4096, 128], replicated, may hold values from -0.5 to 0.5
- probs: bfloat16 [4096, 8], P(('dp', 'expert')), may hold values from 0.019897461 to 0.5
- routes: int32 [4096, 8], P(('dp', 'expert')), may hold values from 0 to 127, as said below
- token_loop: int32 [4096], P(('dp', 'expert')), may hold values from 0 to 1
Outputs:
- hidden_gradient: bfloat16 [4, 8, 128, 768], P('dp', 'expert')
- down_matrix_gradient: float32 [8, 4096, 768], P('expert', 'dp')
- combine_weight_gradient: float32 [4096, 8], P(('dp', 'expert'))
- adapter_in_gradient: float32 [2, 128, 768], P(None, 'expert', 'dp')
- adapter_out_gradient: float32 [2, 4096, 128], P(None, 'dp', 'expert')
The draws below stay inside these ranges and needn't reach their ends.
Inputs may be any that keep to these rules, and one draw needn't show every extreme that they name: `routes`: each row names 8 different experts. In the 128 rows of one device every expert below 8 is named by 4 to 16 rows, and within each index of dp one such expert is named by exactly 16 rows of every device.
All inputs are finite; a program needn't handle non-finite values.
Results may differ from the reference program's by a relative error of at most 0.0049.
Values may be sent and summed in bfloat16 or wider, within the bound.
No kernel may reach another device: no remote copies, remote signals or barrier semaphores. Data moves between devices by JAX's collectives and lax.ppermute only.
A program may use at most 128 MiB of HBM per device.

```python
import math
from functools import partial
import jax
import jax.numpy as jnp
from jax import lax

MODEL_DIM = 4096
HIDDEN_UNITS = 768
EXPERTS = 128
EXPERTS_PER_TOKEN = 8
ADAPTER_RANK = 128
LOOP_TOTAL = 2
TOK_DEV = 128
SLOT_CAPACITY = 16
TOKEN_TOTAL = 4096
N_DP = 4
N_EXPERT = 8


def draw_routes(key, part):
    groups = N_DP
    owner_devices = N_EXPERT
    blocks = groups * owner_devices
    key_full, key_count, key_shuffle, key_fill, key_column = jax.random.split(key, 5)
    full_expert = jax.random.randint(key_full, (groups,), 0, owner_devices)
    lowest = max(1, SLOT_CAPACITY // 4)
    counts = jax.random.randint(key_count, (groups, owner_devices, owner_devices), lowest, SLOT_CAPACITY + 1)
    experts = jnp.arange(owner_devices, dtype=jnp.int32)
    counts = jnp.where(experts[None, None, :] == full_expert[:, None, None], SLOT_CAPACITY, counts).reshape(blocks, owner_devices)
    position = jnp.arange(TOK_DEV, dtype=jnp.int32)
    offset = (position[:, None] - experts[None, :] * SLOT_CAPACITY) % TOK_DEV
    covered = offset[None, :, :] < counts[:, None, :]
    covered_count = covered.astype(jnp.int32)
    order_rank = jnp.cumsum(covered_count, axis=2) - covered_count
    row_count = jnp.sum(covered_count, axis=2)
    column = jnp.arange(EXPERTS_PER_TOKEN, dtype=jnp.int32)
    chosen = covered[:, :, None, :] & (order_rank[:, :, None, :] == column[None, None, :, None])
    window_id = jnp.sum(jnp.where(chosen, experts[None, None, None, :], 0), axis=3)
    remaining = EXPERTS - owner_devices
    fill_start = jax.random.randint(key_fill, (blocks, TOK_DEV, 1), 0, remaining)
    filler = owner_devices + (fill_start + column[None, None, :]) % remaining
    table = jnp.where(column[None, None, :] < row_count[:, :, None], window_id, filler)
    sort_keys = jax.random.randint(key_column, (blocks, TOK_DEV, EXPERTS_PER_TOKEN), 0, 1 << 20) * EXPERTS_PER_TOKEN + column[None, None, :]
    column_order = jnp.argsort(sort_keys, axis=2)
    table = jnp.take_along_axis(table, column_order, axis=2)
    shuffled = jax.vmap(lambda one_key: jax.random.permutation(one_key, TOK_DEV))(jax.random.split(key_shuffle, blocks))
    routed = jnp.take_along_axis(table, shuffled[:, :, None], axis=1)
    return routed.reshape(blocks * TOK_DEV, EXPERTS_PER_TOKEN).astype(jnp.int32)


def touch_ends(entries, own_key, low, high):
    spot = [jax.random.randint(jax.random.fold_in(own_key, axis), (), 0, length) for axis, length in enumerate(entries.shape)]
    main_axis = entries.shape.index(max(entries.shape))
    neighbour = spot[:main_axis] + [(spot[main_axis] + 1) % entries.shape[main_axis]] + spot[main_axis + 1:]
    return entries.at[tuple(spot)].set(low).at[tuple(neighbour)].set(high)


def shard_levels(own_key, shape, cuts, least, largest):
    gain, own = 1.0, jax.random.fold_in(own_key, 6)
    for axis_at, parts in cuts:
        steps = jnp.exp(jax.random.uniform(jax.random.fold_in(own, axis_at), (parts,), jnp.float32, least / len(cuts), largest / len(cuts)))
        gain = gain * jnp.repeat(steps, shape[axis_at] // parts).reshape([-1 if axis == axis_at else 1 for axis in range(len(shape))])
    return gain


def noise(rng, dims, scale, limit, pieces=(), kind=jnp.bfloat16):
    gain = shard_levels(rng, dims, pieces, -0.22, 0.18) if pieces else 1.0
    values = jax.random.normal(rng, dims, jnp.float32) * scale * gain
    return jnp.minimum(jnp.maximum(values, -limit), limit).astype(kind)


def setup_inputs(seed: int = 0) -> dict:
    keys = jax.random.split(jax.random.key(seed), 9)
    return {
        "cotangent": noise(keys[0], (TOKEN_TOTAL, MODEL_DIM), 1.0, 6.0, ((0, 32),)),
        "hidden": noise(keys[1], (N_DP, N_EXPERT, N_EXPERT * SLOT_CAPACITY, HIDDEN_UNITS), 1.0, 6.0, ((0, 4), (1, 8))),
        "down_matrix": noise(keys[2], (N_EXPERT, MODEL_DIM, HIDDEN_UNITS), HIDDEN_UNITS ** -0.5, 0.21875, ((0, 8),)),
        "adapter_in": noise(keys[3], (LOOP_TOTAL, ADAPTER_RANK, HIDDEN_UNITS), HIDDEN_UNITS ** -0.5, 0.21875),
        "adapter_out": noise(keys[4], (LOOP_TOTAL, MODEL_DIM, ADAPTER_RANK), ADAPTER_RANK ** -0.5, 0.5),
        "probs": jnp.clip(jnp.exp(math.log(0.5) - 3.224016 * jax.random.uniform(keys[5], (TOKEN_TOTAL, EXPERTS_PER_TOKEN), jnp.float32) ** shard_levels(keys[5], (TOKEN_TOTAL, EXPERTS_PER_TOKEN), ((0, 32),), -0.2, 0.2)), 0.019897461, 0.5).astype(jnp.bfloat16),
        "routes": draw_routes(jax.random.fold_in(keys[8], 71), 0),
        "token_loop": touch_ends(jax.random.randint(keys[7], (TOKEN_TOTAL,), 0, LOOP_TOTAL), jax.random.fold_in(keys[7], 1), 0, LOOP_TOTAL - 1).astype(jnp.int32),
    }


def route_slots(routes, owner_devices, slot_capacity):
    experts = jnp.arange(owner_devices, dtype=jnp.int32)
    named_count = jnp.sum((routes[:, :, None] == experts[None, None, :]).astype(jnp.int32), axis=1)
    before = jnp.cumsum(named_count, axis=0) - named_count
    in_window = routes < owner_devices
    target = jnp.where(in_window, routes, 0).astype(jnp.int32)
    column = jnp.take_along_axis(before, target, axis=1)
    slot_index = jnp.where(in_window, target * slot_capacity + column, owner_devices * slot_capacity).astype(jnp.int32)
    return in_window, slot_index


def sender_portion(sender_output_gradient, sender_combine_weights, sender_routing, sender_loop, adapter_out_float, owner_devices, slot_capacity):
    slot_count = owner_devices * slot_capacity
    tokens_here = sender_output_gradient.shape[0]
    loop_number = adapter_out_float.shape[0]
    in_window, slot_index = route_slots(sender_routing, owner_devices, slot_capacity)
    token_index = jnp.broadcast_to(jnp.arange(tokens_here, dtype=jnp.int32)[:, None], slot_index.shape)
    slot_token = jnp.full((slot_count,), tokens_here, jnp.int32).at[slot_index.reshape(-1)].set(token_index.reshape(-1), mode="drop")
    slot_weight = jnp.zeros((slot_count,), jnp.float32).at[slot_index.reshape(-1)].set(sender_combine_weights.astype(jnp.float32).reshape(-1), mode="drop")
    loop_mask = (sender_loop[:, None] == jnp.arange(loop_number, dtype=jnp.int32)[None, :]).astype(jnp.float32)
    every_loop = jnp.einsum("xn,jnr->xjr", sender_output_gradient.astype(jnp.float32), adapter_out_float)
    projected = jnp.sum(every_loop * loop_mask[:, :, None], axis=1).astype(jnp.bfloat16)
    padded_dy = jnp.concatenate([sender_output_gradient, jnp.zeros((1, sender_output_gradient.shape[1]), jnp.bfloat16)], axis=0)
    padded_mask = jnp.concatenate([loop_mask, jnp.zeros((1, loop_number), jnp.float32)], axis=0)
    padded_proj = jnp.concatenate([projected, jnp.zeros((1, projected.shape[1]), jnp.bfloat16)], axis=0)
    return (padded_dy[slot_token], slot_weight, padded_mask[slot_token], padded_proj[slot_token], in_window, slot_index, loop_mask)


def finish(in_window, slot_index, back_mix, back_down, sender_output_gradient, loop_mask):
    position = jnp.minimum(slot_index, back_mix.shape[0] - 1)
    combine_weight_gradient = jnp.where(in_window, back_mix[position], 0.0)
    pulled = back_down[position]
    summed = jnp.sum(jnp.where(in_window[:, :, None], pulled, 0.0), axis=1)
    summed = lax.optimization_barrier(summed.astype(jnp.bfloat16)).astype(jnp.float32)
    masked_sum = summed[:, None, :] * loop_mask[:, :, None]
    grad_out = jnp.einsum("td,tlk->ldk", sender_output_gradient.astype(jnp.float32), masked_sum)
    return combine_weight_gradient, grad_out


def reference(cotangent, hidden, down_matrix, adapter_in, adapter_out, probs, routes, token_loop):
    owner_devices = N_EXPERT
    groups = N_DP
    slot_count = owner_devices * SLOT_CAPACITY
    down_matrix_float = down_matrix.astype(jnp.float32)
    adapter_in_float = adapter_in.astype(jnp.float32)
    adapter_out_float = adapter_out.astype(jnp.float32)
    inputs = (cotangent.reshape(groups, owner_devices, TOK_DEV, MODEL_DIM), probs.reshape(groups, owner_devices, TOK_DEV, EXPERTS_PER_TOKEN), routes.reshape(groups, owner_devices, TOK_DEV, EXPERTS_PER_TOKEN), token_loop.reshape(groups, owner_devices, TOK_DEV), hidden)
    per_sender = jax.vmap(partial(sender_portion, adapter_out_float=adapter_out_float, owner_devices=owner_devices, slot_capacity=SLOT_CAPACITY))

    def to_owner(values):
        shaped = values.reshape((owner_devices, owner_devices, SLOT_CAPACITY) + values.shape[2:])
        return jnp.swapaxes(shaped, 0, 1).reshape((owner_devices, slot_count) + values.shape[2:])

    def one_group(running, group_inputs):
        sum_weight, sum_in, sum_out = running
        group_dy, group_probs, group_routes, group_loop, group_hidden = group_inputs
        slot_dy, slot_weight, slot_mask, slot_proj, in_window, slot_index, loop_mask = per_sender(group_dy, group_probs, group_routes, group_loop)
        owner_output_gradient = to_owner(slot_dy).astype(jnp.float32)
        owner_weight = to_owner(slot_weight)
        owner_mask = to_owner(slot_mask)
        owner_proj = to_owner(slot_proj).astype(jnp.float32)
        hidden_float = group_hidden.astype(jnp.float32)
        masked_projection = owner_proj[:, :, None, :] * owner_mask[:, :, :, None]
        input_gradient = jnp.einsum("wug,wgh->wuh", owner_output_gradient, down_matrix_float) + jnp.einsum("phiq,iqt->pht", masked_projection, adapter_in_float)
        hidden_gradient = (owner_weight[:, :, None] * input_gradient).astype(jnp.bfloat16)
        grad_mix = jnp.sum(hidden_float * input_gradient, axis=2)
        scaled = lax.optimization_barrier((owner_weight[:, :, None] * owner_output_gradient).astype(jnp.bfloat16)).astype(jnp.float32)
        sum_weight = sum_weight + jnp.einsum("erd,erf->edf", scaled, hidden_float)
        weighted_proj = lax.optimization_barrier((owner_weight[:, :, None] * owner_proj).astype(jnp.bfloat16)).astype(jnp.float32)
        masked_weighted = weighted_proj[:, :, None, :] * owner_mask[:, :, :, None]
        sum_in = sum_in + jnp.einsum("erlk,erf->lkf", masked_weighted, hidden_float)
        down_weight_stack = jnp.einsum("jog,hpg->johp", hidden_float, adapter_in_float)
        weighted_down = owner_weight[:, :, None] * jnp.sum(down_weight_stack * owner_mask[:, :, :, None], axis=2)
        back_mix = to_owner(grad_mix)
        back_down = to_owner(weighted_down)
        combine_weight_gradient, grad_out = jax.vmap(finish)(in_window, slot_index, back_mix, back_down, group_dy, loop_mask)
        sum_out = sum_out + jnp.sum(grad_out, axis=0)
        return (sum_weight, sum_in, sum_out), (hidden_gradient, combine_weight_gradient)

    start_state = (jnp.zeros((owner_devices, MODEL_DIM, HIDDEN_UNITS), jnp.float32), jnp.zeros((LOOP_TOTAL, ADAPTER_RANK, HIDDEN_UNITS), jnp.float32), jnp.zeros((LOOP_TOTAL, MODEL_DIM, ADAPTER_RANK), jnp.float32))
    closing_state, stacked = lax.scan(one_group, start_state, inputs)
    down_matrix_gradient, adapter_in_gradient, adapter_out_gradient = closing_state
    hidden_gradient, combine_weight_gradient = stacked
    return (hidden_gradient, down_matrix_gradient, combine_weight_gradient.reshape(TOKEN_TOTAL, EXPERTS_PER_TOKEN), adapter_in_gradient, adapter_out_gradient)
```

```python
import functools

import jax
import jax.numpy as jnp
from jax import lax
from jax.experimental import pallas as pl
from jax.experimental.pallas import tpu as pltpu
from jax.sharding import PartitionSpec as P

bf16 = jnp.bfloat16
f32 = jnp.float32
LANES = 128
MIB = 1 << 20


def dot(a, b, dims):
    return lax.dot_general(a, b, (dims, ((), ())), preferred_element_type=f32)


def nn(a, b):
    return dot(a, b, ((1,), (0,)))


def nt(a, b):
    return dot(a, b, ((1,), (1,)))


def tn(a, b):
    return dot(a, b, ((0,), (0,)))


def swap(x, axis, size, mask):
    return lax.ppermute(x, axis, [(i, i ^ mask) for i in range(size)])


def call(body, out_shape, ins, scratch=(), limit=24 * MIB, cost=None):
    specs = [pl.BlockSpec(memory_space=s) for s in ins]
    outs = jax.tree.map(lambda _: pl.BlockSpec(memory_space=pltpu.VMEM), out_shape)
    return pl.pallas_call(
        body,
        out_shape=out_shape,
        in_specs=specs,
        out_specs=outs,
        scratch_shapes=list(scratch),
        cost_estimate=cost,
        compiler_params=pltpu.CompilerParams(vmem_limit_bytes=limit),
    )


def cost(flops, nbytes):
    return pl.CostEstimate(flops=int(flops), bytes_accessed=int(nbytes), transcendentals=0)


def owner_column(place, chips, experts):
    j = lax.broadcasted_iota(jnp.int32, (experts, 1), 0)
    half, hop = j // chips, j % chips
    return ((place // 2) ^ hop) * 2 + ((place % 2) ^ half)


def route_body(chips, cap, place, routes, probs, loops, cot, keep, give, picks, mixed):
    experts = 2 * chips
    ways, toks = routes.shape
    width = cot.shape[1]
    owner = owner_column(place[0], chips, experts)
    named = jnp.zeros((experts, toks), f32)
    weight = jnp.zeros((experts, toks), f32)
    for k in range(ways):
        hit = routes[k : k + 1, :] == owner
        named = named + jnp.where(hit, 1.0, 0.0)
        weight = weight + jnp.where(hit, probs[k : k + 1, :].astype(f32), 0.0)
    earlier = lax.broadcasted_iota(jnp.int32, (toks, toks), 0) < lax.broadcasted_iota(
        jnp.int32, (toks, toks), 1
    )
    before = nn(named.astype(bf16), jnp.where(earlier, 1.0, 0.0).astype(bf16))
    spot = jnp.where(named > 0.0, before, -1.0)
    slot = lax.broadcasted_iota(jnp.int32, (cap, toks), 0).astype(f32)
    for j in range(experts):
        hit = spot[j : j + 1, :] == slot
        rows = slice(j * cap, (j + 1) * cap)
        picks[rows, :] = jnp.where(hit, 1.0, 0.0).astype(bf16)
        mixed[rows, :] = jnp.where(hit, weight[j : j + 1, :], 0.0).astype(bf16)
    loop_rows = lax.broadcasted_iota(jnp.int32, (LANES, toks), 0) == loops[...]
    mix = nt(mixed[...], jnp.where(loop_rows, 1.0, 0.0).astype(bf16)).astype(bf16)
    half = chips * cap
    keep[:, :, width:] = mix[:half].reshape(chips, cap, LANES)
    give[:, :, width:] = mix[half:].reshape(chips, cap, LANES)
    step = min(width, 512)
    for at in range(0, width, step):
        got = nn(picks[...], cot[:, at : at + step]).astype(bf16)
        keep[:, :, at : at + step] = got[:half].reshape(chips, cap, step)
        give[:, :, at : at + step] = got[half:].reshape(chips, cap, step)


def arrive_body(groups, cap, n_far, place, adapter_out, near, sib, *refs):
    far, outs = refs[:n_far], refs[n_far:]
    rows_out, masked_out, parts = outs[0], outs[1], outs[2:]
    loops, width, rank = adapter_out.shape
    e, i = place[0], place[1]
    z, c = e // 2, e % 2
    blocks = [(z * 2 + c, near[0]), (z * 2 + (1 - c), sib[0])]
    for hop in range(1, n_far + 1):
        pair = far[hop - 1]
        blocks += [((z ^ hop) * 2 + c, pair[0]), ((z ^ hop) * 2 + (1 - c), pair[1])]
    for source, block in blocks:
        rows_out[pl.ds(pl.multiple_of(source * cap, cap), cap), :] = block
    mix = rows_out[:, width:].astype(f32)
    weight = jnp.sum(mix, axis=1, keepdims=True)
    part = width // groups
    for hop in range(groups):
        at = pl.multiple_of((i ^ hop) * part, part)
        piece = rows_out[:, pl.ds(at, part)].astype(f32)
        parts[hop][:, :part] = (weight * piece).astype(bf16)
    proj = jnp.zeros((rows_out.shape[0], rank), f32)
    rows = rows_out[:, :width]
    masks = []
    for l in range(loops):
        mask = mix[:, l : l + 1] > 0.0
        masks.append(mask)
        proj = proj + jnp.where(mask, nn(rows, adapter_out[l]), 0.0)
    proj = proj.astype(bf16).astype(f32)
    for l in range(loops):
        masked_out[:, l * rank : (l + 1) * rank] = jnp.where(masks[l], proj, 0.0).astype(bf16)
    weighted = (weight * proj).astype(bf16)
    mix_block = mix.astype(bf16)
    for hop in range(groups):
        parts[hop][:, part : part + rank] = weighted
        parts[hop][:, part + rank :] = mix_block


def inner_body(steps, rows, down, masked, adapter_in, hidden, grad_out, mix_out, total):
    step = pl.program_id(0)
    width = rows.shape[1] - LANES
    part = width // steps
    at = pl.multiple_of(step * part, part)
    term = nn(rows[:, pl.ds(at, part)], down[...])

    @pl.when(step == 0)
    def _():
        total[...] = term + nn(masked[...], adapter_in[...])

    @pl.when(step > 0)
    def _():
        total[...] += term

    @pl.when(step == steps - 1)
    def _():
        grad = total[...]
        weight = jnp.sum(rows[:, width:].astype(f32), axis=1, keepdims=True)
        grad_out[...] = (weight * grad).astype(bf16)
        mix_out[...] = jnp.broadcast_to(
            jnp.sum(hidden[...].astype(f32) * grad, axis=1, keepdims=True), mix_out.shape
        )


def adapter_body(groups, loops, chips, part, cols, place, adapter_in, *refs):
    rows = refs[:groups]
    hids = refs[groups : 2 * groups]
    keep, give, sums, narrow = refs[2 * groups :]
    rank = adapter_in.shape[0] // loops
    share = rank // (2 * chips)
    hid_width = hids[0].shape[1]
    wide = keep.shape[2] - part
    e, i = place[0], place[1]
    pick = lax.broadcasted_iota(jnp.int32, (hid_width, wide), 0)
    lane = lax.broadcasted_iota(jnp.int32, (hid_width, wide), 1)
    pick = jnp.where((pick == lane + i * cols) & (lane < cols), 1.0, 0.0).astype(bf16)
    out = jnp.zeros((loops * rank, part), f32)
    inn = jnp.zeros((loops * rank, wide), f32)
    for g in range(groups):
        hid = hids[g][...]
        down = nt(hid, adapter_in[...])
        mix = rows[g][:, part + rank :].astype(f32)
        weighted = rows[g][:, part : part + rank].astype(f32)
        picked = nn(hid, pick).astype(bf16)
        masks = [mix[:, l : l + 1] > 0.0 for l in range(loops)]
        lefts = [
            jnp.where(masks[l], down[:, l * rank : (l + 1) * rank], 0.0) for l in range(loops)
        ]
        out = out + tn(jnp.concatenate(lefts, axis=1).astype(bf16), rows[g][:, :part])
        lefts = [jnp.where(masks[l], weighted, 0.0) for l in range(loops)]
        inn = inn + tn(jnp.concatenate(lefts, axis=1).astype(bf16), picked)
    sums[...] = out
    narrow[...] = inn
    z, c = e // 2, e % 2
    for hop in range(chips):
        for half, target in ((0, keep), (1, give)):
            owner = (z ^ hop) * 2 + (c ^ half)
            for l in range(loops):
                src = pl.ds(pl.multiple_of(l * rank + owner * share, share), share)
                dst = slice(l * share, (l + 1) * share)
                target[hop, dst, :part] = sums[src, :]
                target[hop, dst, part:] = narrow[src, :]


def pair_body(chips, cap, part, cols, place, keep, got, mix, got_mix, *outs):
    e = place[0]
    z, c = e // 2, e % 2
    wide = keep.shape[2] - part
    lane = lax.broadcasted_iota(jnp.int32, (cap, wide), 1)
    for hop in range(chips):
        total = keep[hop] + got[hop]
        outs[hop][:, :part] = total[:, :part].astype(bf16)
        own = mix[pl.ds(pl.multiple_of(((z ^ hop) * 2 + c) * cap, cap), cap), :]
        sib = got_mix[pl.ds(pl.multiple_of(((z ^ hop) * 2 + c) * cap, cap), cap), :]
        tail = total[:, part:]
        words = []
        for value in (own, sib):
            value = value[:, :1]
            high = value.astype(bf16).astype(f32)
            words += [high, value - high]
        first = tail[:cap]
        for n, word in enumerate(words):
            first = jnp.where(lane == cols + n, word, first)
        outs[hop][:cap, part:] = first.astype(bf16)
        if tail.shape[0] > cap:
            outs[hop][cap:, part:] = tail[cap:].astype(bf16)


def final_body(chips, cap, part, cols, loops, place, routes, picks, *refs):
    blocks, (out_grad, in_grad, combine) = refs[:chips], refs[chips:]
    experts = 2 * chips
    share = out_grad.shape[1]
    total = blocks[0][:, :part].astype(f32)
    tail = blocks[0][:, part:].astype(f32)
    for hop in range(1, chips):
        total = total + blocks[hop][:, :part].astype(f32)
        tail = tail + blocks[hop][:, part:].astype(f32)
    for l in range(loops):
        out_grad[l] = total[l * share : (l + 1) * share]
        in_grad[l] = tail[l * share : (l + 1) * share, :cols]
    owner = owner_column(place[0], chips, experts)
    ways, toks = routes.shape
    sums = jnp.zeros((ways, toks), f32)
    for j in range(experts):
        half, hop = j // chips, j % chips
        words = blocks[hop][:cap, part:].astype(f32)
        at = cols + 2 * half
        value = words[:, at : at + 1] + words[:, at + 1 : at + 2]
        pick = picks[j * cap : (j + 1) * cap, :].astype(f32)
        by_token = jnp.sum(pick * value, axis=0, keepdims=True)
        sums = sums + jnp.where(routes[...] == owner[j : j + 1, :], by_token, 0.0)
    combine[...] = sums


def product_body(groups, part, *refs):
    rows, hids, out = refs[:groups], refs[groups : 2 * groups], refs[2 * groups]
    step = min(part, 256)
    lefts = jnp.concatenate([r[:, :part] for r in rows], axis=0)
    rights = jnp.concatenate([h[...] for h in hids], axis=0)
    for at in range(0, part, step):
        out[0, at : at + step, :] = tn(lefts[:, at : at + step], rights)


def on_device(cotangent, hidden, down_matrix, adapter_in, adapter_out, probs, routes, token_loop):
    experts = lax.axis_size("expert")
    groups = lax.axis_size("dp")
    chips = experts // 2
    toks, width = cotangent.shape
    loops, rank, hid_width = adapter_in.shape
    ways = routes.shape[1]
    slots = hidden.shape[2]
    cap = slots // experts
    part = width // groups
    cols = hid_width // groups
    share = rank // experts
    packed = width + LANES
    S, V = pltpu.SMEM, pltpu.VMEM
    place = jnp.stack([lax.axis_index("expert"), lax.axis_index("dp")]).astype(jnp.int32)
    routes_t = routes.T
    hid = hidden.reshape(slots, hid_width)
    flat_in = adapter_in.reshape(loops * rank, hid_width)

    def shape(dims, kind):
        return jax.ShapeDtypeStruct(dims, kind)

    with jax.named_scope("route"):
        keep, give, picks = call(
            functools.partial(route_body, chips, cap),
            (
                shape((chips, cap, packed), bf16),
                shape((chips, cap, packed), bf16),
                shape((slots, toks), bf16),
            ),
            (S, V, V, V, V),
            scratch=(pltpu.VMEM((slots, toks), bf16),),
            cost=cost(2 * slots * toks * width, 4 * toks * width),
        )(place, routes_t, probs.T, token_loop.reshape(1, toks), cotangent)
    with jax.named_scope("dispatch"):
        sib = swap(give, "expert", experts, 1)
        far = [
            swap(jnp.stack([keep[hop], sib[hop]]), "expert", experts, 2 * hop)
            for hop in range(1, chips)
        ]
        hids = [hid] + [swap(hid, "dp", groups, hop) for hop in range(1, groups)]
    with jax.named_scope("arrive"):
        got = call(
            functools.partial(arrive_body, groups, cap, chips - 1),
            (shape((slots, packed), bf16), shape((slots, loops * rank), bf16))
            + tuple(shape((slots, part + rank + LANES), bf16) for _ in range(groups)),
            (S,) + (V,) * (chips + 2),
            cost=cost(2 * slots * width * loops * rank, 6 * slots * width),
        )(place, adapter_out, keep, sib, *far)
        rows, masked, parts = got[0], got[1], got[2:]
    with jax.named_scope("columns"):
        pieces = [parts[0]] + [swap(parts[hop], "dp", groups, hop) for hop in range(1, groups)]
    with jax.named_scope("inner"):
        steps = max(1, width // 1024)
        grad, mix = pl.pallas_call(
            functools.partial(inner_body, steps),
            grid=(steps,),
            out_shape=(shape((slots, hid_width), bf16), shape((slots, LANES), f32)),
            in_specs=[
                pl.BlockSpec((slots, packed), lambda s: (0, 0)),
                pl.BlockSpec((width // steps, hid_width), lambda s: (s, 0)),
                pl.BlockSpec((slots, loops * rank), lambda s: (0, 0)),
                pl.BlockSpec((loops * rank, hid_width), lambda s: (0, 0)),
                pl.BlockSpec((slots, hid_width), lambda s: (0, 0)),
            ],
            out_specs=(
                pl.BlockSpec((slots, hid_width), lambda s: (0, 0)),
                pl.BlockSpec((slots, LANES), lambda s: (0, 0)),
            ),
            scratch_shapes=[pltpu.VMEM((slots, hid_width), f32)],
            cost_estimate=cost(
                2 * slots * width * hid_width, 2 * (width * hid_width + slots * width)
            ),
            compiler_params=pltpu.CompilerParams(vmem_limit_bytes=24 * MIB),
        )(rows, down_matrix[0], masked, flat_in, hid)
    with jax.named_scope("adapters"):
        wide = -(-(cols + 4) // LANES) * LANES
        block = (chips, loops * share, part + wide)
        keep3, give3 = call(
            functools.partial(adapter_body, groups, loops, chips, part, cols),
            (shape(block, f32), shape(block, f32)),
            (S,) + (V,) * (1 + 2 * groups),
            scratch=(
                pltpu.VMEM((loops * rank, part), f32),
                pltpu.VMEM((loops * rank, wide), f32),
            ),
            limit=40 * MIB,
            cost=cost(4 * groups * slots * loops * rank * part, 4 * groups * slots * part),
        )(place, flat_in, *pieces, *hids)
        got3 = swap(give3, "expert", experts, 1)
        got_mix = swap(mix, "expert", experts, 1)
        ready = call(
            functools.partial(pair_body, chips, cap, part, cols),
            tuple(shape(block[1:], bf16) for _ in range(chips)),
            (S, V, V, V, V),
            cost=cost(1e6, 2e6),
        )(place, keep3, got3, mix, got_mix)
        blocks = [ready[0]] + [
            swap(ready[hop], "expert", experts, 2 * hop) for hop in range(1, chips)
        ]
    with jax.named_scope("product"):
        product = call(
            functools.partial(product_body, groups, part),
            shape((1, part, hid_width), f32),
            (V,) * (2 * groups),
            limit=40 * MIB,
            cost=cost(2 * groups * slots * part * hid_width, 4 * groups * slots * part),
        )(*pieces, *hids)
    with jax.named_scope("final"):
        out_grad, in_grad, combine = call(
            functools.partial(final_body, chips, cap, part, cols, loops),
            (
                shape((loops, share, part), f32),
                shape((loops, share, cols), f32),
                shape((ways, toks), f32),
            ),
            (S, V, V) + (V,) * chips,
            cost=cost(1e6, 2e6),
        )(place, routes_t, picks, *blocks)
    return (
        grad.reshape(hidden.shape),
        product,
        combine.T,
        in_grad,
        jnp.swapaxes(out_grad, 1, 2),
    )


def solution(mesh):
    return jax.shard_map(
        on_device,
        mesh=mesh,
        in_specs=(
            P(("dp", "expert"), None),
            P("dp", "expert", None, None),
            P("expert", None, None),
            P(),
            P(),
            P(("dp", "expert"), None),
            P(("dp", "expert"), None),
            P(("dp", "expert")),
        ),
        out_specs=(
            P("dp", "expert", None, None),
            P("expert", "dp", None),
            P(("dp", "expert"), None),
            P(None, "expert", "dp"),
            P(None, "dp", "expert"),
        ),
        check_vma=False,
    )
```

```python
import functools

import jax
import jax.numpy as jnp
from jax import lax
from jax.experimental import pallas as pl
from jax.experimental.pallas import tpu as pltpu
from jax.sharding import PartitionSpec as P

bf16 = jnp.bfloat16
f32 = jnp.float32
LANES = 128
MIB = 1 << 20
V, A = pltpu.VMEM, pl.ANY


def dot(a, b, dims):
    return lax.dot_general(a, b, (dims, ((), ())), preferred_element_type=f32)


def nn(a, b):
    return dot(a, b, ((1,), (0,)))


def nt(a, b):
    return dot(a, b, ((1,), (1,)))


def tn(a, b):
    return dot(a, b, ((0,), (0,)))


def swap(x, axis, size, mask):
    return lax.ppermute(x, axis, [(i, i ^ mask) for i in range(size)])


def shape(dims, kind):
    return jax.ShapeDtypeStruct(dims, kind)


def here():
    return lax.axis_index("expert"), lax.axis_index("dp")


def call(body, out_shape, ins, scratch=(), limit=24, flops=0, nbytes=0):
    return pl.pallas_call(
        body,
        out_shape=out_shape,
        in_specs=[pl.BlockSpec(memory_space=s) for s in ins],
        out_specs=jax.tree.map(lambda _: pl.BlockSpec(memory_space=V), out_shape),
        scratch_shapes=list(scratch),
        cost_estimate=pl.CostEstimate(
            flops=int(flops), bytes_accessed=int(nbytes), transcendentals=0
        ),
        compiler_params=pltpu.CompilerParams(vmem_limit_bytes=limit * MIB),
    )


def owner_column(place, chips, experts):
    j = lax.broadcasted_iota(jnp.int32, (experts, 1), 0)
    half, hop = j // chips, j % chips
    return ((place[0] // 2) ^ hop) * 2 + ((place[0] % 2) ^ half)


def route_body(chips, cap, ways, small, cot, keep, give, picks, mixed):
    experts = 2 * chips
    toks, width = cot.shape
    owner = owner_column(here(), chips, experts).astype(f32)
    named = jnp.zeros((experts, toks), f32)
    weight = jnp.zeros((experts, toks), f32)
    for k in range(ways):
        hit = small[k : k + 1, :] == owner
        named = named + jnp.where(hit, 1.0, 0.0)
        weight = weight + jnp.where(hit, small[ways + k : ways + k + 1, :], 0.0)
    earlier = lax.broadcasted_iota(jnp.int32, (toks, toks), 0) < lax.broadcasted_iota(
        jnp.int32, (toks, toks), 1
    )
    before = nn(named.astype(bf16), jnp.where(earlier, 1.0, 0.0).astype(bf16))
    spot = jnp.where(named > 0.0, before, -1.0)
    slot = lax.broadcasted_iota(jnp.int32, (cap, toks), 0).astype(f32)
    for j in range(experts):
        hit = spot[j : j + 1, :] == slot
        rows = slice(j * cap, (j + 1) * cap)
        picks[rows, :] = jnp.where(hit, 1.0, 0.0).astype(bf16)
        mixed[rows, :] = jnp.where(hit, weight[j : j + 1, :], 0.0).astype(bf16)
    loop_rows = lax.broadcasted_iota(jnp.int32, (LANES, toks), 0).astype(f32)
    loop_rows = jnp.where(loop_rows == small[2 * ways : 2 * ways + 1, :], 1.0, 0.0).astype(bf16)
    mix = nt(mixed[...], loop_rows).astype(bf16)
    half = chips * cap
    keep[:, :, width:] = mix[:half].reshape(chips, cap, LANES)
    give[:, :, width:] = mix[half:].reshape(chips, cap, LANES)
    step = 1024 if width % 1024 == 0 else width
    for n in range(0, width, step):
        at = slice(n, n + step)
        got = nn(picks[...], cot[:, at]).astype(bf16)
        keep[:, :, at] = got[:half].reshape(chips, cap, step)
        give[:, :, at] = got[half:].reshape(chips, cap, step)


def sources(place, chips):
    z, c = place[0] // 2, place[0] % 2
    return [(z ^ hop) * 2 + (c ^ half) for hop in range(chips) for half in range(2)]


def pack_far_body(chips, keep, sib, *far):
    for n, block in enumerate(far):
        hop = chips - len(far) + n
        block[0] = keep[hop]
        block[1] = sib[hop]


def pack_near_body(chips, cap, keep, sib, hidden, _, ordered, *near):
    for n, block in enumerate(near):
        block[0] = keep[1 + n]
        block[1] = sib[1 + n]
    for n, source in enumerate(sources(here(), chips)):
        rows = pl.ds(pl.multiple_of(source * cap, cap), cap)
        ordered[n * cap : (n + 1) * cap, :] = hidden[rows, :]


def arrive_body(groups, near, adapter_out, *refs):
    blocks = refs[: -2 - groups]
    rows, masked, parts = refs[-2 - groups], refs[-1 - groups], refs[-groups:]
    loops, width, rank = adapter_out.shape
    part = width // groups
    at = 0
    for n, block in enumerate(blocks):
        halves = (block[0],) if near and n < 2 else (block[0], block[1])
        for piece in halves:
            rows[at : at + piece.shape[0], :] = piece
            at += piece.shape[0]
    mix_block = rows[:, width:]
    mix = mix_block.astype(f32)
    weight = jnp.sum(mix, axis=1, keepdims=True)
    for hop in range(groups):
        start = pl.multiple_of((here()[1] ^ hop) * part, part)
        parts[hop][:, :part] = (weight * rows[:, pl.ds(start, part)].astype(f32)).astype(bf16)
    masks = [mix[:, l : l + 1] > 0.0 for l in range(loops)]
    proj = jnp.zeros((rows.shape[0], rank), f32)
    for l in range(loops):
        proj = proj + jnp.where(masks[l], nn(rows[:, :width], adapter_out[l]), 0.0)
    proj = proj.astype(bf16).astype(f32)
    for l in range(loops):
        masked[:, l * rank : (l + 1) * rank] = jnp.where(masks[l], proj, 0.0).astype(bf16)
    weighted = (weight * proj).astype(bf16)
    for hop in range(groups):
        parts[hop][:, part : part + rank] = weighted
        parts[hop][:, part + rank :] = mix_block


def inner_body(chips, cap, early, late, down, masked1, masked2, adapter_in, hidden, *refs):
    grad_out, mix_out = refs
    width, hid_width = down.shape
    step = 256 if hid_width % 256 == 0 else hid_width
    rows = jnp.concatenate([early[...], late[...]], axis=0)
    masked = jnp.concatenate([masked1[...], masked2[...]], axis=0)
    weight = jnp.sum(rows[:, width:].astype(f32), axis=1, keepdims=True)
    sums = jnp.zeros((mix_out.shape[0], 1), f32)
    order = sources(here(), chips)
    for at in range(0, hid_width, step):
        cols = slice(at, at + step)
        grad = nn(masked, adapter_in[:, cols]) + nn(rows[:, :width], down[:, cols])
        sums = sums + jnp.sum(hidden[: mix_out.shape[0], cols].astype(f32) * grad, axis=1, keepdims=True)
        scaled = (weight * grad).astype(bf16)
        for n, source in enumerate(order):
            spot = pl.ds(pl.multiple_of(source * cap, cap), cap)
            grad_out[spot, cols] = scaled[n * cap : (n + 1) * cap]
    mix_out[...] = jnp.broadcast_to(sums, mix_out.shape)


def adapter_sums(groups, loops, cols, start, adapter_in, rows, hids):
    slots = rows[0].shape[0]
    rank = adapter_in.shape[0] // loops
    hid_width = adapter_in.shape[1]
    part = rows[0].shape[1] - rank - LANES
    wide = wide_of(cols)
    row = lax.broadcasted_iota(jnp.int32, (hid_width, wide), 0)
    lane = lax.broadcasted_iota(jnp.int32, (hid_width, wide), 1)
    pick = (row == lane + here()[1] * cols) & (lane < cols)
    pick = jnp.where(pick, 1.0, 0.0).astype(bf16)
    total = hids.shape[0] // groups
    hid = jnp.concatenate(
        [hids[g * total + start : g * total + start + slots, :] for g in range(groups)], axis=0
    )
    tail = jnp.concatenate([r[:, part:] for r in rows], axis=0).astype(f32)
    body = jnp.concatenate([r[:, :part] for r in rows], axis=0)
    down = nt(hid, adapter_in[...])
    picked = nn(hid, pick).astype(bf16)
    masks = [tail[:, rank + l : rank + l + 1] > 0.0 for l in range(loops)]
    left = [jnp.where(masks[l], down[:, l * rank : (l + 1) * rank], 0.0) for l in range(loops)]
    out = tn(jnp.concatenate(left, axis=1).astype(bf16), body)
    left = [jnp.where(masks[l], tail[:, :rank], 0.0) for l in range(loops)]
    return out, tn(jnp.concatenate(left, axis=1).astype(bf16), picked)


def wide_of(cols):
    return -(-(cols + 4) // LANES) * LANES


def adapter_first_body(groups, loops, cols, adapter_in, hids, *refs):
    rows, (out, inn) = refs[:groups], refs[groups:]
    out[...], inn[...] = adapter_sums(groups, loops, cols, 0, adapter_in, rows, hids)


def adapter_last_body(groups, loops, chips, cap, cols, adapter_in, out, inn, mix, hids, *refs):
    rows, (keep, give, sums, narrow) = refs[:groups], refs[groups:]
    slots = rows[0].shape[0]
    rank = adapter_in.shape[0] // loops
    part = out.shape[1]
    share = rank // (2 * chips)
    start = mix.shape[0] - slots
    more = adapter_sums(groups, loops, cols, start, adapter_in, rows, hids)
    sums[...] = out[...] + more[0]
    narrow[...] = inn[...] + more[1]
    owners = sources(here(), chips)
    lane = lax.broadcasted_iota(jnp.int32, (cap, narrow.shape[1]), 1)
    for n, owner in enumerate(owners):
        hop, target = n // 2, (keep, give)[n % 2]
        for l in range(loops):
            src = pl.ds(pl.multiple_of(l * rank + owner * share, share), share)
            dst = slice(l * share, (l + 1) * share)
            target[hop, dst, :part] = sums[src, :]
            target[hop, dst, part:] = narrow[src, :]
        value = mix[n * cap : (n + 1) * cap, :1]
        target[hop, :cap, part:] = jnp.where(lane == cols, value, target[hop, :cap, part:])


def pair_body(chips, cap, part, cols, keep, got, *outs):
    wide = keep.shape[2] - part
    lane = lax.broadcasted_iota(jnp.int32, (cap, wide), 1)
    for hop in range(chips):
        outs[hop][...] = (keep[hop] + got[hop]).astype(bf16)
        tail = keep[hop, :cap, part:] + got[hop, :cap, part:]
        for n, block in enumerate((keep, got)):
            value = block[hop, :cap, part + cols : part + cols + 1]
            high = value.astype(bf16).astype(f32)
            tail = jnp.where(lane == cols + 2 * n, high, tail)
            tail = jnp.where(lane == cols + 2 * n + 1, value - high, tail)
        outs[hop][:cap, part:] = tail.astype(bf16)


def final_body(chips, cap, cols, small, picks, *refs):
    blocks = refs[:chips]
    out_grad, in_grad, combine = refs[chips:]
    loops, share, part = out_grad.shape
    total = blocks[0][...].astype(f32)
    for hop in range(1, chips):
        total = total + blocks[hop][...].astype(f32)
    for l in range(loops):
        rows = slice(l * share, (l + 1) * share)
        out_grad[l] = total[rows, :part]
        in_grad[l] = total[rows, part : part + cols]
    experts = 2 * chips
    owner = owner_column(here(), chips, experts).astype(f32)
    routes = small[: combine.shape[0], :]
    sums = jnp.zeros(combine.shape, f32)
    for j in range(experts):
        half, hop = j // chips, j % chips
        words = blocks[hop][:cap, part:].astype(f32)
        at = cols + 2 * half
        value = words[:, at : at + 1] + words[:, at + 1 : at + 2]
        pick = picks[j * cap : (j + 1) * cap, :].astype(f32)
        by_token = jnp.sum(pick * value, axis=0, keepdims=True)
        sums = sums + jnp.where(routes == owner[j : j + 1, :], by_token, 0.0)
    combine[...] = sums


def product_body(groups, *refs):
    early, late = refs[:groups], refs[groups : 2 * groups]
    hids, out = refs[2 * groups :]
    part = out.shape[1]
    rights = hids[...]
    step = 256 if part % 256 == 0 else LANES
    for at in range(0, part, step):
        left = [p[:, at : at + step] for pair in zip(early, late) for p in pair]
        out[0, at : at + step, :] = tn(jnp.concatenate(left, axis=0), rights)


def on_device(cotangent, hidden, down_matrix, adapter_in, adapter_out, probs, routes, token_loop):
    experts = lax.axis_size("expert")
    groups = lax.axis_size("dp")
    chips = experts // 2
    toks, width = cotangent.shape
    loops, rank, hid_width = adapter_in.shape
    ways = routes.shape[1]
    slots = hidden.shape[2]
    cap = slots // experts
    part = width // groups
    cols = hid_width // groups
    wide = wide_of(cols)
    share = rank // experts
    half = slots // 2
    flat_in = adapter_in.reshape(loops * rank, hid_width)
    small = jnp.concatenate(
        [routes.T.astype(f32), probs.T.astype(f32), token_loop.astype(f32).reshape(1, toks)]
    )

    with jax.named_scope("route"):
        packed = shape((chips, cap, width + LANES), bf16)
        keep, give, picks = call(
            functools.partial(route_body, chips, cap, ways),
            (packed, packed, shape((slots, toks), bf16)),
            (V, V),
            scratch=(pltpu.VMEM((slots, toks), bf16),),
            flops=2 * slots * toks * width,
            nbytes=6 * toks * width,
        )(small, cotangent)
        sib = swap(give, "expert", experts, 1)
    with jax.named_scope("dispatch"):
        pair = shape((2, cap, width + LANES), bf16)
        middle = chips // 2
        packs = call(
            functools.partial(pack_far_body, chips),
            (pair,) * (chips - middle),
            (V, V),
            nbytes=2 * slots * width,
        )(keep, sib)
        far = [swap(x, "expert", experts, 2 * (middle + n)) for n, x in enumerate(packs)]
        got = call(
            functools.partial(pack_near_body, chips, cap),
            (shape((slots, hid_width), bf16),) + (pair,) * (middle - 1),
            (V, V, V, A),
            nbytes=2 * slots * width,
        )(keep, sib, hidden.reshape(slots, hid_width), packs[0])
        near = [swap(x, "expert", experts, 2 * (1 + n)) for n, x in enumerate(got[1:])]
        hids, hop = got[0], 1
        while hop < groups:
            hids = jnp.concatenate([hids, swap(hids, "dp", groups, hop)])
            hop *= 2
    with jax.named_scope("arrive"):
        rows, masked, parts = [], [], []
        for own, blocks in ((True, [keep, sib] + near), (False, far)):
            got = call(
                functools.partial(arrive_body, groups, own),
                (shape((half, width + LANES), bf16), shape((half, loops * rank), bf16))
                + (shape((half, part + rank + LANES), bf16),) * groups,
                (V,) * (1 + len(blocks)),
                flops=2 * half * width * loops * rank,
                nbytes=4 * half * width,
            )(adapter_out, *blocks)
            rows.append(got[0])
            masked.append(got[1])
            parts.append(
                [got[2]] + [swap(got[2 + hop], "dp", groups, hop) for hop in range(1, groups)]
            )
    with jax.named_scope("inner"):
        grad, mix = call(
            functools.partial(inner_body, chips, cap),
            (shape((slots, hid_width), bf16), shape((slots, LANES), f32)),
            (V,) * 7,
            flops=2 * slots * width * hid_width,
            nbytes=2 * width * hid_width,
        )(*rows, down_matrix[0], *masked, flat_in, hids)
    with jax.named_scope("adapters"):
        work = 2 * groups * half * loops * rank * (part + hid_width + wide)
        sums = (shape((loops * rank, part), f32), shape((loops * rank, wide), f32))
        out, inn = call(
            functools.partial(adapter_first_body, groups, loops, cols),
            sums,
            (V,) * (2 + groups),
            flops=work,
            nbytes=2 * groups * half * part,
        )(flat_in, hids, *parts[0])
        block = (chips, loops * share, part + wide)
        keep3, give3 = call(
            functools.partial(adapter_last_body, groups, loops, chips, cap, cols),
            (shape(block, f32), shape(block, f32)),
            (V,) * (5 + groups),
            scratch=[pltpu.VMEM(s.shape, f32) for s in sums],
            flops=work,
            nbytes=2 * groups * half * part,
        )(flat_in, out, inn, mix, hids, *parts[1])
        got3 = swap(give3, "expert", experts, 1)
        ready = call(
            functools.partial(pair_body, chips, cap, part, cols),
            (shape(block[1:], bf16),) * chips,
            (V, V),
            nbytes=1e6,
        )(keep3, got3)
        blocks = list(ready)
        for hop in reversed(range(1, chips)):
            blocks[hop] = swap(ready[hop], "expert", experts, 2 * hop)
    with jax.named_scope("product"):
        product = call(
            functools.partial(product_body, groups),
            shape((1, part, hid_width), f32),
            (V,) * (2 * groups + 1),
            limit=40,
            flops=2 * groups * slots * part * hid_width,
            nbytes=4 * groups * slots * part,
        )(*parts[0], *parts[1], hids)
    with jax.named_scope("final"):
        out_grad, in_grad, combine = call(
            functools.partial(final_body, chips, cap, cols),
            (
                shape((loops, share, part), f32),
                shape((loops, share, cols), f32),
                shape((ways, toks), f32),
            ),
            (V,) * (2 + chips),
            nbytes=1e6,
        )(small, picks, *blocks)
    return (
        grad.reshape(hidden.shape),
        product,
        combine.T,
        in_grad,
        jnp.swapaxes(out_grad, 1, 2),
    )


def solution(mesh):
    return jax.shard_map(
        on_device,
        mesh=mesh,
        in_specs=(
            P(("dp", "expert"), None),
            P("dp", "expert", None, None),
            P("expert", None, None),
            P(),
            P(),
            P(("dp", "expert"), None),
            P(("dp", "expert"), None),
            P(("dp", "expert")),
        ),
        out_specs=(
            P("dp", "expert", None, None),
            P("expert", "dp", None),
            P(("dp", "expert"), None),
            P(None, "expert", "dp"),
            P(None, "dp", "expert"),
        ),
        check_vma=False,
    )
```

```python
import functools

import jax
import jax.numpy as jnp
from jax import lax
from jax.experimental import pallas as pl
from jax.experimental.pallas import tpu as pltpu
from jax.sharding import PartitionSpec as P

bf16 = jnp.bfloat16
f32 = jnp.float32
LANES = 128
MIB = 1 << 20
V, A = pltpu.VMEM, pl.ANY


def dot(a, b, dims):
    return lax.dot_general(a, b, (dims, ((), ())), preferred_element_type=f32)


def nn(a, b):
    return dot(a, b, ((1,), (0,)))


def nt(a, b):
    return dot(a, b, ((1,), (1,)))


def tn(a, b):
    return dot(a, b, ((0,), (0,)))


def swap(x, axis, size, mask):
    return lax.ppermute(x, axis, [(i, i ^ mask) for i in range(size)])


def shape(dims, kind):
    return jax.ShapeDtypeStruct(dims, kind)


def here():
    return lax.axis_index("expert"), lax.axis_index("dp")


def call(body, out_shape, ins, scratch=(), limit=24, flops=0, nbytes=0):
    return pl.pallas_call(
        body,
        out_shape=out_shape,
        in_specs=[pl.BlockSpec(memory_space=s) for s in ins],
        out_specs=jax.tree.map(lambda _: pl.BlockSpec(memory_space=V), out_shape),
        scratch_shapes=list(scratch),
        cost_estimate=pl.CostEstimate(
            flops=int(flops), bytes_accessed=int(nbytes), transcendentals=0
        ),
        compiler_params=pltpu.CompilerParams(vmem_limit_bytes=limit * MIB),
    )


def owner_column(place, chips, experts):
    j = lax.broadcasted_iota(jnp.int32, (experts, 1), 0)
    half, hop = j // chips, j % chips
    return ((place[0] // 2) ^ hop) * 2 + ((place[0] % 2) ^ half)


def decode(small, experts, loops):
    loop = jnp.zeros_like(small)
    for l in range(1, loops):
        loop = loop + jnp.where(small >= l * (experts + 1.0), 1.0, 0.0)
    rest = small - loop * (experts + 1.0)
    route = jnp.floor(rest)
    return route, rest - route, loop[:1]


def route_body(chips, cap, loops, small, cot, keep, give, picks, mixed):
    experts = 2 * chips
    ways = small.shape[0]
    toks, width = cot.shape
    owner = owner_column(here(), chips, experts).astype(f32)
    route, chance, loop = decode(small[...], experts, loops)
    named = jnp.zeros((experts, toks), f32)
    weight = jnp.zeros((experts, toks), f32)
    for k in range(ways):
        hit = route[k : k + 1, :] == owner
        named = named + jnp.where(hit, 1.0, 0.0)
        weight = weight + jnp.where(hit, chance[k : k + 1, :], 0.0)
    earlier = lax.broadcasted_iota(jnp.int32, (toks, toks), 0) < lax.broadcasted_iota(
        jnp.int32, (toks, toks), 1
    )
    before = nn(named.astype(bf16), jnp.where(earlier, 1.0, 0.0).astype(bf16))
    spot = jnp.where(named > 0.0, before, -1.0)
    slot = lax.broadcasted_iota(jnp.int32, (cap, toks), 0).astype(f32)
    for j in range(experts):
        hit = spot[j : j + 1, :] == slot
        rows = slice(j * cap, (j + 1) * cap)
        picks[rows, :] = jnp.where(hit, 1.0, 0.0).astype(bf16)
        mixed[rows, :] = jnp.where(hit, weight[j : j + 1, :], 0.0).astype(bf16)
    loop_rows = lax.broadcasted_iota(jnp.int32, (LANES, toks), 0).astype(f32)
    loop_rows = jnp.where(loop_rows == loop, 1.0, 0.0).astype(bf16)
    mix = nt(mixed[...], loop_rows).astype(bf16)
    half = chips * cap
    keep[:, :, width:] = mix[:half].reshape(chips, cap, LANES)
    give[:, :, width:] = mix[half:].reshape(chips, cap, LANES)
    step = 1024 if width % 1024 == 0 else width
    for n in range(0, width, step):
        at = slice(n, n + step)
        got = nn(picks[...], cot[:, at]).astype(bf16)
        keep[:, :, at] = got[:half].reshape(chips, cap, step)
        give[:, :, at] = got[half:].reshape(chips, cap, step)


def sources(place, chips):
    z, c = place[0] // 2, place[0] % 2
    return [(z ^ hop) * 2 + (c ^ half) for hop in range(chips) for half in range(2)]


def pack_body(chips, keep, sib, *out):
    for hop in range(1, chips):
        out[hop - 1][0] = keep[hop]
        out[hop - 1][1] = sib[hop]


def arrive_body(groups, near, adapter_out, *refs):
    loops, width, rank = adapter_out.shape
    part = width // groups
    parts = refs[-groups:]
    blocks, (rows, masked) = refs[: -2 - groups - near], refs[-2 - groups : -groups]
    at = 0
    for n, block in enumerate(blocks):
        halves = (block[0],) if near and n < 2 else (block[0], block[1])
        for piece in halves:
            rows[at : at + piece.shape[0], :] = piece
            at += piece.shape[0]
    mix_block = rows[:, width:]
    mix = mix_block.astype(f32)
    weight = jnp.sum(mix, axis=1, keepdims=True)
    for hop in range(groups):
        start = pl.multiple_of((here()[1] ^ hop) * part, part)
        parts[hop][:, :part] = (weight * rows[:, pl.ds(start, part)].astype(f32)).astype(bf16)
    masks = [mix[:, l : l + 1] > 0.0 for l in range(loops)]
    proj = jnp.zeros((rows.shape[0], rank), f32)
    for l in range(loops):
        proj = proj + jnp.where(masks[l], nn(rows[:, :width], adapter_out[l]), 0.0)
    proj = proj.astype(bf16).astype(f32)
    for l in range(loops):
        masked[:, l * rank : (l + 1) * rank] = jnp.where(masks[l], proj, 0.0).astype(bf16)
    weighted = (weight * proj).astype(bf16)
    for hop in range(groups):
        parts[hop][:, part : part + rank] = weighted
        parts[hop][:, part + rank :] = mix_block


def inner_body(chips, cap, early, late, down, masked1, masked2, adapter_in, hidden, *refs):
    grad_out, mix_out = refs
    width, hid_width = down.shape
    step = 256 if hid_width % 256 == 0 else hid_width
    rows = jnp.concatenate([early[...], late[...]], axis=0)
    masked = jnp.concatenate([masked1[...], masked2[...]], axis=0)
    weight = jnp.sum(rows[:, width:].astype(f32), axis=1, keepdims=True)
    sums = jnp.zeros((mix_out.shape[0], 1), f32)
    order = sources(here(), chips)
    for at in range(0, hid_width, step):
        cols = slice(at, at + step)
        grad = nn(masked, adapter_in[:, cols]) + nn(rows[:, :width], down[:, cols])
        sums = sums + jnp.sum(hidden[: mix_out.shape[0], cols].astype(f32) * grad, axis=1, keepdims=True)
        scaled = (weight * grad).astype(bf16)
        for n, source in enumerate(order):
            spot = pl.ds(pl.multiple_of(source * cap, cap), cap)
            grad_out[spot, cols] = scaled[n * cap : (n + 1) * cap]
    mix_out[...] = jnp.broadcast_to(sums, mix_out.shape)


def adapter_sums(loops, cols, start, adapter_in, rows, hids):
    rank = adapter_in.shape[0] // loops
    hid_width = adapter_in.shape[1]
    slots = rows[0].shape[0]
    part = rows[0].shape[1] - rank - LANES
    wide = wide_of(cols)
    row = lax.broadcasted_iota(jnp.int32, (hid_width, wide), 0)
    lane = lax.broadcasted_iota(jnp.int32, (hid_width, wide), 1)
    pick = (row == lane + here()[1] * cols) & (lane < cols)
    pick = jnp.where(pick, 1.0, 0.0).astype(bf16)
    total = hids.shape[0] // len(rows)
    starts = [g * total + start for g in range(len(rows))]
    hid = jnp.concatenate([hids[at : at + slots, :] for at in starts], axis=0)
    tail = jnp.concatenate([r[:, part:] for r in rows], axis=0).astype(f32)
    body = jnp.concatenate([r[:, :part] for r in rows], axis=0)
    down = nt(hid, adapter_in[...])
    picked = nn(hid, pick).astype(bf16)
    masks = [tail[:, rank + l : rank + l + 1] > 0.0 for l in range(loops)]
    left = [jnp.where(masks[l], down[:, l * rank : (l + 1) * rank], 0.0) for l in range(loops)]
    out = tn(jnp.concatenate(left, axis=1).astype(bf16), body)
    left = [jnp.where(masks[l], tail[:, :rank], 0.0) for l in range(loops)]
    return out, tn(jnp.concatenate(left, axis=1).astype(bf16), picked)


def wide_of(cols):
    return -(-(cols + 4) // LANES) * LANES


def adapter_first_body(loops, chips, cap, cols, adapter_in, hids, *refs):
    rows, (out, inn, ordered) = refs[:-3], refs[-3:]
    total = hids.shape[0] // len(rows)
    for g in range(len(rows)):
        for n, source in enumerate(sources(here(), chips)):
            spot = pl.ds(pl.multiple_of(g * total + source * cap, cap), cap)
            ordered[g * total + n * cap : g * total + (n + 1) * cap, :] = hids[spot, :]
    out[...], inn[...] = adapter_sums(loops, cols, 0, adapter_in, rows, ordered)


def adapter_last_body(loops, chips, cap, cols, adapter_in, out, inn, mix, hids, *refs):
    rows, (keep, give, sums, narrow) = refs[:-4], refs[-4:]
    rank = adapter_in.shape[0] // loops
    part = out.shape[1]
    share = rank // (2 * chips)
    start = mix.shape[0] - rows[0].shape[0]
    more = adapter_sums(loops, cols, start, adapter_in, rows, hids)
    sums[...] = out[...] + more[0]
    narrow[...] = inn[...] + more[1]
    owners = sources(here(), chips)
    lane = lax.broadcasted_iota(jnp.int32, (cap, narrow.shape[1]), 1)
    for n, owner in enumerate(owners):
        hop, target = n // 2, (keep, give)[n % 2]
        for l in range(loops):
            src = pl.ds(pl.multiple_of(l * rank + owner * share, share), share)
            dst = slice(l * share, (l + 1) * share)
            target[hop, dst, :part] = sums[src, :].astype(target.dtype)
            target[hop, dst, part:] = narrow[src, :].astype(target.dtype)
        value = mix[n * cap : (n + 1) * cap, :1]
        high = value.astype(bf16).astype(f32)
        tail = target[hop, :cap, part:].astype(f32)
        tail = jnp.where(lane == cols + 2 * (n % 2), high, tail)
        tail = jnp.where(lane == cols + 2 * (n % 2) + 1, value - high, tail)
        target[hop, :cap, part:] = tail.astype(target.dtype)


def pair_body(chips, keep, got, *outs):
    for hop in range(chips):
        outs[hop][...] = (keep[hop] + got[hop].astype(f32)).astype(bf16)


def far_first(chips):
    return [0] + list(range(chips // 2, chips)) + list(range(1, chips // 2))


def final_body(chips, cap, cols, small, picks, *refs):
    order = far_first(chips)
    blocks = [refs[order.index(hop)] for hop in range(chips)]
    out_grad, in_grad, combine = refs[chips:]
    loops, share, part = out_grad.shape
    total = blocks[0][...].astype(f32)
    for hop in range(1, chips):
        total = total + blocks[hop][...].astype(f32)
    for l in range(loops):
        rows = slice(l * share, (l + 1) * share)
        out_grad[l] = total[rows, :part]
        in_grad[l] = total[rows, part : part + cols]
    experts = 2 * chips
    owner = owner_column(here(), chips, experts).astype(f32)
    routes = decode(small[...], experts, loops)[0]
    sums = jnp.zeros(combine.shape, f32)
    for j in range(experts):
        half, hop = j // chips, j % chips
        words = blocks[hop][:cap, part:].astype(f32)
        at = cols + 2 * half
        value = words[:, at : at + 1] + words[:, at + 1 : at + 2]
        pick = picks[j * cap : (j + 1) * cap, :].astype(f32)
        by_token = jnp.sum(pick * value, axis=0, keepdims=True)
        sums = sums + jnp.where(routes == owner[j : j + 1, :], by_token, 0.0)
    combine[...] = sums


def product_body(groups, *refs):
    early, late = refs[:groups], refs[groups : 2 * groups]
    hids, out = refs[2 * groups :]
    part = out.shape[1]
    rights = hids[...]
    step = 256 if part % 256 == 0 else LANES
    for at in range(0, part, step):
        left = [p[:, at : at + step] for pair in zip(early, late) for p in pair]
        out[0, at : at + step, :] = tn(jnp.concatenate(left, axis=0), rights)


def on_device(cotangent, hidden, down_matrix, adapter_in, adapter_out, probs, routes, token_loop):
    experts = lax.axis_size("expert")
    groups = lax.axis_size("dp")
    chips = experts // 2
    toks, width = cotangent.shape
    loops, rank, hid_width = adapter_in.shape
    ways = routes.shape[1]
    slots = hidden.shape[2]
    cap = slots // experts
    part = width // groups
    cols = hid_width // groups
    wide = wide_of(cols)
    share = rank // experts
    half = slots // 2
    flat_in = adapter_in.reshape(loops * rank, hid_width)
    small = token_loop.reshape(1, toks) * (experts + 1) + jnp.minimum(routes.T, experts)
    small = small.astype(f32) + probs.T.astype(f32)

    with jax.named_scope("hidden"):
        natural = hidden.reshape(slots, hid_width)
        pair = jnp.concatenate([natural] + [swap(natural, "dp", groups, hop) for hop in range(1, groups)])
    with jax.named_scope("route"):
        packed = shape((chips, cap, width + LANES), bf16)
        keep, give, picks = call(
            functools.partial(route_body, chips, cap, loops),
            (packed, packed, shape((slots, toks), bf16)),
            (V, V),
            scratch=(pltpu.VMEM((slots, toks), bf16),),
            flops=2 * slots * toks * width,
            nbytes=6 * toks * width,
        )(small, cotangent)
        sib = swap(give, "expert", experts, 1)
    with jax.named_scope("dispatch"):
        packs = call(
            functools.partial(pack_body, chips),
            (shape((2, cap, width + LANES), bf16),) * (chips - 1),
            (V, V),
            nbytes=4 * slots * width,
        )(keep, sib)
        far = [swap(x, "expert", experts, 2 * hop) for hop, x in enumerate(packs, 1)]
    with jax.named_scope("arrive"):
        rows, masked, parts = [], [], []
        for near in (True, False):
            blocks = [keep, sib] + far[: chips // 2 - 1] if near else far[chips // 2 - 1 :]
            got = call(
                functools.partial(arrive_body, groups, near),
                (shape((half, width + LANES), bf16), shape((half, loops * rank), bf16))
                + (shape((half, part + rank + LANES), bf16),) * groups,
                (V,) * (1 + len(blocks)) + (A,) * near,
                flops=2 * half * width * loops * rank,
                nbytes=4 * half * width,
            )(adapter_out, *blocks, *([pair] if near else []))
            rows.append(got[0])
            masked.append(got[1])
            parts.append(
                [got[2]] + [swap(got[2 + hop], "dp", groups, hop) for hop in range(1, groups)]
            )
        hids, hop = pair, groups
        while hop < groups:
            hids = jnp.concatenate([hids, swap(hids, "dp", groups, hop)])
            hop *= 2
    with jax.named_scope("adapters"):
        work = 2 * groups * half * loops * rank * (part + hid_width + wide)
        sums = (shape((loops * rank, part), f32), shape((loops * rank, wide), f32))
        out, inn, ordered = call(
            functools.partial(adapter_first_body, loops, chips, cap, cols),
            sums + (shape((groups * slots, hid_width), bf16),),
            (V,) * (2 + groups),
            flops=work,
            nbytes=2 * groups * half * part,
        )(flat_in, hids, *parts[0])
    with jax.named_scope("inner"):
        grad, mix = call(
            functools.partial(inner_body, chips, cap),
            (shape((slots, hid_width), bf16), shape((slots, LANES), f32)),
            (V,) * 7,
            flops=2 * slots * width * hid_width,
            nbytes=2 * width * hid_width,
        )(*rows, down_matrix[0], *masked, flat_in, ordered)
    with jax.named_scope("adapters"):
        block = (chips, loops * share, part + wide)
        keep3, give3 = call(
            functools.partial(adapter_last_body, loops, chips, cap, cols),
            (shape(block, f32), shape(block, bf16)),
            (V,) * (5 + groups),
            scratch=[pltpu.VMEM(s.shape, f32) for s in sums],
            flops=work,
            nbytes=2 * groups * half * part,
        )(flat_in, out, inn, mix, ordered, *parts[1])
        got3 = swap(give3, "expert", experts, 1)
        ready = call(
            functools.partial(pair_body, chips),
            (shape(block[1:], bf16),) * chips,
            (V, V),
            nbytes=1e6,
        )(keep3, got3)
        blocks = list(ready)
        for hop in far_first(chips)[1:]:
            blocks[hop] = swap(ready[hop], "expert", experts, 2 * hop)
    with jax.named_scope("product"):
        product = call(
            functools.partial(product_body, groups),
            shape((1, part, hid_width), f32),
            (V,) * (2 * groups + 1),
            limit=40,
            flops=2 * groups * slots * part * hid_width,
            nbytes=4 * groups * slots * part,
        )(*parts[0], *parts[1], ordered)
    with jax.named_scope("final"):
        out_grad, in_grad, combine = call(
            functools.partial(final_body, chips, cap, cols),
            (
                shape((loops, share, part), f32),
                shape((loops, share, cols), f32),
                shape((ways, toks), f32),
            ),
            (V,) * (2 + chips),
            nbytes=1e6,
        )(small, picks, *(blocks[hop] for hop in far_first(chips)))
    return (
        grad.reshape(hidden.shape),
        product,
        combine.T,
        in_grad,
        jnp.swapaxes(out_grad, 1, 2),
    )


def solution(mesh):
    return jax.shard_map(
        on_device,
        mesh=mesh,
        in_specs=(
            P(("dp", "expert"), None),
            P("dp", "expert", None, None),
            P("expert", None, None),
            P(),
            P(),
            P(("dp", "expert"), None),
            P(("dp", "expert"), None),
            P(("dp", "expert")),
        ),
        out_specs=(
            P("dp", "expert", None, None),
            P("expert", "dp", None),
            P(("dp", "expert"), None),
            P(None, "expert", "dp"),
            P(None, "dp", "expert"),
        ),
        check_vma=False,
    )
```

```python
import functools

import jax
import jax.numpy as jnp
from jax import lax
from jax.experimental import pallas as pl
from jax.experimental.pallas import tpu as pltpu
from jax.sharding import PartitionSpec as P

bf16 = jnp.bfloat16
f32 = jnp.float32
LANES = 128
MIB = 1 << 20
V, A = pltpu.VMEM, pl.ANY


def dot(a, b, dims):
    return lax.dot_general(a, b, (dims, ((), ())), preferred_element_type=f32)


def nn(a, b):
    return dot(a, b, ((1,), (0,)))


def nt(a, b):
    return dot(a, b, ((1,), (1,)))


def tn(a, b):
    return dot(a, b, ((0,), (0,)))


def swap(x, axis, size, mask):
    return lax.ppermute(x, axis, [(i, i ^ mask) for i in range(size)])


def shape(dims, kind):
    return jax.ShapeDtypeStruct(dims, kind)


def here():
    return lax.axis_index("expert"), lax.axis_index("dp")


def call(body, out_shape, ins, scratch=(), limit=24, flops=0, nbytes=0):
    return pl.pallas_call(
        body,
        out_shape=out_shape,
        in_specs=[pl.BlockSpec(memory_space=s) for s in ins],
        out_specs=jax.tree.map(lambda _: pl.BlockSpec(memory_space=V), out_shape),
        scratch_shapes=list(scratch),
        cost_estimate=pl.CostEstimate(
            flops=int(flops), bytes_accessed=int(nbytes), transcendentals=0
        ),
        compiler_params=pltpu.CompilerParams(vmem_limit_bytes=limit * MIB),
    )


def owner_column(place, chips, experts):
    j = lax.broadcasted_iota(jnp.int32, (experts, 1), 0)
    half, hop = j // chips, j % chips
    return ((place[0] // 2) ^ hop) * 2 + ((place[0] % 2) ^ half)


def decode(small, experts, loops):
    loop = jnp.zeros_like(small)
    for l in range(1, loops):
        loop = loop + jnp.where(small >= l * (experts + 1.0), 1.0, 0.0)
    rest = small - loop * (experts + 1.0)
    route = jnp.floor(rest)
    return route, rest - route, loop[:1]


def route_body(chips, cap, loops, small, cot, keep, give, picks, mixed):
    experts = 2 * chips
    ways = small.shape[0]
    toks, width = cot.shape
    owner = owner_column(here(), chips, experts).astype(f32)
    route, chance, loop = decode(small[...], experts, loops)
    named = jnp.zeros((experts, toks), f32)
    weight = jnp.zeros((experts, toks), f32)
    for k in range(ways):
        hit = route[k : k + 1, :] == owner
        named = named + jnp.where(hit, 1.0, 0.0)
        weight = weight + jnp.where(hit, chance[k : k + 1, :], 0.0)
    earlier = lax.broadcasted_iota(jnp.int32, (toks, toks), 0) < lax.broadcasted_iota(
        jnp.int32, (toks, toks), 1
    )
    before = nn(named.astype(bf16), jnp.where(earlier, 1.0, 0.0).astype(bf16))
    spot = jnp.where(named > 0.0, before, -1.0)
    slot = lax.broadcasted_iota(jnp.int32, (cap, toks), 0).astype(f32)
    for j in range(experts):
        hit = spot[j : j + 1, :] == slot
        rows = slice(j * cap, (j + 1) * cap)
        picks[rows, :] = jnp.where(hit, 1.0, 0.0).astype(bf16)
        mixed[rows, :] = jnp.where(hit, weight[j : j + 1, :], 0.0).astype(bf16)
    loop_rows = lax.broadcasted_iota(jnp.int32, (LANES, toks), 0).astype(f32)
    loop_rows = jnp.where(loop_rows == loop, 1.0, 0.0).astype(bf16)
    mix = nt(mixed[...], loop_rows).astype(bf16)
    half = chips * cap
    keep[:, :, width:] = mix[:half].reshape(chips, cap, LANES)
    give[:, :, width:] = mix[half:].reshape(chips, cap, LANES)
    step = 1024 if width % 1024 == 0 else width
    for n in range(0, width, step):
        at = slice(n, n + step)
        got = nn(picks[...], cot[:, at]).astype(bf16)
        keep[:, :, at] = got[:half].reshape(chips, cap, step)
        give[:, :, at] = got[half:].reshape(chips, cap, step)


def sources(place, chips):
    z, c = place[0] // 2, place[0] % 2
    return [(z ^ hop) * 2 + (c ^ half) for hop in range(chips) for half in range(2)]


def pack_body(hops, keep, sib, *refs):
    for hop, out in zip(hops, refs[-len(hops) :]):
        out[0] = keep[hop]
        out[1] = sib[hop]


def arrive_body(groups, chips, cap, own, extra, adapter_out, *refs):
    loops, width, rank = adapter_out.shape
    part = width // groups
    side = part + rank + LANES
    parts = refs[-groups:]
    blocks, (rows, masked) = refs[: -2 - groups - extra], refs[-2 - groups : -groups]
    if own:
        hidden, blocks = blocks[0], blocks[1:]
        hid_width = hidden.shape[1]
        for n, source in enumerate(sources(here(), chips)):
            block = hidden[pl.ds(pl.multiple_of(source * cap, cap), cap), :]
            start, at = side + (n // 2) * hid_width, (n % 2) * cap
            for target in parts:
                target[at : at + cap, start : start + hid_width] = block
    at = 0
    for block in blocks:
        halves = (block[0],) if own else (block[0], block[1])
        for piece in halves:
            rows[at : at + piece.shape[0], :] = piece
            at += piece.shape[0]
    mix_block = rows[:, width:]
    mix = mix_block.astype(f32)
    weight = jnp.sum(mix, axis=1, keepdims=True)
    for hop in range(groups):
        start = pl.multiple_of((here()[1] ^ hop) * part, part)
        parts[hop][:, :part] = (weight * rows[:, pl.ds(start, part)].astype(f32)).astype(bf16)
    masks = [mix[:, l : l + 1] > 0.0 for l in range(loops)]
    proj = jnp.zeros((rows.shape[0], rank), f32)
    for l in range(loops):
        proj = proj + jnp.where(masks[l], nn(rows[:, :width], adapter_out[l]), 0.0)
    proj = proj.astype(bf16).astype(f32)
    for l in range(loops):
        masked[:, l * rank : (l + 1) * rank] = jnp.where(masks[l], proj, 0.0).astype(bf16)
    weighted = (weight * proj).astype(bf16)
    for hop in range(groups):
        parts[hop][:, part : part + rank] = weighted
        parts[hop][:, part + rank : side] = mix_block


def inner_body(chips, cap, chunks, down, adapter_in, hidden, *refs):
    grad_out, mix_out = refs[-2:]
    width, hid_width = down.shape
    step = 256 if hid_width % 256 == 0 else hid_width
    rows = jnp.concatenate([r[...] for r in refs[:chunks]], axis=0)
    masked = jnp.concatenate([r[...] for r in refs[chunks : 2 * chunks]], axis=0)
    weight = jnp.sum(rows[:, width:].astype(f32), axis=1, keepdims=True)
    sums = jnp.zeros((mix_out.shape[0], 1), f32)
    order = sources(here(), chips)
    for at in range(0, hid_width, step):
        cols = slice(at, at + step)
        grad = nn(masked, adapter_in[:, cols]) + nn(rows[:, :width], down[:, cols])
        spots = [pl.ds(pl.multiple_of(source * cap, cap), cap) for source in order]
        hid = jnp.concatenate([hidden[spot, cols] for spot in spots], axis=0)
        sums = sums + jnp.sum(hid.astype(f32) * grad, axis=1, keepdims=True)
        scaled = (weight * grad).astype(bf16)
        for n, spot in enumerate(spots):
            grad_out[spot, cols] = scaled[n * cap : (n + 1) * cap]
    mix_out[...] = jnp.broadcast_to(sums, mix_out.shape)


def hidden_rows(holder, hid_width, chips, start, stop):
    size = holder.shape[0]
    side = holder.shape[1] - chips * hid_width
    blocks = [side + n * hid_width for n in range(start // size, stop // size)]
    return [holder[:, at : at + hid_width] for at in blocks]


def adapter_sums(loops, chips, cols, part, start, adapter_in, rows, holders):
    rank = adapter_in.shape[0] // loops
    hid_width = adapter_in.shape[1]
    stop = start + rows[0].shape[0]
    side = part + rank + LANES
    wide = wide_of(cols)
    row = lax.broadcasted_iota(jnp.int32, (hid_width, wide), 0)
    lane = lax.broadcasted_iota(jnp.int32, (hid_width, wide), 1)
    pick = (row == lane + here()[1] * cols) & (lane < cols)
    pick = jnp.where(pick, 1.0, 0.0).astype(bf16)
    hid = [x for h in holders for x in hidden_rows(h, hid_width, chips, start, stop)]
    hid = jnp.concatenate(hid, axis=0)
    tail = jnp.concatenate([r[:, part:side] for r in rows], axis=0).astype(f32)
    body = jnp.concatenate([r[:, :part] for r in rows], axis=0)
    down = nt(hid, adapter_in[...])
    picked = nn(hid, pick).astype(bf16)
    masks = [tail[:, rank + l : rank + l + 1] > 0.0 for l in range(loops)]
    left = [jnp.where(masks[l], down[:, l * rank : (l + 1) * rank], 0.0) for l in range(loops)]
    out = tn(jnp.concatenate(left, axis=1).astype(bf16), body)
    left = [jnp.where(masks[l], tail[:, :rank], 0.0) for l in range(loops)]
    return out, tn(jnp.concatenate(left, axis=1).astype(bf16), picked)


def wide_of(cols):
    return -(-(cols + 4) // LANES) * LANES


def adapter_first_body(loops, chips, cols, groups, adapter_in, _, *refs):
    rows, (out, inn) = refs[:-2], refs[-2:]
    start = 0
    for at in range(0, len(rows), groups):
        chunk = rows[at : at + groups]
        terms = adapter_sums(
            loops, chips, cols, out.shape[1], start, adapter_in, chunk, rows[:groups]
        )
        for target, term in zip((out, inn), terms):
            target[...] = target[...] + term if start else term
        start += chunk[0].shape[0]


def adapter_last_body(loops, chips, cap, cols, groups, adapter_in, out, inn, mix, *refs):
    holders, rows, (keep, give, sums, narrow) = refs[:groups], refs[groups:-4], refs[-4:]
    rank = adapter_in.shape[0] // loops
    part = out.shape[1]
    share = rank // (2 * chips)
    start = mix.shape[0] - rows[0].shape[0]
    more = adapter_sums(loops, chips, cols, part, start, adapter_in, rows, holders)
    sums[...] = out[...] + more[0]
    narrow[...] = inn[...] + more[1]
    owners = sources(here(), chips)
    lane = lax.broadcasted_iota(jnp.int32, (cap, narrow.shape[1]), 1)
    for n, owner in enumerate(owners):
        hop, target = n // 2, (keep, give)[n % 2]
        for l in range(loops):
            src = pl.ds(pl.multiple_of(l * rank + owner * share, share), share)
            dst = slice(l * share, (l + 1) * share)
            target[hop, dst, :part] = sums[src, :].astype(target.dtype)
            target[hop, dst, part:] = narrow[src, :].astype(target.dtype)
        value = mix[n * cap : (n + 1) * cap, :1]
        high = value.astype(bf16).astype(f32)
        tail = target[hop, :cap, part:].astype(f32)
        tail = jnp.where(lane == cols + 2 * (n % 2), high, tail)
        tail = jnp.where(lane == cols + 2 * (n % 2) + 1, value - high, tail)
        target[hop, :cap, part:] = tail.astype(target.dtype)


def pair_body(chips, keep, got, *outs):
    for hop in range(chips):
        outs[hop][...] = (keep[hop] + got[hop].astype(f32)).astype(bf16)


def far_first(chips):
    return [0] + list(range(chips // 2, chips)) + list(range(1, chips // 2))


def final_body(chips, cap, cols, small, picks, *refs):
    order = far_first(chips)
    blocks = [refs[order.index(hop)] for hop in range(chips)]
    out_grad, in_grad, combine = refs[chips:]
    loops, share, part = out_grad.shape
    total = blocks[0][...].astype(f32)
    for hop in range(1, chips):
        total = total + blocks[hop][...].astype(f32)
    for l in range(loops):
        rows = slice(l * share, (l + 1) * share)
        out_grad[l] = total[rows, :part]
        in_grad[l] = total[rows, part : part + cols]
    experts = 2 * chips
    owner = owner_column(here(), chips, experts).astype(f32)
    routes = decode(small[...], experts, loops)[0]
    sums = jnp.zeros(combine.shape, f32)
    for j in range(experts):
        half, hop = j // chips, j % chips
        words = blocks[hop][:cap, part:].astype(f32)
        at = cols + 2 * half
        value = words[:, at : at + 1] + words[:, at + 1 : at + 2]
        pick = picks[j * cap : (j + 1) * cap, :].astype(f32)
        by_token = jnp.sum(pick * value, axis=0, keepdims=True)
        sums = sums + jnp.where(routes == owner[j : j + 1, :], by_token, 0.0)
    combine[...] = sums


def product_body(groups, chips, *refs):
    rows, out = refs[:-1], refs[-1]
    _, part, hid_width = out.shape
    slots = chips * rows[0].shape[0]
    rights = [x for h in rows[:groups] for x in hidden_rows(h, hid_width, chips, 0, slots)]
    rights = jnp.concatenate(rights, axis=0)
    step = 256 if part % 256 == 0 else LANES
    for at in range(0, part, step):
        left = [p[:, at : at + step] for g in range(groups) for p in rows[g::groups]]
        out[0, at : at + step, :] = tn(jnp.concatenate(left, axis=0), rights)


def on_device(cotangent, hidden, down_matrix, adapter_in, adapter_out, probs, routes, token_loop):
    experts = lax.axis_size("expert")
    groups = lax.axis_size("dp")
    chips = experts // 2
    toks, width = cotangent.shape
    loops, rank, hid_width = adapter_in.shape
    ways = routes.shape[1]
    slots = hidden.shape[2]
    cap = slots // experts
    part = width // groups
    cols = hid_width // groups
    wide = wide_of(cols)
    share = rank // experts
    bounds = [0, 1, max(2, 3 * chips // 4), chips]
    chunks = [range(a, b) for a, b in zip(bounds[:-1], bounds[1:])]
    flat_in = adapter_in.reshape(loops * rank, hid_width)
    small = token_loop.reshape(1, toks) * (experts + 1) + jnp.minimum(routes.T, experts)
    small = small.astype(f32) + probs.T.astype(f32)

    turns = range(groups - 1, 0, -1)
    natural = hidden.reshape(slots, hid_width)

    with jax.named_scope("route"):
        packed = shape((chips, cap, width + LANES), bf16)
        keep, give, picks = call(
            functools.partial(route_body, chips, cap, loops),
            (packed, packed, shape((slots, toks), bf16)),
            (V, V),
            scratch=(pltpu.VMEM((slots, toks), bf16),),
            flops=2 * slots * toks * width,
            nbytes=6 * toks * width,
        )(small, cotangent)
        sib = swap(give, "expert", experts, 1)
    with jax.named_scope("dispatch"):
        far = []
        for hops in (range(1, bounds[-2]), chunks[-1]):
            packs = call(
                functools.partial(pack_body, hops),
                (shape((2, cap, width + LANES), bf16),) * len(hops),
                (V, V) + (A,) * len(far[-1:]),
                nbytes=4 * slots * width,
            )(keep, sib, *far[-1:])
            far += [swap(x, "expert", experts, 2 * hop) for hop, x in zip(hops, packs)]
    with jax.named_scope("arrive"):
        rows, masked, parts = [], [], []
        for hops in chunks:
            own, half = hops[0] == 0, 2 * len(hops) * cap
            blocks = [natural, keep, sib] if own else far[hops[0] - 1 : hops[-1]]
            before = parts[0][1:] if len(parts) == 1 else []
            sent = part + rank + LANES + chips * hid_width * own
            got = call(
                functools.partial(arrive_body, groups, chips, cap, own, len(before)),
                (shape((half, width + LANES), bf16), shape((half, loops * rank), bf16))
                + (shape((half, sent), bf16),) * groups,
                (V,) * (1 + len(blocks)) + (A,) * len(before),
                flops=2 * half * width * loops * rank,
                nbytes=4 * half * width,
            )(adapter_out, *blocks, *before)
            rows.append(got[0])
            masked.append(got[1])
            parts.append([got[2]] + [swap(got[2 + hop], "dp", groups, hop) for hop in turns])
    with jax.named_scope("inner"):
        grad, mix = call(
            functools.partial(inner_body, chips, cap, len(chunks)),
            (shape((slots, hid_width), bf16), shape((slots, LANES), f32)),
            (V,) * (3 + 2 * len(chunks)),
            flops=2 * slots * width * hid_width,
            nbytes=2 * width * hid_width,
        )(down_matrix[0], flat_in, natural, *rows, *masked)
    with jax.named_scope("adapters"):
        work = groups * slots * loops * rank * (part + hid_width + wide)
        sums = (shape((loops * rank, part), f32), shape((loops * rank, wide), f32))
        out, inn = call(
            functools.partial(adapter_first_body, loops, chips, cols, groups),
            sums,
            (V, A) + (V,) * (groups * (len(chunks) - 1)),
            flops=work,
            nbytes=groups * slots * part,
        )(flat_in, mix, *(p for chunk in parts[:-1] for p in chunk))
        block = (chips, loops * share, part + wide)
        keep3, give3 = call(
            functools.partial(adapter_last_body, loops, chips, cap, cols, groups),
            (shape(block, f32), shape(block, bf16)),
            (V,) * (4 + 2 * groups),
            scratch=[pltpu.VMEM(s.shape, f32) for s in sums],
            flops=work,
            nbytes=groups * slots * part,
        )(flat_in, out, inn, mix, *parts[0], *parts[-1])
        got3 = swap(give3, "expert", experts, 1)
        ready = call(
            functools.partial(pair_body, chips),
            (shape(block[1:], bf16),) * chips,
            (V, V),
            nbytes=1e6,
        )(keep3, got3)
        blocks = list(ready)
        for hop in far_first(chips)[1:]:
            blocks[hop] = swap(ready[hop], "expert", experts, 2 * hop)
    with jax.named_scope("product"):
        product = call(
            functools.partial(product_body, groups, chips),
            shape((1, part, hid_width), f32),
            (V,) * (groups * len(chunks)),
            limit=40,
            flops=2 * groups * slots * part * hid_width,
            nbytes=4 * groups * slots * part,
        )(*(p for chunk in parts for p in chunk))
    with jax.named_scope("final"):
        out_grad, in_grad, combine = call(
            functools.partial(final_body, chips, cap, cols),
            (
                shape((loops, share, part), f32),
                shape((loops, share, cols), f32),
                shape((ways, toks), f32),
            ),
            (V,) * (2 + chips),
            nbytes=1e6,
        )(small, picks, *(blocks[hop] for hop in far_first(chips)))
    return (
        grad.reshape(hidden.shape),
        product,
        combine.T,
        in_grad,
        jnp.swapaxes(out_grad, 1, 2),
    )


def solution(mesh):
    return jax.shard_map(
        on_device,
        mesh=mesh,
        in_specs=(
            P(("dp", "expert"), None),
            P("dp", "expert", None, None),
            P("expert", None, None),
            P(),
            P(),
            P(("dp", "expert"), None),
            P(("dp", "expert"), None),
            P(("dp", "expert")),
        ),
        out_specs=(
            P("dp", "expert", None, None),
            P("expert", "dp", None),
            P(("dp", "expert"), None),
            P(None, "expert", "dp"),
            P(None, "dp", "expert"),
        ),
        check_vma=False,
    )
```

```python
import functools

import jax
import jax.numpy as jnp
from jax import lax
from jax.experimental import pallas as pl
from jax.experimental.pallas import tpu as pltpu
from jax.sharding import PartitionSpec as P

bf16 = jnp.bfloat16
f32 = jnp.float32
LANES = 128
MIB = 1 << 20
V, A = pltpu.VMEM, pl.ANY


def dot(a, b, dims):
    return lax.dot_general(a, b, (dims, ((), ())), preferred_element_type=f32)


def nn(a, b):
    return dot(a, b, ((1,), (0,)))


def nt(a, b):
    return dot(a, b, ((1,), (1,)))


def tn(a, b):
    return dot(a, b, ((0,), (0,)))


def swap(x, axis, size, mask):
    return lax.ppermute(x, axis, [(i, i ^ mask) for i in range(size)])


def shape(dims, kind):
    return jax.ShapeDtypeStruct(dims, kind)


def here():
    return lax.axis_index("expert"), lax.axis_index("dp")


def call(body, out_shape, ins, scratch=(), limit=24, flops=0, nbytes=0):
    return pl.pallas_call(
        body,
        out_shape=out_shape,
        in_specs=[pl.BlockSpec(memory_space=s) for s in ins],
        out_specs=jax.tree.map(lambda _: pl.BlockSpec(memory_space=V), out_shape),
        scratch_shapes=list(scratch),
        cost_estimate=pl.CostEstimate(
            flops=int(flops), bytes_accessed=int(nbytes), transcendentals=0
        ),
        compiler_params=pltpu.CompilerParams(vmem_limit_bytes=limit * MIB),
    )


def owner_column(place, chips, experts):
    j = lax.broadcasted_iota(jnp.int32, (experts, 1), 0)
    half, hop = j // chips, j % chips
    return ((place[0] // 2) ^ hop) * 2 + ((place[0] % 2) ^ half)


def decode(small, experts, loops):
    loop = jnp.zeros_like(small)
    for l in range(1, loops):
        loop = loop + jnp.where(small >= l * (experts + 1.0), 1.0, 0.0)
    rest = small - loop * (experts + 1.0)
    route = jnp.floor(rest)
    return route, rest - route, loop[:1]


def deal_rows(middle, rows, at, keep, lead, give):
    chips = keep.shape[0]
    keep[:, :, at] = rows[:chips]
    lead[0, :, at], lead[1, :, at] = rows[middle], rows[chips + middle]
    give[:middle, :, at] = rows[chips : chips + middle]
    if middle + 1 < chips:
        give[middle:, :, at] = rows[chips + middle + 1 :]


def route_body(chips, cap, loops, small, cot, keep, lead, give, picks, mixed):
    middle = chips // 2
    experts = 2 * chips
    ways = small.shape[0]
    toks, width = cot.shape
    owner = owner_column(here(), chips, experts).astype(f32)
    route, chance, loop = decode(small[...], experts, loops)
    named = jnp.zeros((experts, toks), f32)
    weight = jnp.zeros((experts, toks), f32)
    for k in range(ways):
        hit = route[k : k + 1, :] == owner
        named = named + jnp.where(hit, 1.0, 0.0)
        weight = weight + jnp.where(hit, chance[k : k + 1, :], 0.0)
    earlier = lax.broadcasted_iota(jnp.int32, (toks, toks), 0) < lax.broadcasted_iota(
        jnp.int32, (toks, toks), 1
    )
    before = nn(named.astype(bf16), jnp.where(earlier, 1.0, 0.0).astype(bf16))
    spot = jnp.where(named > 0.0, before, -1.0)
    slot = lax.broadcasted_iota(jnp.int32, (cap, toks), 0).astype(f32)
    for j in range(experts):
        hit = spot[j : j + 1, :] == slot
        rows = slice(j * cap, (j + 1) * cap)
        picks[rows, :] = jnp.where(hit, 1.0, 0.0).astype(bf16)
        mixed[rows, :] = jnp.where(hit, weight[j : j + 1, :], 0.0).astype(bf16)
    loop_rows = lax.broadcasted_iota(jnp.int32, (LANES, toks), 0).astype(f32)
    loop_rows = jnp.where(loop_rows == loop, 1.0, 0.0).astype(bf16)
    mix = nt(mixed[...], loop_rows).astype(bf16)
    deal_rows(middle, mix.reshape(2 * chips, cap, LANES), slice(width, width + LANES), keep, lead, give)
    step = 1024 if width % 1024 == 0 else width
    for n in range(0, width, step):
        at = slice(n, n + step)
        got = nn(picks[...], cot[:, at]).astype(bf16)
        deal_rows(middle, got.reshape(2 * chips, cap, step), at, keep, lead, give)


def sources(place, chips):
    z, c = place[0] // 2, place[0] % 2
    return [(z ^ hop) * 2 + (c ^ half) for hop in range(chips) for half in range(2)]


def pack_body(hops, chips, keep, sib, *refs):
    for hop, out in zip(hops, refs[-len(hops) :]):
        out[0, :, : keep.shape[2]] = keep[hop]
        out[1, :, : keep.shape[2]] = sib[hop - (hop > chips // 2)]


def arrive_body(groups, chips, cap, own, extra, adapter_out, *refs):
    loops, width, rank = adapter_out.shape
    part = width // groups
    side = part + rank + LANES
    parts = refs[-groups:]
    blocks, (rows, masked) = refs[: -2 - groups - extra], refs[-2 - groups : -groups]
    if own:
        hidden, blocks = blocks[0], blocks[1:]
        hid_width = hidden.shape[1]
        for n, source in enumerate(sources(here(), chips)):
            block = hidden[pl.ds(pl.multiple_of(source * cap, cap), cap), :]
            start, at = side + (n // 2) * hid_width, (n % 2) * cap
            for target in parts:
                target[at : at + cap, start : start + hid_width] = block
    at = 0
    for block in blocks:
        if len(block.shape) == 2:
            halves = (block[...],)
        else:
            halves = (block[0],) if own else (block[0], block[1])
        for piece in halves:
            rows[at : at + piece.shape[0], :] = piece[:, : rows.shape[1]]
            at += piece.shape[0]
    mix_block = rows[:, width:]
    mix = mix_block.astype(f32)
    weight = jnp.sum(mix, axis=1, keepdims=True)
    for hop in range(groups):
        start = pl.multiple_of((here()[1] ^ hop) * part, part)
        parts[hop][:, :part] = (weight * rows[:, pl.ds(start, part)].astype(f32)).astype(bf16)
    masks = [mix[:, l : l + 1] > 0.0 for l in range(loops)]
    proj = jnp.zeros((rows.shape[0], rank), f32)
    for l in range(loops):
        proj = proj + jnp.where(masks[l], nn(rows[:, :width], adapter_out[l]), 0.0)
    proj = proj.astype(bf16).astype(f32)
    for l in range(loops):
        masked[:, l * rank : (l + 1) * rank] = jnp.where(masks[l], proj, 0.0).astype(bf16)
    weighted = (weight * proj).astype(bf16)
    for hop in range(groups):
        parts[hop][:, part : part + rank] = weighted
        parts[hop][:, part + rank : side] = mix_block


def inner_body(chips, cap, chunks, down, adapter_in, hidden, *refs):
    grad_out, mix_out = refs[-2:]
    width, hid_width = down.shape
    step = 256 if hid_width % 256 == 0 else hid_width
    rows = jnp.concatenate([r[...] for r in refs[:chunks]], axis=0)
    masked = jnp.concatenate([r[...] for r in refs[chunks : 2 * chunks]], axis=0)
    weight = jnp.sum(rows[:, width:].astype(f32), axis=1, keepdims=True)
    sums = jnp.zeros((mix_out.shape[0], 1), f32)
    order = sources(here(), chips)
    for at in range(0, hid_width, step):
        cols = slice(at, at + step)
        grad = nn(masked, adapter_in[:, cols]) + nn(rows[:, :width], down[:, cols])
        spots = [pl.ds(pl.multiple_of(source * cap, cap), cap) for source in order]
        hid = jnp.concatenate([hidden[spot, cols] for spot in spots], axis=0)
        sums = sums + jnp.sum(hid.astype(f32) * grad, axis=1, keepdims=True)
        scaled = (weight * grad).astype(bf16)
        for n, spot in enumerate(spots):
            grad_out[spot, cols] = scaled[n * cap : (n + 1) * cap]
    mix_out[...] = jnp.broadcast_to(sums, mix_out.shape)


def hidden_rows(holder, hid_width, chips, start, stop):
    size = holder.shape[0]
    side = holder.shape[1] - chips * hid_width
    blocks = [side + n * hid_width for n in range(start // size, stop // size)]
    return [holder[:, at : at + hid_width] for at in blocks]


def adapter_sums(loops, chips, cols, part, start, adapter_in, rows, holders):
    rank = adapter_in.shape[0] // loops
    hid_width = adapter_in.shape[1]
    stop = start + rows[0].shape[0]
    side = part + rank + LANES
    wide = wide_of(cols)
    row = lax.broadcasted_iota(jnp.int32, (hid_width, wide), 0)
    lane = lax.broadcasted_iota(jnp.int32, (hid_width, wide), 1)
    pick = (row == lane + here()[1] * cols) & (lane < cols)
    pick = jnp.where(pick, 1.0, 0.0).astype(bf16)
    hid = [x for h in holders for x in hidden_rows(h, hid_width, chips, start, stop)]
    hid = jnp.concatenate(hid, axis=0)
    tail = jnp.concatenate([r[:, part:side] for r in rows], axis=0).astype(f32)
    body = jnp.concatenate([r[:, :part] for r in rows], axis=0)
    down = nt(hid, adapter_in[...])
    picked = nn(hid, pick).astype(bf16)
    masks = [tail[:, rank + l : rank + l + 1] > 0.0 for l in range(loops)]
    left = [jnp.where(masks[l], down[:, l * rank : (l + 1) * rank], 0.0) for l in range(loops)]
    out = tn(jnp.concatenate(left, axis=1).astype(bf16), body)
    left = [jnp.where(masks[l], tail[:, :rank], 0.0) for l in range(loops)]
    return out, tn(jnp.concatenate(left, axis=1).astype(bf16), picked)


def wide_of(cols):
    return -(-(cols + 4) // LANES) * LANES


def adapter_first_body(loops, chips, cols, groups, adapter_in, _, *refs):
    rows, (out, inn) = refs[:-2], refs[-2:]
    start = 0
    for at in range(0, len(rows), groups):
        chunk = rows[at : at + groups]
        terms = adapter_sums(
            loops, chips, cols, out.shape[1], start, adapter_in, chunk, rows[:groups]
        )
        for target, term in zip((out, inn), terms):
            target[...] = target[...] + term if start else term
        start += chunk[0].shape[0]


def adapter_last_body(loops, chips, cap, cols, groups, adapter_in, out, inn, mix, *refs):
    holders, rows, (keep, give, sums, narrow) = refs[:groups], refs[groups:-4], refs[-4:]
    rank = adapter_in.shape[0] // loops
    part = out.shape[1]
    share = rank // (2 * chips)
    start = mix.shape[0] - rows[0].shape[0]
    more = adapter_sums(loops, chips, cols, part, start, adapter_in, rows, holders)
    sums[...] = out[...] + more[0]
    narrow[...] = inn[...] + more[1]
    owners = sources(here(), chips)
    lane = lax.broadcasted_iota(jnp.int32, (cap, narrow.shape[1]), 1)
    for n, owner in enumerate(owners):
        hop, target = n // 2, (keep, give)[n % 2]
        for l in range(loops):
            src = pl.ds(pl.multiple_of(l * rank + owner * share, share), share)
            dst = slice(l * share, (l + 1) * share)
            target[hop, dst, :part] = sums[src, :].astype(target.dtype)
            target[hop, dst, part:] = narrow[src, :].astype(target.dtype)
        value = mix[n * cap : (n + 1) * cap, :1]
        high = value.astype(bf16).astype(f32)
        tail = target[hop, :cap, part:].astype(f32)
        tail = jnp.where(lane == cols + 2 * (n % 2), high, tail)
        tail = jnp.where(lane == cols + 2 * (n % 2) + 1, value - high, tail)
        target[hop, :cap, part:] = tail.astype(target.dtype)


def pair_body(chips, keep, got, *outs):
    for hop in range(chips):
        outs[hop][...] = (keep[hop] + got[hop].astype(f32)).astype(bf16)


def far_first(chips):
    return [0] + list(range(chips // 2, chips)) + list(range(1, chips // 2))


def final_body(chips, cap, cols, small, picks, *refs):
    order = far_first(chips)
    blocks = [refs[order.index(hop)] for hop in range(chips)]
    out_grad, in_grad, combine = refs[chips:]
    loops, share, part = out_grad.shape
    total = blocks[0][...].astype(f32)
    for hop in range(1, chips):
        total = total + blocks[hop][...].astype(f32)
    for l in range(loops):
        rows = slice(l * share, (l + 1) * share)
        out_grad[l] = total[rows, :part]
        in_grad[l] = total[rows, part : part + cols]
    experts = 2 * chips
    owner = owner_column(here(), chips, experts).astype(f32)
    routes = decode(small[...], experts, loops)[0]
    sums = jnp.zeros(combine.shape, f32)
    for j in range(experts):
        half, hop = j // chips, j % chips
        words = blocks[hop][:cap, part:].astype(f32)
        at = cols + 2 * half
        value = words[:, at : at + 1] + words[:, at + 1 : at + 2]
        pick = picks[j * cap : (j + 1) * cap, :].astype(f32)
        by_token = jnp.sum(pick * value, axis=0, keepdims=True)
        sums = sums + jnp.where(routes == owner[j : j + 1, :], by_token, 0.0)
    combine[...] = sums


def product_body(groups, chips, *refs):
    rows, out = refs[:-1], refs[-1]
    _, part, hid_width = out.shape
    slots = chips * rows[0].shape[0]
    rights = [x for h in rows[:groups] for x in hidden_rows(h, hid_width, chips, 0, slots)]
    rights = jnp.concatenate(rights, axis=0)
    step = 256 if part % 256 == 0 else LANES
    for at in range(0, part, step):
        left = [p[:, at : at + step] for g in range(groups) for p in rows[g::groups]]
        out[0, at : at + step, :] = tn(jnp.concatenate(left, axis=0), rights)


def on_device(cotangent, hidden, down_matrix, adapter_in, adapter_out, probs, routes, token_loop):
    experts = lax.axis_size("expert")
    groups = lax.axis_size("dp")
    chips = experts // 2
    toks, width = cotangent.shape
    loops, rank, hid_width = adapter_in.shape
    ways = routes.shape[1]
    slots = hidden.shape[2]
    cap = slots // experts
    part = width // groups
    cols = hid_width // groups
    wide = wide_of(cols)
    share = rank // experts
    bounds = [0, 1, max(2, 3 * chips // 4), chips]
    chunks = [range(a, b) for a, b in zip(bounds[:-1], bounds[1:])]
    flat_in = adapter_in.reshape(loops * rank, hid_width)
    small = token_loop.reshape(1, toks) * (experts + 1) + jnp.minimum(routes.T, experts)
    small = small.astype(f32) + probs.T.astype(f32)

    turns = range(groups - 1, 0, -1)
    natural = hidden.reshape(slots, hid_width)

    with jax.named_scope("route"):
        packed = shape((chips, cap, width + LANES), bf16)
        keep, lead, give, picks = call(
            functools.partial(route_body, chips, cap, loops),
            (
                packed,
                shape((2,) + packed.shape[1:], bf16),
                shape((chips - 1,) + packed.shape[1:], bf16),
                shape((slots, toks), bf16),
            ),
            (V, V),
            scratch=(pltpu.VMEM((slots, toks), bf16),),
            flops=2 * slots * toks * width,
            nbytes=6 * toks * width,
        )(small, cotangent)
        sib = swap(give, "expert", experts, 1)
    with jax.named_scope("dispatch"):
        middle = chips // 2
        lead = swap(lead, "expert", experts, 2 * middle)
        far = {middle: [lead[0], swap(lead[1], "expert", experts, 1)]}
        others = [hop for hop in range(1, bounds[-2]) if hop != middle]
        for hops, after in ((others, []), (chunks[-1], 1)):
            packs = call(
                functools.partial(pack_body, hops, chips),
                tuple(shape((2, cap, width + (3 if hop == 1 else 1) * LANES), bf16) for hop in hops),
                (V, V) + (A,) * bool(after),
                nbytes=4 * slots * width,
            )(keep, sib, *(far[1] if after else []))
            far.update((hop, [swap(x, "expert", experts, 2 * hop)]) for hop, x in zip(hops, packs))
    with jax.named_scope("arrive"):
        rows, masked, parts = [], [], []
        for hops in chunks:
            own, half = hops[0] == 0, 2 * len(hops) * cap
            blocks = [natural, keep, sib] if own else [x for hop in hops for x in far[hop]]
            before = parts[0][1:] if len(parts) == 1 else []
            sent = part + rank + LANES + chips * hid_width * own
            got = call(
                functools.partial(arrive_body, groups, chips, cap, own, len(before)),
                (shape((half, width + LANES), bf16), shape((half, loops * rank), bf16))
                + (shape((half, sent), bf16),) * groups,
                (V,) * (1 + len(blocks)) + (A,) * len(before),
                flops=2 * half * width * loops * rank,
                nbytes=4 * half * width,
            )(adapter_out, *blocks, *before)
            rows.append(got[0])
            masked.append(got[1])
            parts.append([got[2]] + [swap(got[2 + hop], "dp", groups, hop) for hop in turns])
    with jax.named_scope("inner"):
        grad, mix = call(
            functools.partial(inner_body, chips, cap, len(chunks)),
            (shape((slots, hid_width), bf16), shape((slots, LANES), f32)),
            (V,) * (3 + 2 * len(chunks)),
            flops=2 * slots * width * hid_width,
            nbytes=2 * width * hid_width,
        )(down_matrix[0], flat_in, natural, *rows, *masked)
    with jax.named_scope("adapters"):
        work = groups * slots * loops * rank * (part + hid_width + wide)
        sums = (shape((loops * rank, part), f32), shape((loops * rank, wide), f32))
        out, inn = call(
            functools.partial(adapter_first_body, loops, chips, cols, groups),
            sums,
            (V, A) + (V,) * (groups * (len(chunks) - 1)),
            flops=work,
            nbytes=groups * slots * part,
        )(flat_in, mix, *(p for chunk in parts[:-1] for p in chunk))
        block = (chips, loops * share, part + wide)
        keep3, give3 = call(
            functools.partial(adapter_last_body, loops, chips, cap, cols, groups),
            (shape(block, f32), shape(block, bf16)),
            (V,) * (4 + 2 * groups),
            scratch=[pltpu.VMEM(s.shape, f32) for s in sums],
            flops=work,
            nbytes=groups * slots * part,
        )(flat_in, out, inn, mix, *parts[0], *parts[-1])
        got3 = swap(give3, "expert", experts, 1)
        ready = call(
            functools.partial(pair_body, chips),
            (shape(block[1:], bf16),) * chips,
            (V, V),
            nbytes=1e6,
        )(keep3, got3)
        blocks = list(ready)
        for hop in far_first(chips)[1:]:
            blocks[hop] = swap(ready[hop], "expert", experts, 2 * hop)
    with jax.named_scope("product"):
        product = call(
            functools.partial(product_body, groups, chips),
            shape((1, part, hid_width), f32),
            (V,) * (groups * len(chunks)),
            limit=40,
            flops=2 * groups * slots * part * hid_width,
            nbytes=4 * groups * slots * part,
        )(*(p for chunk in parts for p in chunk))
    with jax.named_scope("final"):
        out_grad, in_grad, combine = call(
            functools.partial(final_body, chips, cap, cols),
            (
                shape((loops, share, part), f32),
                shape((loops, share, cols), f32),
                shape((ways, toks), f32),
            ),
            (V,) * (2 + chips),
            nbytes=1e6,
        )(small, picks, *(blocks[hop] for hop in far_first(chips)))
    return (
        grad.reshape(hidden.shape),
        product,
        combine.T,
        in_grad,
        jnp.swapaxes(out_grad, 1, 2),
    )


def solution(mesh):
    return jax.shard_map(
        on_device,
        mesh=mesh,
        in_specs=(
            P(("dp", "expert"), None),
            P("dp", "expert", None, None),
            P("expert", None, None),
            P(),
            P(),
            P(("dp", "expert"), None),
            P(("dp", "expert"), None),
            P(("dp", "expert")),
        ),
        out_specs=(
            P("dp", "expert", None, None),
            P("expert", "dp", None),
            P(("dp", "expert"), None),
            P(None, "expert", "dp"),
            P(None, "dp", "expert"),
        ),
        check_vma=False,
    )
```

```python
import functools

import jax
import jax.numpy as jnp
from jax import lax
from jax.experimental import pallas as pl
from jax.experimental.pallas import tpu as pltpu
from jax.sharding import PartitionSpec as P

bf16 = jnp.bfloat16
f32 = jnp.float32
LANES = 128
MIB = 1 << 20
V, A = pltpu.VMEM, pl.ANY


def dot(a, b, dims):
    return lax.dot_general(a, b, (dims, ((), ())), preferred_element_type=f32)


def nn(a, b):
    return dot(a, b, ((1,), (0,)))


def nt(a, b):
    return dot(a, b, ((1,), (1,)))


def tn(a, b):
    return dot(a, b, ((0,), (0,)))


def swap(x, axis, size, mask):
    return lax.ppermute(x, axis, [(i, i ^ mask) for i in range(size)])


def shape(dims, kind):
    return jax.ShapeDtypeStruct(dims, kind)


def here():
    return lax.axis_index("expert"), lax.axis_index("dp")


def call(body, out_shape, ins, scratch=(), limit=24, flops=0, nbytes=0):
    return pl.pallas_call(
        body,
        out_shape=out_shape,
        in_specs=[pl.BlockSpec(memory_space=s) for s in ins],
        out_specs=jax.tree.map(lambda _: pl.BlockSpec(memory_space=V), out_shape),
        scratch_shapes=list(scratch),
        cost_estimate=pl.CostEstimate(
            flops=int(flops), bytes_accessed=int(nbytes), transcendentals=0
        ),
        compiler_params=pltpu.CompilerParams(vmem_limit_bytes=limit * MIB),
    )


def owner_column(place, chips, experts):
    j = lax.broadcasted_iota(jnp.int32, (experts, 1), 0)
    half, hop = j // chips, j % chips
    return ((place[0] // 2) ^ hop) * 2 + ((place[0] % 2) ^ half)


def decode(small, experts, loops):
    loop = jnp.zeros_like(small)
    for l in range(1, loops):
        loop = loop + jnp.where(small >= l * (experts + 1.0), 1.0, 0.0)
    rest = small - loop * (experts + 1.0)
    route = jnp.floor(rest)
    return route, rest - route, loop[:1]


def deal_rows(middle, rows, at, keep, lead, give):
    chips = keep.shape[0]
    keep[:, :, at] = rows[:chips]
    lead[0, :, at], lead[1, :, at] = rows[middle], rows[chips + middle]
    give[:middle, :, at] = rows[chips : chips + middle]
    if middle + 1 < chips:
        give[middle:, :, at] = rows[chips + middle + 1 :]


def route_body(chips, cap, loops, small, cot, keep, lead, give, picks, mixed):
    middle = chips // 2
    experts = 2 * chips
    ways = small.shape[0]
    toks, width = cot.shape
    owner = owner_column(here(), chips, experts).astype(f32)
    route, chance, loop = decode(small[...], experts, loops)
    named = jnp.zeros((experts, toks), f32)
    weight = jnp.zeros((experts, toks), f32)
    for k in range(ways):
        hit = route[k : k + 1, :] == owner
        named = named + jnp.where(hit, 1.0, 0.0)
        weight = weight + jnp.where(hit, chance[k : k + 1, :], 0.0)
    earlier = lax.broadcasted_iota(jnp.int32, (toks, toks), 0) < lax.broadcasted_iota(
        jnp.int32, (toks, toks), 1
    )
    before = nn(named.astype(bf16), jnp.where(earlier, 1.0, 0.0).astype(bf16))
    spot = jnp.where(named > 0.0, before, -1.0)
    slot = lax.broadcasted_iota(jnp.int32, (cap, toks), 0).astype(f32)
    for j in range(experts):
        hit = spot[j : j + 1, :] == slot
        rows = slice(j * cap, (j + 1) * cap)
        picks[rows, :] = jnp.where(hit, 1.0, 0.0).astype(bf16)
        mixed[rows, :] = jnp.where(hit, weight[j : j + 1, :], 0.0).astype(bf16)
    loop_rows = lax.broadcasted_iota(jnp.int32, (LANES, toks), 0).astype(f32)
    loop_rows = jnp.where(loop_rows == loop, 1.0, 0.0).astype(bf16)
    mix = nt(mixed[...], loop_rows).astype(bf16)
    deal_rows(middle, mix.reshape(2 * chips, cap, LANES), slice(width, width + LANES), keep, lead, give)
    step = 1024 if width % 1024 == 0 else width
    for n in range(0, width, step):
        at = slice(n, n + step)
        got = nn(picks[...], cot[:, at]).astype(bf16)
        deal_rows(middle, got.reshape(2 * chips, cap, step), at, keep, lead, give)


def sources(place, chips):
    z, c = place[0] // 2, place[0] % 2
    return [(z ^ hop) * 2 + (c ^ half) for hop in range(chips) for half in range(2)]


def pack_body(hops, chips, keep, sib, *refs):
    for hop, out in zip(hops, refs[-len(hops) :]):
        out[0, :, : keep.shape[2]] = keep[hop]
        out[1, :, : keep.shape[2]] = sib[hop - (hop > chips // 2)]


def arrive_body(groups, chips, cap, own, extra, adapter_out, *refs):
    loops, width, rank = adapter_out.shape
    part = width // groups
    side = part + rank + LANES
    parts = refs[-groups:]
    blocks, (rows, masked) = refs[: -2 - groups - extra], refs[-2 - groups : -groups]
    if own:
        hidden, blocks = blocks[0], blocks[1:]
        hid_width = hidden.shape[1]
        for n, source in enumerate(sources(here(), chips)):
            block = hidden[pl.ds(pl.multiple_of(source * cap, cap), cap), :]
            start, at = side + (n // 2) * hid_width, (n % 2) * cap
            for target in parts:
                target[at : at + cap, start : start + hid_width] = block
    at = 0
    for block in blocks:
        if len(block.shape) == 2:
            halves = (block[...],)
        else:
            halves = (block[0],) if own else (block[0], block[1])
        for piece in halves:
            rows[at : at + piece.shape[0], :] = piece[:, : rows.shape[1]]
            at += piece.shape[0]
    mix_block = rows[:, width:]
    mix = mix_block.astype(f32)
    weight = jnp.sum(mix, axis=1, keepdims=True)
    for hop in range(groups):
        start = pl.multiple_of((here()[1] ^ hop) * part, part)
        parts[hop][:, :part] = (weight * rows[:, pl.ds(start, part)].astype(f32)).astype(bf16)
    masks = [mix[:, l : l + 1] > 0.0 for l in range(loops)]
    proj = jnp.zeros((rows.shape[0], rank), f32)
    for l in range(loops):
        proj = proj + jnp.where(masks[l], nn(rows[:, :width], adapter_out[l]), 0.0)
    proj = proj.astype(bf16).astype(f32)
    for l in range(loops):
        masked[:, l * rank : (l + 1) * rank] = jnp.where(masks[l], proj, 0.0).astype(bf16)
    weighted = (weight * proj).astype(bf16)
    for hop in range(groups):
        parts[hop][:, part : part + rank] = weighted
        parts[hop][:, part + rank : side] = mix_block


def inner_body(chips, cap, chunks, down, adapter_in, hidden, *refs):
    grad_out, mix_out = refs[-2:]
    width, hid_width = down.shape
    step = 256 if hid_width % 256 == 0 else hid_width
    rows = jnp.concatenate([r[...] for r in refs[:chunks]], axis=0)
    masked = jnp.concatenate([r[...] for r in refs[chunks : 2 * chunks]], axis=0)
    weight = jnp.sum(rows[:, width:].astype(f32), axis=1, keepdims=True)
    sums = jnp.zeros((mix_out.shape[0], 1), f32)
    order = sources(here(), chips)
    for at in range(0, hid_width, step):
        cols = slice(at, at + step)
        grad = nn(masked, adapter_in[:, cols]) + nn(rows[:, :width], down[:, cols])
        spots = [pl.ds(pl.multiple_of(source * cap, cap), cap) for source in order]
        hid = jnp.concatenate([hidden[spot, cols] for spot in spots], axis=0)
        sums = sums + jnp.sum(hid.astype(f32) * grad, axis=1, keepdims=True)
        scaled = (weight * grad).astype(bf16)
        for n, spot in enumerate(spots):
            grad_out[spot, cols] = scaled[n * cap : (n + 1) * cap]
    mix_out[...] = jnp.broadcast_to(sums, mix_out.shape)


def hidden_rows(holder, hid_width, chips, start, stop):
    size = holder.shape[0]
    side = holder.shape[1] - chips * hid_width
    blocks = [side + n * hid_width for n in range(start // size, stop // size)]
    return [holder[:, at : at + hid_width] for at in blocks]


def adapter_sums(loops, chips, cols, part, start, adapter_in, rows, holders):
    rank = adapter_in.shape[0] // loops
    hid_width = adapter_in.shape[1]
    stop = start + rows[0].shape[0]
    side = part + rank + LANES
    wide = wide_of(cols)
    row = lax.broadcasted_iota(jnp.int32, (hid_width, wide), 0)
    lane = lax.broadcasted_iota(jnp.int32, (hid_width, wide), 1)
    pick = (row == lane + here()[1] * cols) & (lane < cols)
    pick = jnp.where(pick, 1.0, 0.0).astype(bf16)
    hid = [x for h in holders for x in hidden_rows(h, hid_width, chips, start, stop)]
    hid = jnp.concatenate(hid, axis=0)
    tail = jnp.concatenate([r[:, part:side] for r in rows], axis=0).astype(f32)
    body = jnp.concatenate([r[:, :part] for r in rows], axis=0)
    down = nt(hid, adapter_in[...])
    picked = nn(hid, pick).astype(bf16)
    masks = [tail[:, rank + l : rank + l + 1] > 0.0 for l in range(loops)]
    left = [jnp.where(masks[l], down[:, l * rank : (l + 1) * rank], 0.0) for l in range(loops)]
    out = tn(jnp.concatenate(left, axis=1).astype(bf16), body)
    left = [jnp.where(masks[l], tail[:, :rank], 0.0) for l in range(loops)]
    return out, tn(jnp.concatenate(left, axis=1).astype(bf16), picked)


def wide_of(cols):
    return -(-(cols + 4) // LANES) * LANES


def adapter_first_body(loops, chips, cols, groups, adapter_in, _, *refs):
    rows, (out, inn) = refs[:-2], refs[-2:]
    start = 0
    for at in range(0, len(rows), groups):
        chunk = rows[at : at + groups]
        terms = adapter_sums(
            loops, chips, cols, out.shape[1], start, adapter_in, chunk, rows[:groups]
        )
        for target, term in zip((out, inn), terms):
            target[...] = target[...] + term if start else term
        start += chunk[0].shape[0]


def adapter_last_body(loops, chips, cap, cols, groups, adapter_in, out, inn, mix, *refs):
    holders, rows, (keep, give, sums, narrow) = refs[:groups], refs[groups:-4], refs[-4:]
    rank = adapter_in.shape[0] // loops
    part = out.shape[1]
    share = rank // (2 * chips)
    start = mix.shape[0] - rows[0].shape[0]
    more = adapter_sums(loops, chips, cols, part, start, adapter_in, rows, holders)
    sums[...] = out[...] + more[0]
    narrow[...] = inn[...] + more[1]
    owners = sources(here(), chips)
    lane = lax.broadcasted_iota(jnp.int32, (cap, narrow.shape[1]), 1)
    for n, owner in enumerate(owners):
        hop, target = n // 2, (keep, give)[n % 2]
        for l in range(loops):
            src = pl.ds(pl.multiple_of(l * rank + owner * share, share), share)
            dst = slice(l * share, (l + 1) * share)
            target[hop, dst, :part] = sums[src, :].astype(target.dtype)
            target[hop, dst, part:] = narrow[src, :].astype(target.dtype)
        value = mix[n * cap : (n + 1) * cap, :1]
        high = value.astype(bf16).astype(f32)
        tail = target[hop, :cap, part:].astype(f32)
        tail = jnp.where(lane == cols + 2 * (n % 2), high, tail)
        tail = jnp.where(lane == cols + 2 * (n % 2) + 1, value - high, tail)
        target[hop, :cap, part:] = tail.astype(target.dtype)


def pair_body(chips, keep, got, *outs):
    for hop in range(chips):
        outs[hop][...] = (keep[hop] + got[hop].astype(f32)).astype(bf16)


def far_first(chips):
    return [0] + list(range(chips // 2, chips)) + list(range(1, chips // 2))


def final_body(chips, cap, cols, small, picks, *refs):
    order = far_first(chips)
    blocks = [refs[order.index(hop)] for hop in range(chips)]
    out_grad, in_grad, combine = refs[chips:]
    loops, share, part = out_grad.shape
    total = blocks[0][...].astype(f32)
    for hop in range(1, chips):
        total = total + blocks[hop][...].astype(f32)
    for l in range(loops):
        rows = slice(l * share, (l + 1) * share)
        out_grad[l] = total[rows, :part]
        in_grad[l] = total[rows, part : part + cols]
    experts = 2 * chips
    owner = owner_column(here(), chips, experts).astype(f32)
    routes = decode(small[...], experts, loops)[0]
    sums = jnp.zeros(combine.shape, f32)
    for j in range(experts):
        half, hop = j // chips, j % chips
        words = blocks[hop][:cap, part:].astype(f32)
        at = cols + 2 * half
        value = words[:, at : at + 1] + words[:, at + 1 : at + 2]
        pick = picks[j * cap : (j + 1) * cap, :].astype(f32)
        by_token = jnp.sum(pick * value, axis=0, keepdims=True)
        sums = sums + jnp.where(routes == owner[j : j + 1, :], by_token, 0.0)
    combine[...] = sums


def product_body(groups, chips, *refs):
    rows, out = refs[:-1], refs[-1]
    _, part, hid_width = out.shape
    slots = chips * rows[0].shape[0]
    rights = [x for h in rows[:groups] for x in hidden_rows(h, hid_width, chips, 0, slots)]
    rights = jnp.concatenate(rights, axis=0)
    step = 256 if part % 256 == 0 else LANES
    for at in range(0, part, step):
        left = [p[:, at : at + step] for g in range(groups) for p in rows[g::groups]]
        out[0, at : at + step, :] = tn(jnp.concatenate(left, axis=0), rights)


def on_device(cotangent, hidden, down_matrix, adapter_in, adapter_out, probs, routes, token_loop):
    experts = lax.axis_size("expert")
    groups = lax.axis_size("dp")
    chips = experts // 2
    toks, width = cotangent.shape
    loops, rank, hid_width = adapter_in.shape
    ways = routes.shape[1]
    slots = hidden.shape[2]
    cap = slots // experts
    part = width // groups
    cols = hid_width // groups
    wide = wide_of(cols)
    share = rank // experts
    bounds = [0, 1, max(2, 3 * chips // 4), chips]
    chunks = [range(a, b) for a, b in zip(bounds[:-1], bounds[1:])]
    flat_in = adapter_in.reshape(loops * rank, hid_width)
    small = token_loop.reshape(1, toks) * (experts + 1) + jnp.minimum(routes.T, experts)
    small = small.astype(f32) + probs.T.astype(f32)

    turns = range(groups - 1, 0, -1)
    natural = hidden.reshape(slots, hid_width)

    with jax.named_scope("route"):
        packed = shape((chips, cap, width + LANES), bf16)
        keep, lead, give, picks = call(
            functools.partial(route_body, chips, cap, loops),
            (
                packed,
                shape((2,) + packed.shape[1:], bf16),
                shape((chips - 1,) + packed.shape[1:], bf16),
                shape((slots, toks), bf16),
            ),
            (V, V),
            scratch=(pltpu.VMEM((slots, toks), bf16),),
            flops=2 * slots * toks * width,
            nbytes=6 * toks * width,
        )(small, cotangent)
        sib = swap(give, "expert", experts, 1)
    with jax.named_scope("dispatch"):
        middle = chips // 2
        lead = swap(lead, "expert", experts, 2 * middle)
        far = {middle: [lead[0], swap(lead[1], "expert", experts, 1)]}
        others = [hop for hop in range(1, bounds[-2]) if hop != middle]
        for hops, after in ((others, []), (chunks[-1], 1)):
            packs = call(
                functools.partial(pack_body, hops, chips),
                tuple(shape((2, cap, width + LANES), bf16) for hop in hops),
                (V, V) + (A,) * bool(after),
                nbytes=4 * slots * width,
            )(keep, sib, *(far[1] if after else []))
            far.update((hop, [swap(x, "expert", experts, 2 * hop)]) for hop, x in zip(hops, packs))
    with jax.named_scope("arrive"):
        rows, masked, parts = [], [], []
        for hops in chunks:
            own, half = hops[0] == 0, 2 * len(hops) * cap
            blocks = [natural, keep, sib] if own else [x for hop in hops for x in far[hop]]
            before = parts[0][1:] if len(parts) == 1 else []
            sent = part + rank + LANES + chips * hid_width * own
            got = call(
                functools.partial(arrive_body, groups, chips, cap, own, len(before)),
                (shape((half, width + LANES), bf16), shape((half, loops * rank), bf16))
                + (shape((half, sent), bf16),) * groups,
                (V,) * (1 + len(blocks)) + (A,) * len(before),
                flops=2 * half * width * loops * rank,
                nbytes=4 * half * width,
            )(adapter_out, *blocks, *before)
            rows.append(got[0])
            masked.append(got[1])
            parts.append([got[2]] + [swap(got[2 + hop], "dp", groups, hop) for hop in turns])
    with jax.named_scope("inner"):
        grad, mix = call(
            functools.partial(inner_body, chips, cap, len(chunks)),
            (shape((slots, hid_width), bf16), shape((slots, LANES), f32)),
            (V,) * (3 + 2 * len(chunks)),
            flops=2 * slots * width * hid_width,
            nbytes=2 * width * hid_width,
        )(down_matrix[0], flat_in, natural, *rows, *masked)
    with jax.named_scope("adapters"):
        work = groups * slots * loops * rank * (part + hid_width + wide)
        sums = (shape((loops * rank, part), f32), shape((loops * rank, wide), f32))
        out, inn = call(
            functools.partial(adapter_first_body, loops, chips, cols, groups),
            sums,
            (V, A) + (V,) * (groups * (len(chunks) - 1)),
            flops=work,
            nbytes=groups * slots * part,
        )(flat_in, mix, *(p for chunk in parts[:-1] for p in chunk))
        block = (chips, loops * share, part + wide)
        keep3, give3 = call(
            functools.partial(adapter_last_body, loops, chips, cap, cols, groups),
            (shape(block, f32), shape(block, bf16)),
            (V,) * (4 + 2 * groups),
            scratch=[pltpu.VMEM(s.shape, f32) for s in sums],
            flops=work,
            nbytes=groups * slots * part,
        )(flat_in, out, inn, mix, *parts[0], *parts[-1])
        got3 = swap(give3, "expert", experts, 1)
        ready = call(
            functools.partial(pair_body, chips),
            (shape(block[1:], bf16),) * chips,
            (V, V),
            nbytes=1e6,
        )(keep3, got3)
        blocks = list(ready)
        for hop in far_first(chips)[1:]:
            blocks[hop] = swap(ready[hop], "expert", experts, 2 * hop)
    with jax.named_scope("product"):
        product = call(
            functools.partial(product_body, groups, chips),
            shape((1, part, hid_width), f32),
            (V,) * (groups * len(chunks)),
            limit=40,
            flops=2 * groups * slots * part * hid_width,
            nbytes=4 * groups * slots * part,
        )(*(p for chunk in parts for p in chunk))
    with jax.named_scope("final"):
        out_grad, in_grad, combine = call(
            functools.partial(final_body, chips, cap, cols),
            (
                shape((loops, share, part), f32),
                shape((loops, share, cols), f32),
                shape((ways, toks), f32),
            ),
            (V,) * (2 + chips),
            nbytes=1e6,
        )(small, picks, *(blocks[hop] for hop in far_first(chips)))
    return (
        grad.reshape(hidden.shape),
        product,
        combine.T,
        in_grad,
        jnp.swapaxes(out_grad, 1, 2),
    )


def solution(mesh):
    return jax.shard_map(
        on_device,
        mesh=mesh,
        in_specs=(
            P(("dp", "expert"), None),
            P("dp", "expert", None, None),
            P("expert", None, None),
            P(),
            P(),
            P(("dp", "expert"), None),
            P(("dp", "expert"), None),
            P(("dp", "expert")),
        ),
        out_specs=(
            P("dp", "expert", None, None),
            P("expert", "dp", None),
            P(("dp", "expert"), None),
            P(None, "expert", "dp"),
            P(None, "dp", "expert"),
        ),
        check_vma=False,
    )
```

```python
import functools

import jax
import jax.numpy as jnp
from jax import lax
from jax.experimental import pallas as pl
from jax.experimental.pallas import tpu as pltpu
from jax.sharding import PartitionSpec as P

bf16 = jnp.bfloat16
f32 = jnp.float32
LANES = 128
MIB = 1 << 20
V, A = pltpu.VMEM, pl.ANY


def dot(a, b, dims):
    return lax.dot_general(a, b, (dims, ((), ())), preferred_element_type=f32)


def nn(a, b):
    return dot(a, b, ((1,), (0,)))


def nt(a, b):
    return dot(a, b, ((1,), (1,)))


def tn(a, b):
    return dot(a, b, ((0,), (0,)))


def swap(x, axis, size, mask):
    return lax.ppermute(x, axis, [(i, i ^ mask) for i in range(size)])


def shape(dims, kind):
    return jax.ShapeDtypeStruct(dims, kind)


def here():
    return lax.axis_index("expert"), lax.axis_index("dp")


def call(body, out_shape, ins, scratch=(), limit=24, flops=0, nbytes=0):
    return pl.pallas_call(
        body,
        out_shape=out_shape,
        in_specs=[pl.BlockSpec(memory_space=s) for s in ins],
        out_specs=jax.tree.map(lambda _: pl.BlockSpec(memory_space=V), out_shape),
        scratch_shapes=list(scratch),
        cost_estimate=pl.CostEstimate(
            flops=int(flops), bytes_accessed=int(nbytes), transcendentals=0
        ),
        compiler_params=pltpu.CompilerParams(vmem_limit_bytes=limit * MIB),
    )


def owner_column(place, chips, experts):
    j = lax.broadcasted_iota(jnp.int32, (experts, 1), 0)
    half, hop = j // chips, j % chips
    return ((place[0] // 2) ^ hop) * 2 + ((place[0] % 2) ^ half)


def decode(small, experts, loops):
    loop = jnp.zeros_like(small)
    for l in range(1, loops):
        loop = loop + jnp.where(small >= l * (experts + 1.0), 1.0, 0.0)
    rest = small - loop * (experts + 1.0)
    route = jnp.floor(rest)
    return route, rest - route, loop[:1]


def deal_rows(middle, rows, at, keep, lead, give):
    chips = keep.shape[0]
    keep[:, :, at] = rows[:chips]
    lead[0, :, at], lead[1, :, at] = rows[middle], rows[chips + middle]
    give[:middle, :, at] = rows[chips : chips + middle]
    if middle + 1 < chips:
        give[middle:, :, at] = rows[chips + middle + 1 :]


def route_body(chips, cap, loops, small, cot, keep, lead, give, picks, mixed):
    middle = chips // 2
    experts = 2 * chips
    ways = small.shape[0]
    toks, width = cot.shape
    owner = owner_column(here(), chips, experts).astype(f32)
    route, chance, loop = decode(small[...], experts, loops)
    named = jnp.zeros((experts, toks), f32)
    weight = jnp.zeros((experts, toks), f32)
    for k in range(ways):
        hit = route[k : k + 1, :] == owner
        named = named + jnp.where(hit, 1.0, 0.0)
        weight = weight + jnp.where(hit, chance[k : k + 1, :], 0.0)
    earlier = lax.broadcasted_iota(jnp.int32, (toks, toks), 0) < lax.broadcasted_iota(
        jnp.int32, (toks, toks), 1
    )
    before = nn(named.astype(bf16), jnp.where(earlier, 1.0, 0.0).astype(bf16))
    spot = jnp.where(named > 0.0, before, -1.0)
    slot = lax.broadcasted_iota(jnp.int32, (cap, toks), 0).astype(f32)
    for j in range(experts):
        hit = spot[j : j + 1, :] == slot
        rows = slice(j * cap, (j + 1) * cap)
        picks[rows, :] = jnp.where(hit, 1.0, 0.0).astype(bf16)
        mixed[rows, :] = jnp.where(hit, weight[j : j + 1, :], 0.0).astype(bf16)
    loop_rows = lax.broadcasted_iota(jnp.int32, (LANES, toks), 0).astype(f32)
    loop_rows = jnp.where(loop_rows == loop, 1.0, 0.0).astype(bf16)
    mix = nt(mixed[...], loop_rows).astype(bf16)
    deal_rows(middle, mix.reshape(2 * chips, cap, LANES), slice(width, width + LANES), keep, lead, give)
    step = 1024 if width % 1024 == 0 else width
    for n in range(0, width, step):
        at = slice(n, n + step)
        got = nn(picks[...], cot[:, at]).astype(bf16)
        deal_rows(middle, got.reshape(2 * chips, cap, step), at, keep, lead, give)


def sources(place, chips):
    z, c = place[0] // 2, place[0] % 2
    return [(z ^ hop) * 2 + (c ^ half) for hop in range(chips) for half in range(2)]


def pack_body(hops, chips, keep, sib, *refs):
    for hop, out in zip(hops, refs[-len(hops) :]):
        out[0, :, : keep.shape[2]] = keep[hop]
        out[1, :, : keep.shape[2]] = sib[hop - (hop > chips // 2)]


def arrive_body(groups, chips, cap, own, extra, adapter_out, *refs):
    loops, width, rank = adapter_out.shape
    part = width // groups
    side = part + rank + LANES
    parts = refs[-groups:]
    blocks, (rows, masked) = refs[: -2 - groups - extra], refs[-2 - groups : -groups]
    if own:
        hidden, blocks = blocks[0], blocks[1:]
        hid_width = hidden.shape[1]
        for n, source in enumerate(sources(here(), chips)):
            block = hidden[pl.ds(pl.multiple_of(source * cap, cap), cap), :]
            start, at = side + (n // 2) * hid_width, (n % 2) * cap
            for target in parts:
                target[at : at + cap, start : start + hid_width] = block
    at = 0
    for block in blocks:
        if len(block.shape) == 2:
            halves = (block[...],)
        else:
            halves = (block[0],) if own else (block[0], block[1])
        for piece in halves:
            rows[at : at + piece.shape[0], :] = piece[:, : rows.shape[1]]
            at += piece.shape[0]
    mix_block = rows[:, width:]
    mix = mix_block.astype(f32)
    weight = jnp.sum(mix, axis=1, keepdims=True)
    for hop in range(groups):
        start = pl.multiple_of((here()[1] ^ hop) * part, part)
        parts[hop][:, :part] = (weight * rows[:, pl.ds(start, part)].astype(f32)).astype(bf16)
    masks = [mix[:, l : l + 1] > 0.0 for l in range(loops)]
    proj = jnp.zeros((rows.shape[0], rank), f32)
    for l in range(loops):
        proj = proj + jnp.where(masks[l], nn(rows[:, :width], adapter_out[l]), 0.0)
    proj = proj.astype(bf16).astype(f32)
    for l in range(loops):
        masked[:, l * rank : (l + 1) * rank] = jnp.where(masks[l], proj, 0.0).astype(bf16)
    weighted = (weight * proj).astype(bf16)
    for hop in range(groups):
        parts[hop][:, part : part + rank] = weighted
        parts[hop][:, part + rank : side] = mix_block


def inner_body(chips, cap, chunks, down, adapter_in, hidden, *refs):
    grad_out, mix_out = refs[-2:]
    width, hid_width = down.shape
    step = 256 if hid_width % 256 == 0 else hid_width
    rows = jnp.concatenate([r[...] for r in refs[:chunks]], axis=0)
    masked = jnp.concatenate([r[...] for r in refs[chunks : 2 * chunks]], axis=0)
    weight = jnp.sum(rows[:, width:].astype(f32), axis=1, keepdims=True)
    sums = jnp.zeros((mix_out.shape[0], 1), f32)
    order = sources(here(), chips)
    for at in range(0, hid_width, step):
        cols = slice(at, at + step)
        grad = nn(masked, adapter_in[:, cols]) + nn(rows[:, :width], down[:, cols])
        spots = [pl.ds(pl.multiple_of(source * cap, cap), cap) for source in order]
        hid = jnp.concatenate([hidden[spot, cols] for spot in spots], axis=0)
        sums = sums + jnp.sum(hid.astype(f32) * grad, axis=1, keepdims=True)
        scaled = (weight * grad).astype(bf16)
        for n, spot in enumerate(spots):
            grad_out[spot, cols] = scaled[n * cap : (n + 1) * cap]
    mix_out[...] = jnp.broadcast_to(sums, mix_out.shape)


def hidden_rows(holder, hid_width, chips, start, stop):
    size = holder.shape[0]
    side = holder.shape[1] - chips * hid_width
    blocks = [side + n * hid_width for n in range(start // size, stop // size)]
    return [holder[:, at : at + hid_width] for at in blocks]


def from_hidden(chips, cols, wide, start, stop, adapter_in, holders):
    hid_width = adapter_in.shape[1]
    row = lax.broadcasted_iota(jnp.int32, (hid_width, wide), 0)
    lane = lax.broadcasted_iota(jnp.int32, (hid_width, wide), 1)
    pick = (row == lane + here()[1] * cols) & (lane < cols)
    pick = jnp.where(pick, 1.0, 0.0).astype(bf16)
    hid = [x for h in holders for x in hidden_rows(h, hid_width, chips, start, stop)]
    hid = jnp.concatenate(hid, axis=0)
    return nt(hid, adapter_in[...]).astype(bf16), nn(hid, pick).astype(bf16)


def adapter_sums(loops, part, rows, down, picked):
    rank = down.shape[1] // loops
    side = part + rank + LANES
    tail = jnp.concatenate([r[:, part:side] for r in rows], axis=0).astype(f32)
    body = jnp.concatenate([r[:, :part] for r in rows], axis=0)
    masks = [tail[:, rank + l : rank + l + 1] > 0.0 for l in range(loops)]
    down = down.astype(f32)
    left = [jnp.where(masks[l], down[:, l * rank : (l + 1) * rank], 0.0) for l in range(loops)]
    out = tn(jnp.concatenate(left, axis=1).astype(bf16), body)
    left = [jnp.where(masks[l], tail[:, :rank], 0.0) for l in range(loops)]
    return out, tn(jnp.concatenate(left, axis=1).astype(bf16), picked)


def wide_of(cols):
    return -(-(cols + 4) // LANES) * LANES


def adapter_first_body(loops, chips, cols, groups, adapter_in, _, *refs):
    rows, (out, inn, down_last, picked_last) = refs[:-4], refs[-4:]
    part, wide = out.shape[1], inn.shape[1]
    start = 0
    for at in range(0, len(rows), groups):
        chunk = rows[at : at + groups]
        stop = start + chunk[0].shape[0]
        parts = from_hidden(chips, cols, wide, start, stop, adapter_in, rows[:groups])
        terms = adapter_sums(loops, part, chunk, *parts)
        for target, term in zip((out, inn), terms):
            target[...] = target[...] + term if start else term
        start = stop
    stop = chips * rows[0].shape[0]
    parts = from_hidden(chips, cols, wide, start, stop, adapter_in, rows[:groups])
    down_last[...], picked_last[...] = parts


def adapter_last_body(loops, chips, cap, cols, out, inn, mix, down, picked, *refs):
    rows, (keep, give, sums, narrow) = refs[:-4], refs[-4:]
    rank = out.shape[0] // loops
    part = out.shape[1]
    share = rank // (2 * chips)
    more = adapter_sums(loops, part, rows, down[...], picked[...])
    sums[...] = out[...] + more[0]
    narrow[...] = inn[...] + more[1]
    owners = sources(here(), chips)
    lane = lax.broadcasted_iota(jnp.int32, (cap, narrow.shape[1]), 1)
    for n, owner in enumerate(owners):
        hop, target = n // 2, (keep, give)[n % 2]
        for l in range(loops):
            src = pl.ds(pl.multiple_of(l * rank + owner * share, share), share)
            dst = slice(l * share, (l + 1) * share)
            target[hop, dst, :part] = sums[src, :].astype(target.dtype)
            target[hop, dst, part:] = narrow[src, :].astype(target.dtype)
        value = mix[n * cap : (n + 1) * cap, :1]
        high = value.astype(bf16).astype(f32)
        tail = target[hop, :cap, part:].astype(f32)
        tail = jnp.where(lane == cols + 2 * (n % 2), high, tail)
        tail = jnp.where(lane == cols + 2 * (n % 2) + 1, value - high, tail)
        target[hop, :cap, part:] = tail.astype(target.dtype)


def pair_body(chips, keep, got, *outs):
    for hop in range(chips):
        outs[hop][...] = (keep[hop] + got[hop].astype(f32)).astype(bf16)


def far_first(chips):
    return [0] + list(range(chips // 2, chips)) + list(range(1, chips // 2))


def final_body(chips, cap, cols, small, picks, *refs):
    order = far_first(chips)
    blocks = [refs[order.index(hop)] for hop in range(chips)]
    out_grad, in_grad, combine = refs[chips:]
    loops, share, part = out_grad.shape
    total = blocks[0][...].astype(f32)
    for hop in range(1, chips):
        total = total + blocks[hop][...].astype(f32)
    for l in range(loops):
        rows = slice(l * share, (l + 1) * share)
        out_grad[l] = total[rows, :part]
        in_grad[l] = total[rows, part : part + cols]
    experts = 2 * chips
    owner = owner_column(here(), chips, experts).astype(f32)
    routes = decode(small[...], experts, loops)[0]
    sums = jnp.zeros(combine.shape, f32)
    for j in range(experts):
        half, hop = j // chips, j % chips
        words = blocks[hop][:cap, part:].astype(f32)
        at = cols + 2 * half
        value = words[:, at : at + 1] + words[:, at + 1 : at + 2]
        pick = picks[j * cap : (j + 1) * cap, :].astype(f32)
        by_token = jnp.sum(pick * value, axis=0, keepdims=True)
        sums = sums + jnp.where(routes == owner[j : j + 1, :], by_token, 0.0)
    combine[...] = sums


def product_body(groups, chips, *refs):
    rows, out = refs[:-1], refs[-1]
    _, part, hid_width = out.shape
    slots = chips * rows[0].shape[0]
    rights = [x for h in rows[:groups] for x in hidden_rows(h, hid_width, chips, 0, slots)]
    rights = jnp.concatenate(rights, axis=0)
    step = 256 if part % 256 == 0 else LANES
    for at in range(0, part, step):
        left = [p[:, at : at + step] for g in range(groups) for p in rows[g::groups]]
        out[0, at : at + step, :] = tn(jnp.concatenate(left, axis=0), rights)


def on_device(cotangent, hidden, down_matrix, adapter_in, adapter_out, probs, routes, token_loop):
    experts = lax.axis_size("expert")
    groups = lax.axis_size("dp")
    chips = experts // 2
    toks, width = cotangent.shape
    loops, rank, hid_width = adapter_in.shape
    ways = routes.shape[1]
    slots = hidden.shape[2]
    cap = slots // experts
    part = width // groups
    cols = hid_width // groups
    wide = wide_of(cols)
    share = rank // experts
    bounds = [0, 1, max(2, 3 * chips // 4), chips]
    chunks = [range(a, b) for a, b in zip(bounds[:-1], bounds[1:])]
    flat_in = adapter_in.reshape(loops * rank, hid_width)
    small = token_loop.reshape(1, toks) * (experts + 1) + jnp.minimum(routes.T, experts)
    small = small.astype(f32) + probs.T.astype(f32)

    turns = range(groups - 1, 0, -1)
    natural = hidden.reshape(slots, hid_width)

    with jax.named_scope("route"):
        packed = shape((chips, cap, width + LANES), bf16)
        keep, lead, give, picks = call(
            functools.partial(route_body, chips, cap, loops),
            (
                packed,
                shape((2,) + packed.shape[1:], bf16),
                shape((chips - 1,) + packed.shape[1:], bf16),
                shape((slots, toks), bf16),
            ),
            (V, V),
            scratch=(pltpu.VMEM((slots, toks), bf16),),
            flops=2 * slots * toks * width,
            nbytes=6 * toks * width,
        )(small, cotangent)
        sib = swap(give, "expert", experts, 1)
    with jax.named_scope("dispatch"):
        middle = chips // 2
        lead = swap(lead, "expert", experts, 2 * middle)
        far = {middle: [lead[0], swap(lead[1], "expert", experts, 1)]}
        others = [hop for hop in range(1, bounds[-2]) if hop != middle]
        for hops, after in ((others, []), (chunks[-1], 1)):
            packs = call(
                functools.partial(pack_body, hops, chips),
                tuple(shape((2, cap, width + LANES), bf16) for hop in hops),
                (V, V) + (A,) * bool(after),
                nbytes=4 * slots * width,
            )(keep, sib, *(far[1] if after else []))
            far.update((hop, [swap(x, "expert", experts, 2 * hop)]) for hop, x in zip(hops, packs))
    with jax.named_scope("arrive"):
        rows, masked, parts = [], [], []
        for hops in chunks:
            own, half = hops[0] == 0, 2 * len(hops) * cap
            blocks = [natural, keep, sib] if own else [x for hop in hops for x in far[hop]]
            before = parts[0][1:] if len(parts) == 1 else []
            sent = part + rank + LANES + chips * hid_width * own
            got = call(
                functools.partial(arrive_body, groups, chips, cap, own, len(before)),
                (shape((half, width + LANES), bf16), shape((half, loops * rank), bf16))
                + (shape((half, sent), bf16),) * groups,
                (V,) * (1 + len(blocks)) + (A,) * len(before),
                flops=2 * half * width * loops * rank,
                nbytes=4 * half * width,
            )(adapter_out, *blocks, *before)
            rows.append(got[0])
            masked.append(got[1])
            parts.append([got[2]] + [swap(got[2 + hop], "dp", groups, hop) for hop in turns])
    with jax.named_scope("inner"):
        grad, mix = call(
            functools.partial(inner_body, chips, cap, len(chunks)),
            (shape((slots, hid_width), bf16), shape((slots, LANES), f32)),
            (V,) * (3 + 2 * len(chunks)),
            flops=2 * slots * width * hid_width,
            nbytes=2 * width * hid_width,
        )(down_matrix[0], flat_in, natural, *rows, *masked)
    with jax.named_scope("adapters"):
        work = groups * slots * loops * rank * (part + hid_width + wide)
        sums = (shape((loops * rank, part), f32), shape((loops * rank, wide), f32))
        size = groups * 2 * len(chunks[-1]) * cap
        out, inn, down, picked = call(
            functools.partial(adapter_first_body, loops, chips, cols, groups),
            sums + (shape((size, loops * rank), bf16), shape((size, wide), bf16)),
            (V, A) + (V,) * (groups * (len(chunks) - 1)),
            flops=work,
            nbytes=groups * slots * part,
        )(flat_in, mix, *(p for chunk in parts[:-1] for p in chunk))
        block = (chips, loops * share, part + wide)
        keep3, give3 = call(
            functools.partial(adapter_last_body, loops, chips, cap, cols),
            (shape(block, f32), shape(block, bf16)),
            (V,) * (5 + groups),
            scratch=[pltpu.VMEM(s.shape, f32) for s in sums],
            flops=work,
            nbytes=groups * slots * part,
        )(out, inn, mix, down, picked, *parts[-1])
        got3 = swap(give3, "expert", experts, 1)
        ready = call(
            functools.partial(pair_body, chips),
            (shape(block[1:], bf16),) * chips,
            (V, V),
            nbytes=1e6,
        )(keep3, got3)
        blocks = list(ready)
        for hop in far_first(chips)[1:]:
            blocks[hop] = swap(ready[hop], "expert", experts, 2 * hop)
    with jax.named_scope("product"):
        product = call(
            functools.partial(product_body, groups, chips),
            shape((1, part, hid_width), f32),
            (V,) * (groups * len(chunks)),
            limit=40,
            flops=2 * groups * slots * part * hid_width,
            nbytes=4 * groups * slots * part,
        )(*(p for chunk in parts for p in chunk))
    with jax.named_scope("final"):
        out_grad, in_grad, combine = call(
            functools.partial(final_body, chips, cap, cols),
            (
                shape((loops, share, part), f32),
                shape((loops, share, cols), f32),
                shape((ways, toks), f32),
            ),
            (V,) * (2 + chips),
            nbytes=1e6,
        )(small, picks, *(blocks[hop] for hop in far_first(chips)))
    return (
        grad.reshape(hidden.shape),
        product,
        combine.T,
        in_grad,
        jnp.swapaxes(out_grad, 1, 2),
    )


def solution(mesh):
    return jax.shard_map(
        on_device,
        mesh=mesh,
        in_specs=(
            P(("dp", "expert"), None),
            P("dp", "expert", None, None),
            P("expert", None, None),
            P(),
            P(),
            P(("dp", "expert"), None),
            P(("dp", "expert"), None),
            P(("dp", "expert")),
        ),
        out_specs=(
            P("dp", "expert", None, None),
            P("expert", "dp", None),
            P(("dp", "expert"), None),
            P(None, "expert", "dp"),
            P(None, "dp", "expert"),
        ),
        check_vma=False,
    )
```

```python
import functools

import jax
import jax.numpy as jnp
from jax import lax
from jax.experimental import pallas as pl
from jax.experimental.pallas import tpu as pltpu
from jax.sharding import PartitionSpec as P

bf16 = jnp.bfloat16
f32 = jnp.float32
LANES = 128
MIB = 1 << 20
V, A = pltpu.VMEM, pl.ANY


def dot(a, b, dims):
    return lax.dot_general(a, b, (dims, ((), ())), preferred_element_type=f32)


def nn(a, b):
    return dot(a, b, ((1,), (0,)))


def nt(a, b):
    return dot(a, b, ((1,), (1,)))


def tn(a, b):
    return dot(a, b, ((0,), (0,)))


def swap(x, axis, size, mask):
    return lax.ppermute(x, axis, [(i, i ^ mask) for i in range(size)])


def shape(dims, kind):
    return jax.ShapeDtypeStruct(dims, kind)


def here():
    return lax.axis_index("expert"), lax.axis_index("dp")


def call(body, out_shape, ins, scratch=(), limit=24, flops=0, nbytes=0):
    return pl.pallas_call(
        body,
        out_shape=out_shape,
        in_specs=[pl.BlockSpec(memory_space=s) for s in ins],
        out_specs=jax.tree.map(lambda _: pl.BlockSpec(memory_space=V), out_shape),
        scratch_shapes=list(scratch),
        cost_estimate=pl.CostEstimate(
            flops=int(flops), bytes_accessed=int(nbytes), transcendentals=0
        ),
        compiler_params=pltpu.CompilerParams(vmem_limit_bytes=limit * MIB),
    )


def owner_column(place, chips, experts):
    j = lax.broadcasted_iota(jnp.int32, (experts, 1), 0)
    half, hop = j // chips, j % chips
    return ((place[0] // 2) ^ hop) * 2 + ((place[0] % 2) ^ half)


def decode(small, loops):
    whole = jnp.floor(small)
    route = jnp.floor((whole + 0.5) * (1.0 / loops))
    return route, small - whole, (whole - route * loops)[:1]


def deal_rows(middle, rows, at, keep, lead, give):
    chips = keep.shape[0]
    keep[:, :, at] = rows[:chips]
    lead[0, :, at], lead[1, :, at] = rows[middle], rows[chips + middle]
    give[:middle, :, at] = rows[chips : chips + middle]
    if middle + 1 < chips:
        give[middle:, :, at] = rows[chips + middle + 1 :]


def route_body(chips, cap, loops, small, cot, keep, lead, give, picks, mixed):
    middle = chips // 2
    experts = 2 * chips
    ways = small.shape[0]
    toks, width = cot.shape
    owner = owner_column(here(), chips, experts).astype(f32)
    route, chance, loop = decode(small[...], loops)
    named = jnp.zeros((experts, toks), f32)
    weight = jnp.zeros((experts, toks), f32)
    for k in range(ways):
        hit = route[k : k + 1, :] == owner
        named = named + jnp.where(hit, 1.0, 0.0)
        weight = weight + jnp.where(hit, chance[k : k + 1, :], 0.0)
    earlier = lax.broadcasted_iota(jnp.int32, (toks, toks), 0) < lax.broadcasted_iota(
        jnp.int32, (toks, toks), 1
    )
    before = nn(named.astype(bf16), jnp.where(earlier, 1.0, 0.0).astype(bf16))
    spot = jnp.where(named > 0.0, before, -1.0)
    slot = lax.broadcasted_iota(jnp.int32, (cap, toks), 0).astype(f32)
    for j in range(experts):
        hit = spot[j : j + 1, :] == slot
        rows = slice(j * cap, (j + 1) * cap)
        picks[rows, :] = jnp.where(hit, 1.0, 0.0).astype(bf16)
        mixed[rows, :] = jnp.where(hit, weight[j : j + 1, :], 0.0).astype(bf16)
    loop_rows = lax.broadcasted_iota(jnp.int32, (LANES, toks), 0).astype(f32)
    loop_rows = jnp.where(loop_rows == loop, 1.0, 0.0).astype(bf16)
    mix = nt(mixed[...], loop_rows).astype(bf16)
    deal_rows(middle, mix.reshape(2 * chips, cap, LANES), slice(width, width + LANES), keep, lead, give)
    step = 1024 if width % 1024 == 0 else width
    for n in range(0, width, step):
        at = slice(n, n + step)
        got = nn(picks[...], cot[:, at]).astype(bf16)
        deal_rows(middle, got.reshape(2 * chips, cap, step), at, keep, lead, give)


def sources(place, chips):
    z, c = place[0] // 2, place[0] % 2
    return [(z ^ hop) * 2 + (c ^ half) for hop in range(chips) for half in range(2)]


def pack_body(hops, chips, keep, sib, *refs):
    for hop, out in zip(hops, refs[-len(hops) :]):
        out[0, :, : keep.shape[2]] = keep[hop]
        out[1, :, : keep.shape[2]] = sib[hop - (hop > chips // 2)]


def arrive_body(groups, chips, cap, own, extra, adapter_out, *refs):
    loops, width, rank = adapter_out.shape
    part = width // groups
    side = part + rank + LANES
    parts = refs[-groups:]
    blocks, (rows, masked) = refs[: -2 - groups - extra], refs[-2 - groups : -groups]
    if own:
        hidden, blocks = blocks[0], blocks[1:]
        hid_width = hidden.shape[1]
        for n, source in enumerate(sources(here(), chips)):
            block = hidden[pl.ds(pl.multiple_of(source * cap, cap), cap), :]
            start, at = side + (n // 2) * hid_width, (n % 2) * cap
            for target in parts:
                target[at : at + cap, start : start + hid_width] = block
    at = 0
    for block in blocks:
        if len(block.shape) == 2:
            halves = (block[...],)
        else:
            halves = (block[0],) if own else (block[0], block[1])
        for piece in halves:
            rows[at : at + piece.shape[0], :] = piece[:, : rows.shape[1]]
            at += piece.shape[0]
    mix_block = rows[:, width:]
    mix = mix_block.astype(f32)
    weight = jnp.sum(mix, axis=1, keepdims=True)
    for hop in range(groups):
        start = pl.multiple_of((here()[1] ^ hop) * part, part)
        parts[hop][:, :part] = (weight * rows[:, pl.ds(start, part)].astype(f32)).astype(bf16)
    masks = [mix[:, l : l + 1] > 0.0 for l in range(loops)]
    proj = jnp.zeros((rows.shape[0], rank), f32)
    for l in range(loops):
        proj = proj + jnp.where(masks[l], nn(rows[:, :width], adapter_out[l]), 0.0)
    proj = proj.astype(bf16).astype(f32)
    for l in range(loops):
        masked[:, l * rank : (l + 1) * rank] = jnp.where(masks[l], proj, 0.0).astype(bf16)
    weighted = (weight * proj).astype(bf16)
    for hop in range(groups):
        parts[hop][:, part : part + rank] = weighted
        parts[hop][:, part + rank : side] = mix_block


def inner_body(chips, cap, chunks, down, adapter_in, hidden, *refs):
    grad_out, mix_out = refs[-2:]
    width, hid_width = down.shape
    step = 256 if hid_width % 256 == 0 else hid_width
    rows = jnp.concatenate([r[...] for r in refs[:chunks]], axis=0)
    masked = jnp.concatenate([r[...] for r in refs[chunks : 2 * chunks]], axis=0)
    weight = jnp.sum(rows[:, width:].astype(f32), axis=1, keepdims=True)
    sums = jnp.zeros((mix_out.shape[0], 1), f32)
    order = sources(here(), chips)
    for at in range(0, hid_width, step):
        cols = slice(at, at + step)
        grad = nn(masked, adapter_in[:, cols]) + nn(rows[:, :width], down[:, cols])
        spots = [pl.ds(pl.multiple_of(source * cap, cap), cap) for source in order]
        hid = jnp.concatenate([hidden[spot, cols] for spot in spots], axis=0)
        sums = sums + jnp.sum(hid.astype(f32) * grad, axis=1, keepdims=True)
        scaled = (weight * grad).astype(bf16)
        for n, spot in enumerate(spots):
            grad_out[spot, cols] = scaled[n * cap : (n + 1) * cap]
    mix_out[...] = jnp.broadcast_to(sums, mix_out.shape)


def hidden_rows(holder, hid_width, chips, start, stop):
    size = holder.shape[0]
    side = holder.shape[1] - chips * hid_width
    blocks = [side + n * hid_width for n in range(start // size, stop // size)]
    return [holder[:, at : at + hid_width] for at in blocks]


def from_hidden(chips, cols, wide, start, stop, adapter_in, holders):
    hid_width = adapter_in.shape[1]
    row = lax.broadcasted_iota(jnp.int32, (hid_width, wide), 0)
    lane = lax.broadcasted_iota(jnp.int32, (hid_width, wide), 1)
    pick = (row == lane + here()[1] * cols) & (lane < cols)
    pick = jnp.where(pick, 1.0, 0.0).astype(bf16)
    hid = [x for h in holders for x in hidden_rows(h, hid_width, chips, start, stop)]
    hid = jnp.concatenate(hid, axis=0)
    return nt(hid, adapter_in[...]).astype(bf16), nn(hid, pick).astype(bf16)


def adapter_sums(loops, part, rows, down, picked):
    rank = down.shape[1] // loops
    side = part + rank + LANES
    tail = jnp.concatenate([r[:, part:side] for r in rows], axis=0).astype(f32)
    body = jnp.concatenate([r[:, :part] for r in rows], axis=0)
    masks = [tail[:, rank + l : rank + l + 1] > 0.0 for l in range(loops)]
    down = down.astype(f32)
    left = [jnp.where(masks[l], down[:, l * rank : (l + 1) * rank], 0.0) for l in range(loops)]
    out = tn(jnp.concatenate(left, axis=1).astype(bf16), body)
    left = [jnp.where(masks[l], tail[:, :rank], 0.0) for l in range(loops)]
    return out, tn(jnp.concatenate(left, axis=1).astype(bf16), picked)


def wide_of(cols):
    return -(-(cols + 4) // LANES) * LANES


def adapter_first_body(loops, chips, cols, groups, adapter_in, _, *refs):
    rows, (out, inn, down_last, picked_last) = refs[:-4], refs[-4:]
    part, wide = out.shape[1], inn.shape[1]
    start = 0
    for at in range(0, len(rows), groups):
        chunk = rows[at : at + groups]
        stop = start + chunk[0].shape[0]
        parts = from_hidden(chips, cols, wide, start, stop, adapter_in, rows[:groups])
        terms = adapter_sums(loops, part, chunk, *parts)
        for target, term in zip((out, inn), terms):
            target[...] = target[...] + term if start else term
        start = stop
    stop = chips * rows[0].shape[0]
    parts = from_hidden(chips, cols, wide, start, stop, adapter_in, rows[:groups])
    down_last[...], picked_last[...] = parts


def adapter_last_body(loops, chips, cap, cols, out, inn, mix, down, picked, *refs):
    rows, (keep, give, sums, narrow) = refs[:-4], refs[-4:]
    rank = out.shape[0] // loops
    part = out.shape[1]
    share = rank // (2 * chips)
    more = adapter_sums(loops, part, rows, down[...], picked[...])
    sums[...] = out[...] + more[0]
    narrow[...] = inn[...] + more[1]
    owners = sources(here(), chips)
    lane = lax.broadcasted_iota(jnp.int32, (cap, narrow.shape[1]), 1)
    for n, owner in enumerate(owners):
        hop, target = n // 2, (keep, give)[n % 2]
        for l in range(loops):
            src = pl.ds(pl.multiple_of(l * rank + owner * share, share), share)
            dst = slice(l * share, (l + 1) * share)
            target[hop, dst, :part] = sums[src, :].astype(target.dtype)
            target[hop, dst, part:] = narrow[src, :].astype(target.dtype)
        value = mix[n * cap : (n + 1) * cap, :1]
        high = value.astype(bf16).astype(f32)
        tail = target[hop, :cap, part:].astype(f32)
        tail = jnp.where(lane == cols + 2 * (n % 2), high, tail)
        tail = jnp.where(lane == cols + 2 * (n % 2) + 1, value - high, tail)
        target[hop, :cap, part:] = tail.astype(target.dtype)


def pair_body(chips, keep, got, *outs):
    for hop in range(chips):
        outs[hop][...] = (keep[hop] + got[hop].astype(f32)).astype(bf16)


def far_first(chips):
    return [0] + list(range(chips // 2, chips)) + list(range(1, chips // 2))


def final_body(chips, cap, cols, small, picks, *refs):
    order = far_first(chips)
    blocks = [refs[order.index(hop)] for hop in range(chips)]
    out_grad, in_grad, combine = refs[chips:]
    loops, share, part = out_grad.shape
    total = blocks[0][...].astype(f32)
    for hop in range(1, chips):
        total = total + blocks[hop][...].astype(f32)
    for l in range(loops):
        rows = slice(l * share, (l + 1) * share)
        out_grad[l] = total[rows, :part]
        in_grad[l] = total[rows, part : part + cols]
    experts = 2 * chips
    owner = owner_column(here(), chips, experts).astype(f32)
    routes = decode(small[...], loops)[0]
    sums = jnp.zeros(combine.shape, f32)
    for j in range(experts):
        half, hop = j // chips, j % chips
        words = blocks[hop][:cap, part:].astype(f32)
        at = cols + 2 * half
        value = words[:, at : at + 1] + words[:, at + 1 : at + 2]
        pick = picks[j * cap : (j + 1) * cap, :].astype(f32)
        by_token = jnp.sum(pick * value, axis=0, keepdims=True)
        sums = sums + jnp.where(routes == owner[j : j + 1, :], by_token, 0.0)
    combine[...] = sums


def product_body(groups, chips, *refs):
    rows, out = refs[:-1], refs[-1]
    _, part, hid_width = out.shape
    slots = chips * rows[0].shape[0]
    rights = [x for h in rows[:groups] for x in hidden_rows(h, hid_width, chips, 0, slots)]
    rights = jnp.concatenate(rights, axis=0)
    step = 256 if part % 256 == 0 else LANES
    for at in range(0, part, step):
        left = [p[:, at : at + step] for g in range(groups) for p in rows[g::groups]]
        out[0, at : at + step, :] = tn(jnp.concatenate(left, axis=0), rights)


def on_device(cotangent, hidden, down_matrix, adapter_in, adapter_out, probs, routes, token_loop):
    experts = lax.axis_size("expert")
    groups = lax.axis_size("dp")
    chips = experts // 2
    toks, width = cotangent.shape
    loops, rank, hid_width = adapter_in.shape
    ways = routes.shape[1]
    slots = hidden.shape[2]
    cap = slots // experts
    part = width // groups
    cols = hid_width // groups
    wide = wide_of(cols)
    share = rank // experts
    bounds = [0, 1, max(2, 3 * chips // 4), chips]
    chunks = [range(a, b) for a, b in zip(bounds[:-1], bounds[1:])]
    flat_in = adapter_in.reshape(loops * rank, hid_width)
    small = jnp.minimum(routes.T, experts) * loops + token_loop.reshape(1, toks)
    small = small.astype(f32) + probs.T.astype(f32)

    turns = range(groups - 1, 0, -1)
    natural = hidden.reshape(slots, hid_width)

    with jax.named_scope("route"):
        packed = shape((chips, cap, width + LANES), bf16)
        keep, lead, give, picks = call(
            functools.partial(route_body, chips, cap, loops),
            (
                packed,
                shape((2,) + packed.shape[1:], bf16),
                shape((chips - 1,) + packed.shape[1:], bf16),
                shape((slots, toks), bf16),
            ),
            (V, V),
            scratch=(pltpu.VMEM((slots, toks), bf16),),
            flops=2 * slots * toks * width,
            nbytes=6 * toks * width,
        )(small, cotangent)
        sib = swap(give, "expert", experts, 1)
    with jax.named_scope("dispatch"):
        middle = chips // 2
        lead = swap(lead, "expert", experts, 2 * middle)
        far = {middle: [lead[0], swap(lead[1], "expert", experts, 1)]}
        others = [hop for hop in range(1, bounds[-2]) if hop != middle]
        for hops, after in ((others, []), (chunks[-1], 1)):
            packs = call(
                functools.partial(pack_body, hops, chips),
                tuple(shape((2, cap, width + LANES), bf16) for hop in hops),
                (V, V) + (A,) * bool(after),
                nbytes=4 * slots * width,
            )(keep, sib, *(far[1] if after else []))
            far.update((hop, [swap(x, "expert", experts, 2 * hop)]) for hop, x in zip(hops, packs))
    with jax.named_scope("arrive"):
        rows, masked, parts = [], [], []
        for hops in chunks:
            own, half = hops[0] == 0, 2 * len(hops) * cap
            blocks = [natural, keep, sib] if own else [x for hop in hops for x in far[hop]]
            before = parts[0][1:] if len(parts) == 1 else []
            sent = part + rank + LANES + chips * hid_width * own
            got = call(
                functools.partial(arrive_body, groups, chips, cap, own, len(before)),
                (shape((half, width + LANES), bf16), shape((half, loops * rank), bf16))
                + (shape((half, sent), bf16),) * groups,
                (V,) * (1 + len(blocks)) + (A,) * len(before),
                flops=2 * half * width * loops * rank,
                nbytes=4 * half * width,
            )(adapter_out, *blocks, *before)
            rows.append(got[0])
            masked.append(got[1])
            parts.append([got[2]] + [swap(got[2 + hop], "dp", groups, hop) for hop in turns])
    with jax.named_scope("inner"):
        grad, mix = call(
            functools.partial(inner_body, chips, cap, len(chunks)),
            (shape((slots, hid_width), bf16), shape((slots, LANES), f32)),
            (V,) * (3 + 2 * len(chunks)),
            flops=2 * slots * width * hid_width,
            nbytes=2 * width * hid_width,
        )(down_matrix[0], flat_in, natural, *rows, *masked)
    with jax.named_scope("adapters"):
        work = groups * slots * loops * rank * (part + hid_width + wide)
        sums = (shape((loops * rank, part), f32), shape((loops * rank, wide), f32))
        size = groups * 2 * len(chunks[-1]) * cap
        out, inn, down, picked = call(
            functools.partial(adapter_first_body, loops, chips, cols, groups),
            sums + (shape((size, loops * rank), bf16), shape((size, wide), bf16)),
            (V, A) + (V,) * (groups * (len(chunks) - 1)),
            flops=work,
            nbytes=groups * slots * part,
        )(flat_in, mix, *(p for chunk in parts[:-1] for p in chunk))
        block = (chips, loops * share, part + wide)
        keep3, give3 = call(
            functools.partial(adapter_last_body, loops, chips, cap, cols),
            (shape(block, f32), shape(block, bf16)),
            (V,) * (5 + groups),
            scratch=[pltpu.VMEM(s.shape, f32) for s in sums],
            flops=work,
            nbytes=groups * slots * part,
        )(out, inn, mix, down, picked, *parts[-1])
        got3 = swap(give3, "expert", experts, 1)
        ready = call(
            functools.partial(pair_body, chips),
            (shape(block[1:], bf16),) * chips,
            (V, V),
            nbytes=1e6,
        )(keep3, got3)
        blocks = list(ready)
        for hop in far_first(chips)[1:]:
            blocks[hop] = swap(ready[hop], "expert", experts, 2 * hop)
    with jax.named_scope("product"):
        product = call(
            functools.partial(product_body, groups, chips),
            shape((1, part, hid_width), f32),
            (V,) * (groups * len(chunks)),
            limit=40,
            flops=2 * groups * slots * part * hid_width,
            nbytes=4 * groups * slots * part,
        )(*(p for chunk in parts for p in chunk))
    with jax.named_scope("final"):
        out_grad, in_grad, combine = call(
            functools.partial(final_body, chips, cap, cols),
            (
                shape((loops, share, part), f32),
                shape((loops, share, cols), f32),
                shape((ways, toks), f32),
            ),
            (V,) * (2 + chips),
            nbytes=1e6,
        )(small, picks, *(blocks[hop] for hop in far_first(chips)))
    return (
        grad.reshape(hidden.shape),
        product,
        combine.T,
        in_grad,
        jnp.swapaxes(out_grad, 1, 2),
    )


def solution(mesh):
    return jax.shard_map(
        on_device,
        mesh=mesh,
        in_specs=(
            P(("dp", "expert"), None),
            P("dp", "expert", None, None),
            P("expert", None, None),
            P(),
            P(),
            P(("dp", "expert"), None),
            P(("dp", "expert"), None),
            P(("dp", "expert")),
        ),
        out_specs=(
            P("dp", "expert", None, None),
            P("expert", "dp", None),
            P(("dp", "expert"), None),
            P(None, "expert", "dp"),
            P(None, "dp", "expert"),
        ),
        check_vma=False,
    )
```

```python
import functools

import jax
import jax.numpy as jnp
from jax import lax
from jax.experimental import pallas as pl
from jax.experimental.pallas import tpu as pltpu
from jax.sharding import PartitionSpec as P

bf16 = jnp.bfloat16
f32 = jnp.float32
LANES = 128
MIB = 1 << 20
V, A = pltpu.VMEM, pl.ANY


def dot(a, b, dims):
    return lax.dot_general(a, b, (dims, ((), ())), preferred_element_type=f32)


def nn(a, b):
    return dot(a, b, ((1,), (0,)))


def nt(a, b):
    return dot(a, b, ((1,), (1,)))


def tn(a, b):
    return dot(a, b, ((0,), (0,)))


def swap(x, axis, size, mask):
    return lax.ppermute(x, axis, [(i, i ^ mask) for i in range(size)])


def shape(dims, kind):
    return jax.ShapeDtypeStruct(dims, kind)


def here():
    return lax.axis_index("expert"), lax.axis_index("dp")


def call(body, out_shape, ins, scratch=(), limit=24, flops=0, nbytes=0):
    return pl.pallas_call(
        body,
        out_shape=out_shape,
        in_specs=[pl.BlockSpec(memory_space=s) for s in ins],
        out_specs=jax.tree.map(lambda _: pl.BlockSpec(memory_space=V), out_shape),
        scratch_shapes=list(scratch),
        cost_estimate=pl.CostEstimate(
            flops=int(flops), bytes_accessed=int(nbytes), transcendentals=0
        ),
        compiler_params=pltpu.CompilerParams(vmem_limit_bytes=limit * MIB),
    )


def owner_column(place, chips, experts):
    j = lax.broadcasted_iota(jnp.int32, (experts, 1), 0)
    half, hop = j // chips, j % chips
    return ((place[0] // 2) ^ hop) * 2 + ((place[0] % 2) ^ half)


def decode(small, loops):
    whole = jnp.floor(small)
    route = jnp.floor((whole + 0.5) * (1.0 / loops))
    return route, small - whole, (whole - route * loops)[:1]


def deal_rows(middle, rows, at, keep, lead, give):
    chips = keep.shape[0]
    keep[:, :, at] = rows[:chips]
    lead[0, :, at], lead[1, :, at] = rows[middle], rows[chips + middle]
    give[:middle, :, at] = rows[chips : chips + middle]
    if middle + 1 < chips:
        give[middle:, :, at] = rows[chips + middle + 1 :]


def route_body(chips, cap, loops, small, cot_h, keep, lead, give, picks, cot, mixed, sems):
    step = cot.shape[1] // sems.shape[0]
    columns = [
        pltpu.make_async_copy(
            cot_h.at[:, pl.ds(n, step)], cot.at[:, pl.ds(n, step)], sems.at[n // step]
        )
        for n in range(0, cot.shape[1], step)
    ]
    for column in columns:
        column.start()
    middle = chips // 2
    experts = 2 * chips
    ways = small.shape[0]
    toks, width = cot.shape
    owner = owner_column(here(), chips, experts).astype(f32)
    route, chance, loop = decode(small[...], loops)
    named = jnp.zeros((experts, toks), f32)
    weight = jnp.zeros((experts, toks), f32)
    for k in range(ways):
        hit = route[k : k + 1, :] == owner
        named = named + jnp.where(hit, 1.0, 0.0)
        weight = weight + jnp.where(hit, chance[k : k + 1, :], 0.0)
    earlier = lax.broadcasted_iota(jnp.int32, (toks, toks), 0) < lax.broadcasted_iota(
        jnp.int32, (toks, toks), 1
    )
    before = nn(named.astype(bf16), jnp.where(earlier, 1.0, 0.0).astype(bf16))
    spot = jnp.where(named > 0.0, before, -1.0)
    slot = lax.broadcasted_iota(jnp.int32, (cap, toks), 0).astype(f32)
    for j in range(experts):
        hit = spot[j : j + 1, :] == slot
        rows = slice(j * cap, (j + 1) * cap)
        picks[rows, :] = jnp.where(hit, 1.0, 0.0).astype(bf16)
        mixed[rows, :] = jnp.where(hit, weight[j : j + 1, :], 0.0).astype(bf16)
    loop_rows = lax.broadcasted_iota(jnp.int32, (LANES, toks), 0).astype(f32)
    loop_rows = jnp.where(loop_rows == loop, 1.0, 0.0).astype(bf16)
    mix = nt(mixed[...], loop_rows).astype(bf16)
    deal_rows(middle, mix.reshape(2 * chips, cap, LANES), slice(width, width + LANES), keep, lead, give)
    for n in range(0, width, step):
        columns[n // step].wait()
        at = slice(n, n + step)
        got = nn(picks[...], cot[:, at]).astype(bf16)
        deal_rows(middle, got.reshape(2 * chips, cap, step), at, keep, lead, give)


def sources(place, chips):
    z, c = place[0] // 2, place[0] % 2
    return [(z ^ hop) * 2 + (c ^ half) for hop in range(chips) for half in range(2)]


def pack_body(hops, chips, keep, sib, *refs):
    for hop, out in zip(hops, refs[-len(hops) :]):
        out[0, :, : keep.shape[2]] = keep[hop]
        out[1, :, : keep.shape[2]] = sib[hop - (hop > chips // 2)]


def arrive_body(groups, chips, cap, own, extra, adapter_out, *refs):
    loops, width, rank = adapter_out.shape
    part = width // groups
    side = part + rank + LANES
    parts = refs[-groups:]
    blocks, (rows, masked) = refs[: -2 - groups - extra], refs[-2 - groups : -groups]
    if own:
        hidden, blocks = blocks[0], blocks[1:]
        hid_width = hidden.shape[1]
        for n, source in enumerate(sources(here(), chips)):
            block = hidden[pl.ds(pl.multiple_of(source * cap, cap), cap), :]
            start, at = side + (n // 2) * hid_width, (n % 2) * cap
            for target in parts:
                target[at : at + cap, start : start + hid_width] = block
    at = 0
    for block in blocks:
        if len(block.shape) == 2:
            halves = (block[...],)
        else:
            halves = (block[0],) if own else (block[0], block[1])
        for piece in halves:
            rows[at : at + piece.shape[0], :] = piece[:, : rows.shape[1]]
            at += piece.shape[0]
    mix_block = rows[:, width:]
    mix = mix_block.astype(f32)
    weight = jnp.sum(mix, axis=1, keepdims=True)
    for hop in range(groups):
        start = pl.multiple_of((here()[1] ^ hop) * part, part)
        parts[hop][:, :part] = (weight * rows[:, pl.ds(start, part)].astype(f32)).astype(bf16)
    masks = [mix[:, l : l + 1] > 0.0 for l in range(loops)]
    proj = jnp.zeros((rows.shape[0], rank), f32)
    for l in range(loops):
        proj = proj + jnp.where(masks[l], nn(rows[:, :width], adapter_out[l]), 0.0)
    proj = proj.astype(bf16).astype(f32)
    for l in range(loops):
        masked[:, l * rank : (l + 1) * rank] = jnp.where(masks[l], proj, 0.0).astype(bf16)
    weighted = (weight * proj).astype(bf16)
    for hop in range(groups):
        parts[hop][:, part : part + rank] = weighted
        parts[hop][:, part + rank : side] = mix_block


def inner_body(chips, cap, chunks, down, adapter_in, hidden, *refs):
    grad_out, mix_out = refs[-2:]
    width, hid_width = down.shape
    step = 256 if hid_width % 256 == 0 else hid_width
    rows = jnp.concatenate([r[...] for r in refs[:chunks]], axis=0)
    masked = jnp.concatenate([r[...] for r in refs[chunks : 2 * chunks]], axis=0)
    weight = jnp.sum(rows[:, width:].astype(f32), axis=1, keepdims=True)
    sums = jnp.zeros((mix_out.shape[0], 1), f32)
    order = sources(here(), chips)
    for at in range(0, hid_width, step):
        cols = slice(at, at + step)
        grad = nn(masked, adapter_in[:, cols]) + nn(rows[:, :width], down[:, cols])
        spots = [pl.ds(pl.multiple_of(source * cap, cap), cap) for source in order]
        hid = jnp.concatenate([hidden[spot, cols] for spot in spots], axis=0)
        sums = sums + jnp.sum(hid.astype(f32) * grad, axis=1, keepdims=True)
        scaled = (weight * grad).astype(bf16)
        for n, spot in enumerate(spots):
            grad_out[spot, cols] = scaled[n * cap : (n + 1) * cap]
    mix_out[...] = jnp.broadcast_to(sums, mix_out.shape)


def hidden_rows(holder, hid_width, chips, start, stop):
    size = holder.shape[0]
    side = holder.shape[1] - chips * hid_width
    blocks = [side + n * hid_width for n in range(start // size, stop // size)]
    return [holder[:, at : at + hid_width] for at in blocks]


def from_hidden(chips, cols, wide, start, stop, adapter_in, holders):
    hid_width = adapter_in.shape[1]
    row = lax.broadcasted_iota(jnp.int32, (hid_width, wide), 0)
    lane = lax.broadcasted_iota(jnp.int32, (hid_width, wide), 1)
    pick = (row == lane + here()[1] * cols) & (lane < cols)
    pick = jnp.where(pick, 1.0, 0.0).astype(bf16)
    hid = [x for h in holders for x in hidden_rows(h, hid_width, chips, start, stop)]
    hid = jnp.concatenate(hid, axis=0)
    return nt(hid, adapter_in[...]).astype(bf16), nn(hid, pick).astype(bf16)


def adapter_sums(loops, part, rows, down, picked):
    rank = down.shape[1] // loops
    side = part + rank + LANES
    tail = jnp.concatenate([r[:, part:side] for r in rows], axis=0).astype(f32)
    body = jnp.concatenate([r[:, :part] for r in rows], axis=0)
    masks = [tail[:, rank + l : rank + l + 1] > 0.0 for l in range(loops)]
    down = down.astype(f32)
    left = [jnp.where(masks[l], down[:, l * rank : (l + 1) * rank], 0.0) for l in range(loops)]
    out = tn(jnp.concatenate(left, axis=1).astype(bf16), body)
    left = [jnp.where(masks[l], tail[:, :rank], 0.0) for l in range(loops)]
    return out, tn(jnp.concatenate(left, axis=1).astype(bf16), picked)


def wide_of(cols):
    return -(-(cols + 4) // LANES) * LANES


def adapter_first_body(loops, chips, cols, groups, adapter_in, _, *refs):
    rows, (out, inn, down_last, picked_last) = refs[:-4], refs[-4:]
    part, wide = out.shape[1], inn.shape[1]
    start = 0
    for at in range(0, len(rows), groups):
        chunk = rows[at : at + groups]
        stop = start + chunk[0].shape[0]
        parts = from_hidden(chips, cols, wide, start, stop, adapter_in, rows[:groups])
        terms = adapter_sums(loops, part, chunk, *parts)
        for target, term in zip((out, inn), terms):
            target[...] = target[...] + term if start else term
        start = stop
    stop = chips * rows[0].shape[0]
    parts = from_hidden(chips, cols, wide, start, stop, adapter_in, rows[:groups])
    down_last[...], picked_last[...] = parts


def adapter_last_body(loops, chips, cap, cols, out, inn, mix, down, picked, *refs):
    rows, (keep, give, sums, narrow) = refs[:-4], refs[-4:]
    rank = out.shape[0] // loops
    part = out.shape[1]
    share = rank // (2 * chips)
    more = adapter_sums(loops, part, rows, down[...], picked[...])
    sums[...] = out[...] + more[0]
    narrow[...] = inn[...] + more[1]
    owners = sources(here(), chips)
    lane = lax.broadcasted_iota(jnp.int32, (cap, narrow.shape[1]), 1)
    for n, owner in enumerate(owners):
        hop, target = n // 2, (keep, give)[n % 2]
        for l in range(loops):
            src = pl.ds(pl.multiple_of(l * rank + owner * share, share), share)
            dst = slice(l * share, (l + 1) * share)
            target[hop, dst, :part] = sums[src, :].astype(target.dtype)
            target[hop, dst, part:] = narrow[src, :].astype(target.dtype)
        value = mix[n * cap : (n + 1) * cap, :1]
        high = value.astype(bf16).astype(f32)
        tail = target[hop, :cap, part:].astype(f32)
        tail = jnp.where(lane == cols + 2 * (n % 2), high, tail)
        tail = jnp.where(lane == cols + 2 * (n % 2) + 1, value - high, tail)
        target[hop, :cap, part:] = tail.astype(target.dtype)


def pair_body(chips, keep, got, *outs):
    for hop in range(chips):
        outs[hop][...] = (keep[hop] + got[hop].astype(f32)).astype(bf16)


def far_first(chips):
    return [0] + list(range(chips // 2, chips)) + list(range(1, chips // 2))


def final_body(chips, cap, cols, small, picks, *refs):
    order = far_first(chips)
    blocks = [refs[order.index(hop)] for hop in range(chips)]
    out_grad, in_grad, combine = refs[chips:]
    loops, share, part = out_grad.shape
    total = blocks[0][...].astype(f32)
    for hop in range(1, chips):
        total = total + blocks[hop][...].astype(f32)
    for l in range(loops):
        rows = slice(l * share, (l + 1) * share)
        out_grad[l] = total[rows, :part]
        in_grad[l] = total[rows, part : part + cols]
    experts = 2 * chips
    owner = owner_column(here(), chips, experts).astype(f32)
    routes = decode(small[...], loops)[0]
    sums = jnp.zeros(combine.shape, f32)
    for j in range(experts):
        half, hop = j // chips, j % chips
        words = blocks[hop][:cap, part:].astype(f32)
        at = cols + 2 * half
        value = words[:, at : at + 1] + words[:, at + 1 : at + 2]
        pick = picks[j * cap : (j + 1) * cap, :].astype(f32)
        by_token = jnp.sum(pick * value, axis=0, keepdims=True)
        sums = sums + jnp.where(routes == owner[j : j + 1, :], by_token, 0.0)
    combine[...] = sums


def product_body(groups, chips, *refs):
    rows, out = refs[:-1], refs[-1]
    _, part, hid_width = out.shape
    slots = chips * rows[0].shape[0]
    rights = [x for h in rows[:groups] for x in hidden_rows(h, hid_width, chips, 0, slots)]
    rights = jnp.concatenate(rights, axis=0)
    step = 256 if part % 256 == 0 else LANES
    for at in range(0, part, step):
        left = [p[:, at : at + step] for g in range(groups) for p in rows[g::groups]]
        out[0, at : at + step, :] = tn(jnp.concatenate(left, axis=0), rights)


def on_device(cotangent, hidden, down_matrix, adapter_in, adapter_out, probs, routes, token_loop):
    experts = lax.axis_size("expert")
    groups = lax.axis_size("dp")
    chips = experts // 2
    toks, width = cotangent.shape
    loops, rank, hid_width = adapter_in.shape
    ways = routes.shape[1]
    slots = hidden.shape[2]
    cap = slots // experts
    part = width // groups
    cols = hid_width // groups
    wide = wide_of(cols)
    share = rank // experts
    bounds = [0, 1, max(2, 3 * chips // 4), chips]
    chunks = [range(a, b) for a, b in zip(bounds[:-1], bounds[1:])]
    flat_in = adapter_in.reshape(loops * rank, hid_width)
    small = jnp.minimum(routes.T, experts) * loops + token_loop.reshape(1, toks)
    small = small.astype(f32) + probs.T.astype(f32)

    turns = range(groups - 1, 0, -1)
    natural = hidden.reshape(slots, hid_width)

    with jax.named_scope("route"):
        packed = shape((chips, cap, width + LANES), bf16)
        keep, lead, give, picks = call(
            functools.partial(route_body, chips, cap, loops),
            (
                packed,
                shape((2,) + packed.shape[1:], bf16),
                shape((chips - 1,) + packed.shape[1:], bf16),
                shape((slots, toks), bf16),
            ),
            (V, pltpu.HBM),
            scratch=(
                pltpu.VMEM((toks, width), bf16),
                pltpu.VMEM((slots, toks), bf16),
                pltpu.SemaphoreType.DMA((2,)),
            ),
            limit=52,
            flops=2 * slots * toks * width,
            nbytes=6 * toks * width,
        )(small, cotangent)
        sib = swap(give, "expert", experts, 1)
    with jax.named_scope("dispatch"):
        middle = chips // 2
        lead = swap(lead, "expert", experts, 2 * middle)
        far = {middle: [lead[0], swap(lead[1], "expert", experts, 1)]}
        others = [hop for hop in range(1, bounds[-2]) if hop != middle]
        for hops, after in ((others, []), (chunks[-1], 1)):
            packs = call(
                functools.partial(pack_body, hops, chips),
                tuple(shape((2, cap, width + LANES), bf16) for hop in hops),
                (V, V) + (A,) * bool(after),
                nbytes=4 * slots * width,
            )(keep, sib, *(far[1] if after else []))
            far.update((hop, [swap(x, "expert", experts, 2 * hop)]) for hop, x in zip(hops, packs))
    with jax.named_scope("arrive"):
        rows, masked, parts = [], [], []
        for hops in chunks:
            own, half = hops[0] == 0, 2 * len(hops) * cap
            blocks = [natural, keep, sib] if own else [x for hop in hops for x in far[hop]]
            before = parts[0][1:] if len(parts) == 1 else []
            sent = part + rank + LANES + chips * hid_width * own
            got = call(
                functools.partial(arrive_body, groups, chips, cap, own, len(before)),
                (shape((half, width + LANES), bf16), shape((half, loops * rank), bf16))
                + (shape((half, sent), bf16),) * groups,
                (V,) * (1 + len(blocks)) + (A,) * len(before),
                flops=2 * half * width * loops * rank,
                nbytes=4 * half * width,
            )(adapter_out, *blocks, *before)
            rows.append(got[0])
            masked.append(got[1])
            parts.append([got[2]] + [swap(got[2 + hop], "dp", groups, hop) for hop in turns])
    with jax.named_scope("inner"):
        grad, mix = call(
            functools.partial(inner_body, chips, cap, len(chunks)),
            (shape((slots, hid_width), bf16), shape((slots, LANES), f32)),
            (V,) * (3 + 2 * len(chunks)),
            flops=2 * slots * width * hid_width,
            nbytes=2 * width * hid_width,
        )(down_matrix[0], flat_in, natural, *rows, *masked)
    with jax.named_scope("adapters"):
        work = groups * slots * loops * rank * (part + hid_width + wide)
        sums = (shape((loops * rank, part), f32), shape((loops * rank, wide), f32))
        size = groups * 2 * len(chunks[-1]) * cap
        out, inn, down, picked = call(
            functools.partial(adapter_first_body, loops, chips, cols, groups),
            sums + (shape((size, loops * rank), bf16), shape((size, wide), bf16)),
            (V, A) + (V,) * (groups * (len(chunks) - 1)),
            flops=work,
            nbytes=groups * slots * part,
        )(flat_in, mix, *(p for chunk in parts[:-1] for p in chunk))
        block = (chips, loops * share, part + wide)
        keep3, give3 = call(
            functools.partial(adapter_last_body, loops, chips, cap, cols),
            (shape(block, f32), shape(block, bf16)),
            (V,) * (5 + groups),
            scratch=[pltpu.VMEM(s.shape, f32) for s in sums],
            flops=work,
            nbytes=groups * slots * part,
        )(out, inn, mix, down, picked, *parts[-1])
        got3 = swap(give3, "expert", experts, 1)
        ready = call(
            functools.partial(pair_body, chips),
            (shape(block[1:], bf16),) * chips,
            (V, V),
            nbytes=1e6,
        )(keep3, got3)
        blocks = list(ready)
        for hop in far_first(chips)[1:]:
            blocks[hop] = swap(ready[hop], "expert", experts, 2 * hop)
    with jax.named_scope("product"):
        product = call(
            functools.partial(product_body, groups, chips),
            shape((1, part, hid_width), f32),
            (V,) * (groups * len(chunks)),
            limit=40,
            flops=2 * groups * slots * part * hid_width,
            nbytes=4 * groups * slots * part,
        )(*(p for chunk in parts for p in chunk))
    with jax.named_scope("final"):
        out_grad, in_grad, combine = call(
            functools.partial(final_body, chips, cap, cols),
            (
                shape((loops, share, part), f32),
                shape((loops, share, cols), f32),
                shape((ways, toks), f32),
            ),
            (V,) * (2 + chips),
            nbytes=1e6,
        )(small, picks, *(blocks[hop] for hop in far_first(chips)))
    return (
        grad.reshape(hidden.shape),
        product,
        combine.T,
        in_grad,
        jnp.swapaxes(out_grad, 1, 2),
    )


def solution(mesh):
    return jax.shard_map(
        on_device,
        mesh=mesh,
        in_specs=(
            P(("dp", "expert"), None),
            P("dp", "expert", None, None),
            P("expert", None, None),
            P(),
            P(),
            P(("dp", "expert"), None),
            P(("dp", "expert"), None),
            P(("dp", "expert")),
        ),
        out_specs=(
            P("dp", "expert", None, None),
            P("expert", "dp", None),
            P(("dp", "expert"), None),
            P(None, "expert", "dp"),
            P(None, "dp", "expert"),
        ),
        check_vma=False,
    )
```

```python
import functools

import jax
import jax.numpy as jnp
from jax import lax
from jax.experimental import pallas as pl
from jax.experimental.pallas import tpu as pltpu
from jax.sharding import PartitionSpec as P

bf16 = jnp.bfloat16
f32 = jnp.float32
LANES = 128
MIB = 1 << 20
V, A = pltpu.VMEM, pl.ANY


def dot(a, b, dims):
    return lax.dot_general(a, b, (dims, ((), ())), preferred_element_type=f32)


def nn(a, b):
    return dot(a, b, ((1,), (0,)))


def nt(a, b):
    return dot(a, b, ((1,), (1,)))


def tn(a, b):
    return dot(a, b, ((0,), (0,)))


def swap(x, axis, size, mask):
    return lax.ppermute(x, axis, [(i, i ^ mask) for i in range(size)])


def shape(dims, kind):
    return jax.ShapeDtypeStruct(dims, kind)


def here():
    return lax.axis_index("expert"), lax.axis_index("dp")


def call(body, out_shape, ins, scratch=(), limit=24, flops=0, nbytes=0):
    return pl.pallas_call(
        body,
        out_shape=out_shape,
        in_specs=[pl.BlockSpec(memory_space=s) for s in ins],
        out_specs=jax.tree.map(lambda _: pl.BlockSpec(memory_space=V), out_shape),
        scratch_shapes=list(scratch),
        cost_estimate=pl.CostEstimate(
            flops=int(flops), bytes_accessed=int(nbytes), transcendentals=0
        ),
        compiler_params=pltpu.CompilerParams(vmem_limit_bytes=limit * MIB),
    )


def owner_column(place, chips, experts):
    j = lax.broadcasted_iota(jnp.int32, (experts, 1), 0)
    half, hop = j // chips, j % chips
    return ((place[0] // 2) ^ hop) * 2 + ((place[0] % 2) ^ half)


def decode(small, loops):
    whole = jnp.floor(small)
    route = jnp.floor((whole + 0.5) * (1.0 / loops))
    return route, small - whole, (whole - route * loops)[:1]


def deal_rows(middle, rows, at, keep, lead, give):
    chips = keep.shape[0]
    keep[:, :, at] = rows[:chips]
    lead[0, :, at], lead[1, :, at] = rows[middle], rows[chips + middle]
    give[:middle, :, at] = rows[chips : chips + middle]
    if middle + 1 < chips:
        give[middle:, :, at] = rows[chips + middle + 1 :]


def route_body(chips, cap, loops, small, cot, keep, lead, give, picks, mixed):
    middle = chips // 2
    experts = 2 * chips
    ways = small.shape[0]
    toks, width = cot.shape
    owner = owner_column(here(), chips, experts).astype(f32)
    route, chance, loop = decode(small[...], loops)
    named = jnp.zeros((experts, toks), f32)
    weight = jnp.zeros((experts, toks), f32)
    for k in range(ways):
        hit = route[k : k + 1, :] == owner
        named = named + jnp.where(hit, 1.0, 0.0)
        weight = weight + jnp.where(hit, chance[k : k + 1, :], 0.0)
    earlier = lax.broadcasted_iota(jnp.int32, (toks, toks), 0) < lax.broadcasted_iota(
        jnp.int32, (toks, toks), 1
    )
    before = nn(named.astype(bf16), jnp.where(earlier, 1.0, 0.0).astype(bf16))
    spot = jnp.where(named > 0.0, before, -1.0)
    slot = lax.broadcasted_iota(jnp.int32, (cap, toks), 0).astype(f32)
    for j in range(experts):
        hit = spot[j : j + 1, :] == slot
        rows = slice(j * cap, (j + 1) * cap)
        picks[rows, :] = jnp.where(hit, 1.0, 0.0).astype(bf16)
        mixed[rows, :] = jnp.where(hit, weight[j : j + 1, :], 0.0).astype(bf16)
    loop_rows = lax.broadcasted_iota(jnp.int32, (LANES, toks), 0).astype(f32)
    loop_rows = jnp.where(loop_rows == loop, 1.0, 0.0).astype(bf16)
    mix = nt(mixed[...], loop_rows).astype(bf16)
    deal_rows(middle, mix.reshape(2 * chips, cap, LANES), slice(width, width + LANES), keep, lead, give)
    step = 2048 if width % 2048 == 0 else width
    for n in range(0, width, step):
        at = slice(n, n + step)
        got = nn(picks[...], cot[:, at]).astype(bf16)
        deal_rows(middle, got.reshape(2 * chips, cap, step), at, keep, lead, give)


def sources(place, chips):
    z, c = place[0] // 2, place[0] % 2
    return [(z ^ hop) * 2 + (c ^ half) for hop in range(chips) for half in range(2)]


def pack_body(hops, chips, keep, sib, *refs):
    for hop, out in zip(hops, refs[-len(hops) :]):
        out[0, :, : keep.shape[2]] = keep[hop]
        out[1, :, : keep.shape[2]] = sib[hop - (hop > chips // 2)]


def arrive_body(groups, chips, cap, own, extra, adapter_out, *refs):
    loops, width, rank = adapter_out.shape
    part = width // groups
    side = part + rank + LANES
    parts = refs[-groups:]
    blocks, (rows, masked) = refs[: -2 - groups - extra], refs[-2 - groups : -groups]
    if own:
        hidden, blocks = blocks[0], blocks[1:]
        hid_width = hidden.shape[1]
        for n, source in enumerate(sources(here(), chips)):
            block = hidden[pl.ds(pl.multiple_of(source * cap, cap), cap), :]
            start, at = side + (n // 2) * hid_width, (n % 2) * cap
            for target in parts:
                target[at : at + cap, start : start + hid_width] = block
    at = 0
    for block in blocks:
        if len(block.shape) == 2:
            halves = (block[...],)
        else:
            halves = (block[0],) if own else (block[0], block[1])
        for piece in halves:
            rows[at : at + piece.shape[0], :] = piece[:, : rows.shape[1]]
            at += piece.shape[0]
    mix_block = rows[:, width:]
    mix = mix_block.astype(f32)
    weight = jnp.sum(mix, axis=1, keepdims=True)
    for hop in range(groups):
        start = pl.multiple_of((here()[1] ^ hop) * part, part)
        parts[hop][:, :part] = (weight * rows[:, pl.ds(start, part)].astype(f32)).astype(bf16)
    masks = [mix[:, l : l + 1] > 0.0 for l in range(loops)]
    proj = jnp.zeros((rows.shape[0], rank), f32)
    for l in range(loops):
        proj = proj + jnp.where(masks[l], nn(rows[:, :width], adapter_out[l]), 0.0)
    proj = proj.astype(bf16).astype(f32)
    for l in range(loops):
        masked[:, l * rank : (l + 1) * rank] = jnp.where(masks[l], proj, 0.0).astype(bf16)
    weighted = (weight * proj).astype(bf16)
    for hop in range(groups):
        parts[hop][:, part : part + rank] = weighted
        parts[hop][:, part + rank : side] = mix_block


def inner_body(chips, cap, chunks, down, adapter_in, hidden, *refs):
    grad_out, mix_out = refs[-2:]
    width, hid_width = down.shape
    step = 256 if hid_width % 256 == 0 else hid_width
    rows = jnp.concatenate([r[...] for r in refs[:chunks]], axis=0)
    masked = jnp.concatenate([r[...] for r in refs[chunks : 2 * chunks]], axis=0)
    weight = jnp.sum(rows[:, width:].astype(f32), axis=1, keepdims=True)
    sums = jnp.zeros((mix_out.shape[0], 1), f32)
    order = sources(here(), chips)
    for at in range(0, hid_width, step):
        cols = slice(at, at + step)
        grad = nn(masked, adapter_in[:, cols]) + nn(rows[:, :width], down[:, cols])
        spots = [pl.ds(pl.multiple_of(source * cap, cap), cap) for source in order]
        hid = jnp.concatenate([hidden[spot, cols] for spot in spots], axis=0)
        sums = sums + jnp.sum(hid.astype(f32) * grad, axis=1, keepdims=True)
        scaled = (weight * grad).astype(bf16)
        for n, spot in enumerate(spots):
            grad_out[spot, cols] = scaled[n * cap : (n + 1) * cap]
    mix_out[...] = jnp.broadcast_to(sums, mix_out.shape)


def hidden_rows(holder, hid_width, chips, start, stop):
    size = holder.shape[0]
    side = holder.shape[1] - chips * hid_width
    blocks = [side + n * hid_width for n in range(start // size, stop // size)]
    return [holder[:, at : at + hid_width] for at in blocks]


def from_hidden(chips, cols, wide, start, stop, adapter_in, holders):
    hid_width = adapter_in.shape[1]
    row = lax.broadcasted_iota(jnp.int32, (hid_width, wide), 0)
    lane = lax.broadcasted_iota(jnp.int32, (hid_width, wide), 1)
    pick = (row == lane + here()[1] * cols) & (lane < cols)
    pick = jnp.where(pick, 1.0, 0.0).astype(bf16)
    hid = [x for h in holders for x in hidden_rows(h, hid_width, chips, start, stop)]
    hid = jnp.concatenate(hid, axis=0)
    return nt(hid, adapter_in[...]).astype(bf16), nn(hid, pick).astype(bf16)


def adapter_sums(loops, part, rows, down, picked):
    rank = down.shape[1] // loops
    side = part + rank + LANES
    tail = jnp.concatenate([r[:, part:side] for r in rows], axis=0).astype(f32)
    body = jnp.concatenate([r[:, :part] for r in rows], axis=0)
    masks = [tail[:, rank + l : rank + l + 1] > 0.0 for l in range(loops)]
    down = down.astype(f32)
    left = [jnp.where(masks[l], down[:, l * rank : (l + 1) * rank], 0.0) for l in range(loops)]
    out = tn(jnp.concatenate(left, axis=1).astype(bf16), body)
    left = [jnp.where(masks[l], tail[:, :rank], 0.0) for l in range(loops)]
    return out, tn(jnp.concatenate(left, axis=1).astype(bf16), picked)


def wide_of(cols):
    return -(-(cols + 4) // LANES) * LANES


def adapter_first_body(loops, chips, cols, groups, adapter_in, _, *refs):
    rows, (out, inn, down_last, picked_last) = refs[:-4], refs[-4:]
    part, wide = out.shape[1], inn.shape[1]
    start = 0
    for at in range(0, len(rows), groups):
        chunk = rows[at : at + groups]
        stop = start + chunk[0].shape[0]
        parts = from_hidden(chips, cols, wide, start, stop, adapter_in, rows[:groups])
        terms = adapter_sums(loops, part, chunk, *parts)
        for target, term in zip((out, inn), terms):
            target[...] = target[...] + term if start else term
        start = stop
    stop = chips * rows[0].shape[0]
    parts = from_hidden(chips, cols, wide, start, stop, adapter_in, rows[:groups])
    down_last[...], picked_last[...] = parts


def adapter_last_body(loops, chips, cap, cols, out, inn, mix, down, picked, *refs):
    rows, (keep, give, sums, narrow) = refs[:-4], refs[-4:]
    rank = out.shape[0] // loops
    part = out.shape[1]
    share = rank // (2 * chips)
    more = adapter_sums(loops, part, rows, down[...], picked[...])
    sums[...] = out[...] + more[0]
    narrow[...] = inn[...] + more[1]
    owners = sources(here(), chips)
    lane = lax.broadcasted_iota(jnp.int32, (cap, narrow.shape[1]), 1)
    for n, owner in enumerate(owners):
        hop, target = n // 2, (keep, give)[n % 2]
        for l in range(loops):
            src = pl.ds(pl.multiple_of(l * rank + owner * share, share), share)
            dst = slice(l * share, (l + 1) * share)
            target[hop, dst, :part] = sums[src, :].astype(target.dtype)
            target[hop, dst, part:] = narrow[src, :].astype(target.dtype)
        value = mix[n * cap : (n + 1) * cap, :1]
        high = value.astype(bf16).astype(f32)
        tail = target[hop, :cap, part:].astype(f32)
        tail = jnp.where(lane == cols + 2 * (n % 2), high, tail)
        tail = jnp.where(lane == cols + 2 * (n % 2) + 1, value - high, tail)
        target[hop, :cap, part:] = tail.astype(target.dtype)


def pair_body(chips, keep, got, *outs):
    for hop in range(chips):
        outs[hop][...] = (keep[hop] + got[hop].astype(f32)).astype(bf16)


def far_first(chips):
    return [0] + list(range(chips // 2, chips)) + list(range(1, chips // 2))


def final_body(chips, cap, cols, small, picks, *refs):
    order = far_first(chips)
    blocks = [refs[order.index(hop)] for hop in range(chips)]
    out_grad, in_grad, combine = refs[chips:]
    loops, share, part = out_grad.shape
    total = blocks[0][...].astype(f32)
    for hop in range(1, chips):
        total = total + blocks[hop][...].astype(f32)
    for l in range(loops):
        rows = slice(l * share, (l + 1) * share)
        out_grad[l] = total[rows, :part]
        in_grad[l] = total[rows, part : part + cols]
    experts = 2 * chips
    owner = owner_column(here(), chips, experts).astype(f32)
    routes = decode(small[...], loops)[0]
    sums = jnp.zeros(combine.shape, f32)
    for j in range(experts):
        half, hop = j // chips, j % chips
        words = blocks[hop][:cap, part:].astype(f32)
        at = cols + 2 * half
        value = words[:, at : at + 1] + words[:, at + 1 : at + 2]
        pick = picks[j * cap : (j + 1) * cap, :].astype(f32)
        by_token = jnp.sum(pick * value, axis=0, keepdims=True)
        sums = sums + jnp.where(routes == owner[j : j + 1, :], by_token, 0.0)
    combine[...] = sums


def product_body(groups, chips, *refs):
    rows, out = refs[:-1], refs[-1]
    _, part, hid_width = out.shape
    slots = chips * rows[0].shape[0]
    rights = [x for h in rows[:groups] for x in hidden_rows(h, hid_width, chips, 0, slots)]
    rights = jnp.concatenate(rights, axis=0)
    step = 256 if part % 256 == 0 else LANES
    for at in range(0, part, step):
        left = [p[:, at : at + step] for g in range(groups) for p in rows[g::groups]]
        out[0, at : at + step, :] = tn(jnp.concatenate(left, axis=0), rights)


def on_device(cotangent, hidden, down_matrix, adapter_in, adapter_out, probs, routes, token_loop):
    experts = lax.axis_size("expert")
    groups = lax.axis_size("dp")
    chips = experts // 2
    toks, width = cotangent.shape
    loops, rank, hid_width = adapter_in.shape
    ways = routes.shape[1]
    slots = hidden.shape[2]
    cap = slots // experts
    part = width // groups
    cols = hid_width // groups
    wide = wide_of(cols)
    share = rank // experts
    bounds = [0, 1, max(2, 3 * chips // 4), chips]
    chunks = [range(a, b) for a, b in zip(bounds[:-1], bounds[1:])]
    flat_in = adapter_in.reshape(loops * rank, hid_width)
    small = jnp.minimum(routes.T, experts) * loops + token_loop.reshape(1, toks)
    small = small.astype(f32) + probs.T.astype(f32)

    turns = range(groups - 1, 0, -1)
    natural = hidden.reshape(slots, hid_width)

    with jax.named_scope("route"):
        packed = shape((chips, cap, width + LANES), bf16)
        keep, lead, give, picks = call(
            functools.partial(route_body, chips, cap, loops),
            (
                packed,
                shape((2,) + packed.shape[1:], bf16),
                shape((chips - 1,) + packed.shape[1:], bf16),
                shape((slots, toks), bf16),
            ),
            (V, V),
            scratch=(pltpu.VMEM((slots, toks), bf16),),
            flops=2 * slots * toks * width,
            nbytes=6 * toks * width,
        )(small, cotangent)
        sib = swap(give, "expert", experts, 1)
    with jax.named_scope("dispatch"):
        middle = chips // 2
        lead = swap(lead, "expert", experts, 2 * middle)
        far = {middle: [lead[0], swap(lead[1], "expert", experts, 1)]}
        others = [hop for hop in range(1, bounds[-2]) if hop != middle]
        for hops, after in ((others, []), (chunks[-1], 1)):
            packs = call(
                functools.partial(pack_body, hops, chips),
                tuple(shape((2, cap, width + LANES), bf16) for hop in hops),
                (V, V) + (A,) * bool(after),
                nbytes=4 * slots * width,
            )(keep, sib, *(far[1] if after else []))
            far.update((hop, [swap(x, "expert", experts, 2 * hop)]) for hop, x in zip(hops, packs))
    with jax.named_scope("arrive"):
        rows, masked, parts = [], [], []
        for hops in chunks:
            own, half = hops[0] == 0, 2 * len(hops) * cap
            blocks = [natural, keep, sib] if own else [x for hop in hops for x in far[hop]]
            before = parts[0][1:] if len(parts) == 1 else []
            sent = part + rank + LANES + chips * hid_width * own
            got = call(
                functools.partial(arrive_body, groups, chips, cap, own, len(before)),
                (shape((half, width + LANES), bf16), shape((half, loops * rank), bf16))
                + (shape((half, sent), bf16),) * groups,
                (V,) * (1 + len(blocks)) + (A,) * len(before),
                flops=2 * half * width * loops * rank,
                nbytes=4 * half * width,
            )(adapter_out, *blocks, *before)
            rows.append(got[0])
            masked.append(got[1])
            parts.append([got[2]] + [swap(got[2 + hop], "dp", groups, hop) for hop in turns])
    with jax.named_scope("inner"):
        grad, mix = call(
            functools.partial(inner_body, chips, cap, len(chunks)),
            (shape((slots, hid_width), bf16), shape((slots, LANES), f32)),
            (V,) * (3 + 2 * len(chunks)),
            flops=2 * slots * width * hid_width,
            nbytes=2 * width * hid_width,
        )(down_matrix[0], flat_in, natural, *rows, *masked)
    with jax.named_scope("adapters"):
        work = groups * slots * loops * rank * (part + hid_width + wide)
        sums = (shape((loops * rank, part), f32), shape((loops * rank, wide), f32))
        size = groups * 2 * len(chunks[-1]) * cap
        out, inn, down, picked = call(
            functools.partial(adapter_first_body, loops, chips, cols, groups),
            sums + (shape((size, loops * rank), bf16), shape((size, wide), bf16)),
            (V, A) + (V,) * (groups * (len(chunks) - 1)),
            flops=work,
            nbytes=groups * slots * part,
        )(flat_in, mix, *(p for chunk in parts[:-1] for p in chunk))
        block = (chips, loops * share, part + wide)
        keep3, give3 = call(
            functools.partial(adapter_last_body, loops, chips, cap, cols),
            (shape(block, f32), shape(block, bf16)),
            (V,) * (5 + groups),
            scratch=[pltpu.VMEM(s.shape, f32) for s in sums],
            flops=work,
            nbytes=groups * slots * part,
        )(out, inn, mix, down, picked, *parts[-1])
        got3 = swap(give3, "expert", experts, 1)
        ready = call(
            functools.partial(pair_body, chips),
            (shape(block[1:], bf16),) * chips,
            (V, V),
            nbytes=1e6,
        )(keep3, got3)
        blocks = list(ready)
        for hop in far_first(chips)[1:]:
            blocks[hop] = swap(ready[hop], "expert", experts, 2 * hop)
    with jax.named_scope("product"):
        product = call(
            functools.partial(product_body, groups, chips),
            shape((1, part, hid_width), f32),
            (V,) * (groups * len(chunks)),
            limit=40,
            flops=2 * groups * slots * part * hid_width,
            nbytes=4 * groups * slots * part,
        )(*(p for chunk in parts for p in chunk))
    with jax.named_scope("final"):
        out_grad, in_grad, combine = call(
            functools.partial(final_body, chips, cap, cols),
            (
                shape((loops, share, part), f32),
                shape((loops, share, cols), f32),
                shape((ways, toks), f32),
            ),
            (V,) * (2 + chips),
            nbytes=1e6,
        )(small, picks, *(blocks[hop] for hop in far_first(chips)))
    return (
        grad.reshape(hidden.shape),
        product,
        combine.T,
        in_grad,
        jnp.swapaxes(out_grad, 1, 2),
    )


def solution(mesh):
    return jax.shard_map(
        on_device,
        mesh=mesh,
        in_specs=(
            P(("dp", "expert"), None),
            P("dp", "expert", None, None),
            P("expert", None, None),
            P(),
            P(),
            P(("dp", "expert"), None),
            P(("dp", "expert"), None),
            P(("dp", "expert")),
        ),
        out_specs=(
            P("dp", "expert", None, None),
            P("expert", "dp", None),
            P(("dp", "expert"), None),
            P(None, "expert", "dp"),
            P(None, "dp", "expert"),
        ),
        check_vma=False,
    )
```
